32 devices in a mesh: dp: 8 (over y, x, core), tensor: 4 (over z).
Axes of the slice: x: 2, y: 2, z: 4, core: 2. Of those that a mesh axis runs over, the one named last changes fastest.
Arguments:
- hidden: bfloat16 [8192, 768], P('dp'), may hold values from -6 to 6
- out_grad: bfloat16 [8192, 768], P('dp'), may hold values from -6 to 6
- w_query: bfloat16 [768, 768], P(None, 'tensor'), may hold values from -0.21875 to 0.21875
- w_key: bfloat16 [768, 768], P(None, 'tensor'), may hold values from -0.21875 to 0.21875
- w_value: bfloat16 [768, 768], P(None, 'tensor'), may hold values from -0.21875 to 0.21875
- w_out: bfloat16 [768, 768], P('tensor'), may hold values from -2.5 to 2.5
- w_in: bfloat16 [768, 3072], P(None, 'tensor'), may hold values from -0.21875 to 0.21875
- w_down: bfloat16 [3072, 768], P('tensor'), may hold values from -0.109375 to 0.109375
- bucket_table: bfloat16 [512, 768], replicated, may hold values from -6 to 6
- gain_one: float32 [768], replicated, may hold values from 0.5 to 1.5
- bias_one: float32 [768], replicated, may hold values from -2 to 2
- gain_two: float32 [768], replicated, may hold values from 0.5 to 1.5
- bias_two: float32 [768], replicated, may hold values from -2 to 2
- rel_buckets: int32 [1023], replicated, may hold values from 0 to 511
- group_counts: int32 [8, 3], P('dp'), may hold values from 0 to 8, as said below
- key_mask: int32 [8192], P('dp'), may hold values from 0 to 1, as said below
Outputs:
- output: bfloat16 [8192, 768], P('dp')
- grad_hidden: bfloat16 [8192, 768], P('dp')
- grad_query: float32 [768, 768], P(None, 'tensor')
- grad_key: float32 [768, 768], P(None, 'tensor')
- grad_value: float32 [768, 768], P(None, 'tensor')
- grad_out: float32 [768, 768], P('tensor')
- grad_in: float32 [768, 3072], P(None, 'tensor')
- grad_down: float32 [3072, 768], P('tensor')
- grad_table: float32 [512, 768], replicated
- grad_gain_one: float32 [768], replicated
- grad_bias_one: float32 [768], replicated
- grad_gain_two: float32 [768], replicated
- grad_bias_two: float32 [768], replicated
The draws below stay inside these ranges and needn't reach their ends.
Inputs may be any that keep to these rules, and one draw needn't show every extreme that they name: `group_counts`: in each row c0 512 + c1 512 / 2 + c2 512 / 4 = 1024; some row holds only sequences of 128 tokens. `key_mask`: every token whose position in its dp index's buffer is a multiple of 128 is real.
All inputs are finite; a program needn't handle non-finite values.
Results may differ from the reference program's by a relative error of at most 0.02.
Values may be sent and summed in bfloat16 or wider, within the bound.
No kernel may reach another device: no remote copies, remote signals or barrier semaphores. Data moves between devices by JAX's collectives and lax.ppermute only.
A program may use at most 192 MiB of HBM per device.

```python
import math
import jax
import jax.numpy as jnp
from jax import lax

D = 768
HEADS = 12
HEAD_DIM = 64
FF = 3072
SPAN = 256
SEQMAX = 512
TOK_DEV = 1024
TOKENS = 8192
N_TENSOR = 4


def draw_group_counts(key, part):
    first_key, second_key, third_key = jax.random.split(key, 3)
    row_total = TOKENS // TOK_DEV
    longest = jax.random.randint(first_key, (row_total,), 0, TOK_DEV // SEQMAX + 1)
    remaining = TOK_DEV - SEQMAX * longest
    middle = jax.random.randint(second_key, (row_total,), 0, remaining // (SEQMAX // 2) + 1)
    shortest = (remaining - SEQMAX // 2 * middle) // (SEQMAX // 4)
    chosen = jax.random.randint(third_key, (), 0, row_total)
    row_ids = jnp.arange(row_total, dtype=jnp.int32)
    chosen_row = row_ids == chosen
    longest = jnp.where(chosen_row, 0, longest)
    middle = jnp.where(chosen_row, 0, middle)
    shortest = jnp.where(chosen_row, TOK_DEV // (SEQMAX // 4), shortest)
    return jnp.stack([longest, middle, shortest], axis=1).astype(jnp.int32)


def draw_key_mask(key, part):
    dice_rolls = jax.random.randint(key, (TOKENS,), 0, 8)
    places = jnp.arange(TOKENS, dtype=jnp.int32)
    return jnp.where((dice_rolls < 7) | (places % (SEQMAX // 4) == 0), 1, 0).astype(jnp.int32)


def with_ends(drawn, key, smallest, largest):
    dims = drawn.shape
    spot = [jax.random.randint(jax.random.fold_in(key, axis), (), 0, dims[axis]) for axis in range(len(dims))]
    drawn = drawn.at[tuple(spot)].set(smallest)
    longest = dims.index(max(dims))
    spot[longest] = (spot[longest] + 1) % dims[longest]
    return drawn.at[tuple(spot)].set(largest)


def level_of(rng, shape, cuts, low, top_value):
    level = 1.0
    for axis_at, shards_of in cuts:
        heights = jax.random.uniform(jax.random.fold_in(jax.random.fold_in(rng, 6), axis_at), (shards_of,), jnp.float32, low / len(cuts), top_value / len(cuts))
        level = level * jnp.repeat(jnp.exp(heights), shape[axis_at] // shards_of).reshape((-1,) + (1,) * (len(shape) - 1 - axis_at))
    return level


def gaussian(key, extent, width, most, shards=(), kind=jnp.bfloat16):
    level = level_of(key, extent, shards, -0.22, 0.18) if shards else 1.0
    entries = jax.random.normal(key, extent, jnp.float32) * width * level
    return jnp.minimum(jnp.maximum(entries, -most), most).astype(kind)


def setup_inputs(seed: int = 0) -> dict:
    splits = jax.random.split(jax.random.key(seed), 17)
    hidden = gaussian(splits[0], (TOKENS, D), 1.0, 6.0, ((0, 8),))
    out_grad = gaussian(splits[1], (TOKENS, D), 1.0, 6.0, ((0, 8),))
    w_query = gaussian(splits[2], (D, D), D ** -0.5, 0.21875, ((1, 4),))
    w_key = gaussian(splits[3], (D, D), D ** -0.5, 0.21875, ((1, 4),))
    w_value = gaussian(splits[4], (D, D), D ** -0.5, 0.21875, ((1, 4),))
    w_out = gaussian(splits[5], (D, D), (max(D // 128, 1)) ** -0.5, 2.5, ((0, 4),))
    w_in = gaussian(splits[6], (D, FF), D ** -0.5, 0.21875, ((1, 4),))
    w_down = gaussian(splits[7], (FF, D), FF ** -0.5, 0.109375, ((0, 4),))
    bucket_table = gaussian(splits[8], (2 * SPAN, D), 1.0, 6.0)
    gain_one = jnp.clip(1.0 + 0.1 * jax.random.normal(splits[9], (D,), jnp.float32), 0.5, 1.5)
    bias_one = gaussian(splits[10], (D,), 0.3, 2.0, (), jnp.float32)
    gain_two = jnp.clip(1.0 + 0.1 * jax.random.normal(splits[11], (D,), jnp.float32), 0.5, 1.5)
    bias_two = gaussian(splits[12], (D,), 0.3, 2.0, (), jnp.float32)
    rel_buckets = with_ends(jax.random.randint(splits[13], (2 * SEQMAX - 1,), 0, 2 * SPAN), jax.random.fold_in(splits[13], 1), 0, (2 * SPAN) - 1).astype(jnp.int32)
    group_counts = draw_group_counts(jax.random.fold_in(splits[16], 71), 0)
    key_mask = draw_key_mask(jax.random.fold_in(splits[16], 71), 0)
    return {"hidden": hidden, "out_grad": out_grad, "w_query": w_query, "w_key": w_key, "w_value": w_value, "w_out": w_out, "w_in": w_in, "w_down": w_down, "bucket_table": bucket_table, "gain_one": gain_one, "bias_one": bias_one, "gain_two": gain_two, "bias_two": bias_two, "rel_buckets": rel_buckets, "group_counts": group_counts, "key_mask": key_mask}


@jax.custom_vjp
def low(v):
    return lax.optimization_barrier(v.astype(jnp.bfloat16)).astype(jnp.float32)

@jax.custom_vjp
def low_back(v):
    return v

def low_keep(v):
    return (low(v), None)

def low_pass(kept, grad):
    return (grad,)

def back_keep(v):
    return (v, None)

def back_low(kept, grad):
    return (low(grad),)
low.defvjp(low_keep, low_pass)
low_back.defvjp(back_keep, back_low)
NORM_EPS = 1e-07
MAXIMUM_PRECISION = lax.Precision.HIGHEST

def matmul(left, right):
    return jnp.dot(left, right, precision=MAXIMUM_PRECISION, preferred_element_type=jnp.float32)

def layer_norm(resid, gain, offset):
    average = lax.optimization_barrier(jnp.mean(resid, axis=-1, keepdims=True))
    centered = resid - average
    variance = lax.optimization_barrier(jnp.mean(centered * centered, axis=-1, keepdims=True))
    return centered * lax.rsqrt(variance + NORM_EPS) * gain + offset

def exact_gelu(pre_act):
    return jax.nn.gelu(pre_act, approximate=False)

def sequence_starts(counts, tokens):
    places = jnp.arange(tokens, dtype=jnp.int32)
    long_end = SEQMAX * counts[0]
    mid_end = long_end + SEQMAX // 2 * counts[1]
    length = jnp.where(places < long_end, SEQMAX, jnp.where(places < mid_end, SEQMAX // 2, SEQMAX // 4))
    anchor = jnp.where(places < long_end, 0, jnp.where(places < mid_end, long_end, mid_end))
    return anchor + (places - anchor) // length * length

def make_allow(start_blk, valid_blk):
    return (start_blk[:, None] == start_blk[None, :]) & (valid_blk[None, :] == 1)

def attend_block(query_block_rows, key_blk, value_blk, start_blk, valid_blk, position_key, pos_query, bucket_index):
    allowed = make_allow(start_blk, valid_blk)
    head_count = query_block_rows.shape[1]
    wide_index = jnp.broadcast_to(bucket_index[None], (head_count,) + bucket_index.shape)
    content = jnp.einsum('ihd,jhd->hij', query_block_rows, key_blk, precision=MAXIMUM_PRECISION)
    query_position = low_back(jnp.einsum('zgo,ngo->gzn', query_block_rows, position_key, precision=MAXIMUM_PRECISION))
    key_pos = low_back(jnp.einsum('jhd,bhd->hjb', key_blk, pos_query, precision=MAXIMUM_PRECISION))
    raw_scores = content + jnp.take_along_axis(query_position, wide_index, axis=2)
    raw_scores = raw_scores + jnp.swapaxes(jnp.take_along_axis(key_pos, wide_index, axis=2), 1, 2)
    raw_scores = low_back(raw_scores)
    scaled = jnp.where(allowed[None], raw_scores * (1.0 / math.sqrt(3.0 * HEAD_DIM)), -1e+30)
    attn_weights = low(jax.nn.softmax(scaled, axis=-1))
    return low_back(low(jnp.einsum('hij,jhd->ihd', attn_weights, value_blk, precision=MAXIMUM_PRECISION)))

def device_layer(params, hidden_rows, counts, valid_keys, bucket_index):
    w_query, w_key, w_value, w_out, w_in, w_down, bucket_table, gain_one, bias_one, gain_two, bias_two = params
    tokens = hidden_rows.shape[0]
    blocks = tokens // SEQMAX
    block_shape = (blocks, SEQMAX, HEADS, HEAD_DIM)
    query_rows = low_back(low(matmul(hidden_rows, w_query)))
    key_rows = low_back(low(matmul(hidden_rows, w_key)))
    value_rows = low_back(low(matmul(hidden_rows, w_value)))
    position_key = low(matmul(bucket_table, w_key)).reshape(2 * SPAN, HEADS, HEAD_DIM)
    pos_query = low(matmul(bucket_table, w_query)).reshape(2 * SPAN, HEADS, HEAD_DIM)
    starts = sequence_starts(counts, tokens).reshape(blocks, SEQMAX)
    shaped = (query_rows.reshape(block_shape), key_rows.reshape(block_shape), value_rows.reshape(block_shape), starts, valid_keys.reshape(blocks, SEQMAX))

    def one_block(pieces):
        return attend_block(pieces[0], pieces[1], pieces[2], pieces[3], pieces[4], position_key, pos_query, bucket_index)
    context = lax.map(jax.checkpoint(one_block), shaped).reshape(tokens, N_TENSOR, D // N_TENSOR)
    parts_one = jnp.einsum('tnk,nkd->tnd', context, w_out.reshape(N_TENSOR, D // N_TENSOR, D), precision=MAXIMUM_PRECISION)
    attn_out = low_back(lax.optimization_barrier(jnp.sum(low(parts_one), axis=1)))
    first_norm = layer_norm(hidden_rows + attn_out, gain_one, bias_one)
    pre_act = low_back(matmul(low(first_norm), w_in))
    activated = low(exact_gelu(pre_act))
    parts_two = jnp.einsum('tnk,nkd->tnd', activated.reshape(tokens, N_TENSOR, FF // N_TENSOR), w_down.reshape(N_TENSOR, FF // N_TENSOR, D), precision=MAXIMUM_PRECISION)
    ffn_out = low_back(lax.optimization_barrier(jnp.sum(low(parts_two), axis=1)))
    return layer_norm(first_norm + ffn_out, gain_two, bias_two)

def reference(hidden, out_grad, w_query, w_key, w_value, w_out, w_in, w_down, bucket_table, gain_one, bias_one, gain_two, bias_two, rel_buckets, group_counts, key_mask):
    params = (w_query.astype(jnp.float32), w_key.astype(jnp.float32), w_value.astype(jnp.float32), w_out.astype(jnp.float32), w_in.astype(jnp.float32), w_down.astype(jnp.float32), bucket_table.astype(jnp.float32), gain_one.astype(jnp.float32), bias_one.astype(jnp.float32), gain_two.astype(jnp.float32), bias_two.astype(jnp.float32))
    places = jnp.arange(SEQMAX, dtype=jnp.int32)
    bucket_index = rel_buckets[places[:, None] - places[None, :] + (SEQMAX - 1)].astype(jnp.int32)
    devices = hidden.shape[0] // TOK_DEV
    stacked = (hidden.reshape(devices, TOK_DEV, D).astype(jnp.float32), out_grad.reshape(devices, TOK_DEV, D).astype(jnp.float32), group_counts, key_mask.reshape(devices, TOK_DEV))

    def per_device(totals, pieces):
        hidden_rows, cotangent, counts, valid_keys = pieces

        def layer_of(weights, rows_in):
            return device_layer(weights, rows_in, counts, valid_keys, bucket_index)
        result, pull_back = jax.vjp(layer_of, params, hidden_rows)
        weight_grads, row_grads = pull_back(cotangent)
        summed = jax.tree.map(jnp.add, totals, weight_grads)
        return (summed, (result.astype(jnp.bfloat16), row_grads.astype(jnp.bfloat16)))
    zero_grads = jax.tree.map(jnp.zeros_like, params)
    totals, (output, grad_hidden) = lax.scan(per_device, zero_grads, stacked)
    output = output.reshape(devices * TOK_DEV, D)
    grad_hidden = grad_hidden.reshape(devices * TOK_DEV, D)
    return (output, grad_hidden, totals[0], totals[1], totals[2], totals[3], totals[4], totals[5], totals[6], totals[7], totals[8], totals[9], totals[10])
```

```python
import math

import jax
import jax.numpy as jnp
from jax import lax
from jax.experimental import pallas as pl
from jax.experimental.pallas import tpu as pltpu
from jax.sharding import PartitionSpec as P

NORM_EPS = 1e-07
HEAD_DIM = 64
SEQMAX = 512
TILE = 128
WINDOW = SEQMAX + TILE
OFFSETS = 2 * SEQMAX
NEGATIVE = -1e30
F32 = jnp.float32
BF16 = jnp.bfloat16


def score_factor():
    return 1.0 / math.sqrt(3.0 * HEAD_DIM)


def mm(left, right):
    return jnp.dot(left, right, preferred_element_type=F32)


def mm_nt(left, right):
    return lax.dot_general(left, right, (((1,), (1,)), ((), ())), preferred_element_type=F32)


def mm_tn(left, right):
    return lax.dot_general(left, right, (((0,), (0,)), ((), ())), preferred_element_type=F32)


def starts_of(places, counts_ref):
    long_end = SEQMAX * counts_ref[0, 0]
    mid_end = long_end + SEQMAX // 2 * counts_ref[0, 1]
    in_long = places < long_end
    in_mid = places < mid_end
    anchor = jnp.where(in_long, 0, jnp.where(in_mid, long_end, mid_end))
    shift = jnp.where(in_long, 9, jnp.where(in_mid, 8, 7))
    return anchor + lax.shift_left(lax.shift_right_logical(places - anchor, shift), shift)


def tile_iotas():
    rows = lax.broadcasted_iota(jnp.int32, (TILE, TILE), 0)
    lanes = lax.broadcasted_iota(jnp.int32, (TILE, TILE), 1)
    return rows, lanes


def lane_tiles(wide):
    return [wide[:, c : c + TILE] for c in range(0, wide.shape[1], TILE)]


def skew(wide):
    rows, lanes = tile_iotas()
    keep = lanes <= rows
    turned = [pltpu.roll(part, 1, 1, stride=1, stride_axis=0) for part in lane_tiles(wide)]
    return jnp.concatenate(
        [jnp.where(keep, turned[c], turned[c + 1]) for c in range(len(turned) - 1)], axis=1
    )


def unskew(flipped):
    rows, lanes = tile_iotas()
    late = lanes > rows
    turned = [pltpu.roll(part, 1, 1, stride=1, stride_axis=0) for part in lane_tiles(flipped)]
    zero = jnp.zeros((TILE, TILE), F32)
    turned = [zero] + turned + [zero]
    return jnp.concatenate(
        [jnp.where(late, turned[c], turned[c + 1]) for c in range(len(turned) - 1)], axis=1
    )


def window_of(tile_at):
    low = SEQMAX - TILE - tile_at
    return slice(low, low + WINDOW)


def one_hot_columns(rel_ref, row, buckets):
    ids = lax.broadcasted_iota(jnp.int32, (buckets, OFFSETS), 0)
    return (ids == rel_ref[row : row + 1, :]).astype(BF16)


def split_low(wide):
    high = wide.astype(BF16)
    return high, (wide - high.astype(F32)).astype(BF16)


def forward_kernel(
    hidden_ref, wq_ref, wk_ref, wv_ref, table_ref, rel_ref, counts_ref, mask_ref,
    q_ref, k_ref, v_ref, weights_ref, context_ref, pk_back_ref, pq_back_ref,
    pk_ref, pq_ref, bias_ref, rel_score_ref,
):
    block = pl.program_id(0)
    buckets = table_ref.shape[0]
    heads = wq_ref.shape[1] // HEAD_DIM

    @pl.when(block == 0)
    def tables():
        table = table_ref[...]
        pos_key = lax.dot_general(
            wk_ref[...], table, (((0,), (1,)), ((), ())), preferred_element_type=F32
        ).astype(BF16)
        pos_query = lax.dot_general(
            wq_ref[...], table, (((0,), (1,)), ((), ())), preferred_element_type=F32
        ).astype(BF16)
        plain = one_hot_columns(rel_ref, 0, buckets)
        pk_ref[...] = mm(pos_key, plain).astype(BF16)
        pq_ref[...] = mm(pos_query, plain).astype(BF16)
        back = one_hot_columns(rel_ref, 1, buckets)
        pk_back_ref[...] = mm(pos_key, back).astype(BF16)
        pq_back_ref[...] = mm(pos_query, back).astype(BF16)

    first = block * SEQMAX
    column = starts_of(lax.broadcasted_iota(jnp.int32, (SEQMAX, 1), 0) + first, counts_ref)
    row = starts_of(lax.broadcasted_iota(jnp.int32, (1, SEQMAX), 1) + first, counts_ref)
    row = jnp.where(mask_ref[0] == 1, row, -1)
    bias_ref[...] = jnp.where(column == row, 0.0, NEGATIVE)

    hidden = hidden_ref[...]
    q_ref[...] = mm(hidden, wq_ref[...]).astype(BF16)
    k_ref[...] = mm(hidden, wk_ref[...]).astype(BF16)
    v_ref[...] = mm(hidden, wv_ref[...]).astype(BF16)
    for head in range(heads):
        part = slice(head * HEAD_DIM, (head + 1) * HEAD_DIM)
        queries = q_ref[:, part]
        keys = k_ref[:, part]
        values = v_ref[:, part]
        for at in range(0, SEQMAX, TILE):
            rel = mm(keys[at : at + TILE], pq_ref[part, window_of(at)])
            rel_score_ref[at : at + TILE, :] = skew(rel)
        for at in range(0, SEQMAX, TILE):
            rows = slice(at, at + TILE)
            raw = mm_nt(queries[rows], keys)
            raw = raw + skew(mm(queries[rows], pk_ref[part, window_of(at)]))
            raw = raw + rel_score_ref[:, rows].T
            scaled = raw * score_factor() + bias_ref[rows, :]
            top = jnp.max(scaled, axis=-1, keepdims=True)
            exponent = jnp.exp(scaled - top)
            total = jnp.sum(exponent, axis=-1, keepdims=True)
            weights = exponent * (1.0 / total)
            weights_ref[0, head, rows, :] = weights
            context_ref[rows, part] = mm(weights.astype(BF16), values).astype(BF16)


def forward_attention(hidden, w_query, w_key, w_value, table, rel_rows, counts, key_mask):
    tokens, width = hidden.shape
    local = w_query.shape[1]
    heads = local // HEAD_DIM
    buckets = table.shape[0]
    blocks = tokens // SEQMAX
    whole = lambda *shape: pl.BlockSpec(shape, lambda b: (0,) * len(shape))
    rows = lambda w: pl.BlockSpec((SEQMAX, w), lambda b: (b, 0))
    shape = jax.ShapeDtypeStruct
    return pl.pallas_call(
        forward_kernel,
        grid=(blocks,),
        in_specs=[
            rows(width),
            whole(width, local),
            whole(width, local),
            whole(width, local),
            whole(buckets, width),
            whole(2, OFFSETS),
            pl.BlockSpec(memory_space=pltpu.SMEM),
            pl.BlockSpec((1, 1, SEQMAX), lambda b: (b, 0, 0)),
        ],
        out_specs=[
            rows(local),
            rows(local),
            rows(local),
            pl.BlockSpec((1, heads, SEQMAX, SEQMAX), lambda b: (b, 0, 0, 0)),
            rows(local),
            whole(local, OFFSETS),
            whole(local, OFFSETS),
        ],
        out_shape=[
            shape((tokens, local), BF16),
            shape((tokens, local), BF16),
            shape((tokens, local), BF16),
            shape((blocks, heads, SEQMAX, SEQMAX), F32),
            shape((tokens, local), BF16),
            shape((local, OFFSETS), BF16),
            shape((local, OFFSETS), BF16),
        ],
        scratch_shapes=[
            pltpu.VMEM((local, OFFSETS), BF16),
            pltpu.VMEM((local, OFFSETS), BF16),
            pltpu.VMEM((SEQMAX, SEQMAX), F32),
            pltpu.VMEM((SEQMAX, SEQMAX), F32),
        ],
        compiler_params=pltpu.CompilerParams(
            dimension_semantics=("arbitrary",), vmem_limit_bytes=40 * 2**20
        ),
        cost_estimate=pl.CostEstimate(
            flops=8_000_000_000, bytes_accessed=12_000_000, transcendentals=1_600_000
        ),
        name="attention_forward",
    )(hidden, w_query, w_key, w_value, table, rel_rows, counts, key_mask.reshape(blocks, 1, SEQMAX))


def backward_kernel(
    cg_ref, q_ref, k_ref, v_ref, weights_ref, pk_back_ref, pq_back_ref,
    hidden_ref, wq_ref, wk_ref, wv_ref, table_ref, rel_ref,
    part_ref, grads_ref, pos_ref,
    ds_ref, rows_ref, rg_key_ref, rg_query_ref, sum_ref,
):
    block = pl.program_id(0)
    blocks = pl.num_programs(0)
    local = wq_ref.shape[1]
    heads = local // HEAD_DIM
    buckets = table_ref.shape[0]

    @pl.when(block == 0)
    def clear():
        rg_key_ref[...] = jnp.zeros_like(rg_key_ref)
        rg_query_ref[...] = jnp.zeros_like(rg_query_ref)
        sum_ref[...] = jnp.zeros_like(sum_ref)

    tile_rows, tile_lanes = tile_iotas()
    flip = (tile_rows + tile_lanes == TILE - 1).astype(BF16)

    def flipped(low):
        return jnp.concatenate([mm(part, flip) for part in lane_tiles(low)], axis=1)

    for head in range(heads):
        part = slice(head * HEAD_DIM, (head + 1) * HEAD_DIM)
        at_k = slice(local + head * HEAD_DIM, local + (head + 1) * HEAD_DIM)
        at_v = slice(2 * local + head * HEAD_DIM, 2 * local + (head + 1) * HEAD_DIM)
        queries = q_ref[:, part]
        keys = k_ref[:, part]
        values = v_ref[:, part]
        cotangent = cg_ref[:, part]
        value_grad = jnp.zeros((SEQMAX, HEAD_DIM), F32)
        for at in range(0, SEQMAX, TILE):
            rows = slice(at, at + TILE)
            weights = weights_ref[0, head, rows, :]
            weight_grad = mm_nt(cotangent[rows], values)
            inner = jnp.sum(weights * weight_grad, axis=-1, keepdims=True)
            score_grad = (weights * (weight_grad - inner) * score_factor()).astype(BF16)
            ds_ref[rows, :] = score_grad
            value_grad = value_grad + mm_tn(weights.astype(BF16), cotangent[rows])
            by_offset = unskew(flipped(score_grad)).astype(BF16)
            window = window_of(at)
            query_grad = mm(score_grad, keys) + mm_nt(by_offset, pk_back_ref[part, window])
            rows_ref[rows, part] = query_grad.astype(BF16)
            rg_key_ref[part, window] += mm_tn(queries[rows], by_offset)
        rows_ref[:, at_v] = value_grad.astype(BF16)
        for at in range(0, SEQMAX, TILE):
            rows = slice(at, at + TILE)
            turned = ds_ref[:, rows].T
            by_offset = unskew(flipped(turned)).astype(BF16)
            window = window_of(at)
            key_grad = mm(turned, queries) + mm_nt(by_offset, pq_back_ref[part, window])
            rows_ref[rows, at_k] = key_grad.astype(BF16)
            rg_query_ref[part, window] += mm_tn(keys[rows], by_offset)
    total = mm_nt(rows_ref[:, :local], wq_ref[...])
    total = total + mm_nt(rows_ref[:, local : 2 * local], wk_ref[...])
    total = total + mm_nt(rows_ref[:, 2 * local :], wv_ref[...])
    part_ref[...] = total.astype(BF16)
    sum_ref[...] += mm_tn(hidden_ref[...], rows_ref[...])

    @pl.when(block == blocks - 1)
    def finish():
        back = one_hot_columns(rel_ref, 1, buckets)

        def by_bucket(rg_ref):
            high, low = split_low(rg_ref[...])
            return (mm_nt(high, back) + mm_nt(low, back)).T

        def through_table(grad):
            high, low = split_low(grad)
            return mm_tn(table_ref[...], high) + mm_tn(table_ref[...], low)

        pos_key = by_bucket(rg_key_ref)
        pos_query = by_bucket(rg_query_ref)
        pos_ref[:, :local] = pos_key.astype(pos_ref.dtype)
        pos_ref[:, local:] = pos_query.astype(pos_ref.dtype)
        grads_ref[:, :local] = (sum_ref[:, :local] + through_table(pos_query)).astype(
            grads_ref.dtype
        )
        grads_ref[:, local : 2 * local] = (
            sum_ref[:, local : 2 * local] + through_table(pos_key)
        ).astype(grads_ref.dtype)
        grads_ref[:, 2 * local :] = sum_ref[:, 2 * local :].astype(grads_ref.dtype)


def backward_attention(
    context_grad, queries, keys, values, weights, pk_back, pq_back,
    hidden, w_query, w_key, w_value, table, rel_rows, kind,
):
    tokens, width = hidden.shape
    local = w_query.shape[1]
    heads = local // HEAD_DIM
    buckets = table.shape[0]
    blocks = tokens // SEQMAX
    whole = lambda *shape: pl.BlockSpec(shape, lambda b: (0,) * len(shape))
    rows = lambda w: pl.BlockSpec((SEQMAX, w), lambda b: (b, 0))
    shape = jax.ShapeDtypeStruct
    return pl.pallas_call(
        backward_kernel,
        grid=(blocks,),
        in_specs=[
            rows(local),
            rows(local),
            rows(local),
            rows(local),
            pl.BlockSpec((1, heads, SEQMAX, SEQMAX), lambda b: (b, 0, 0, 0)),
            whole(local, OFFSETS),
            whole(local, OFFSETS),
            rows(width),
            whole(width, local),
            whole(width, local),
            whole(width, local),
            whole(buckets, width),
            whole(2, OFFSETS),
        ],
        out_specs=[rows(width), whole(width, 3 * local), whole(buckets, 2 * local)],
        out_shape=[
            shape((tokens, width), BF16),
            shape((width, 3 * local), kind),
            shape((buckets, 2 * local), kind),
        ],
        scratch_shapes=[
            pltpu.VMEM((SEQMAX, SEQMAX), BF16),
            pltpu.VMEM((SEQMAX, 3 * local), BF16),
            pltpu.VMEM((local, OFFSETS), F32),
            pltpu.VMEM((local, OFFSETS), F32),
            pltpu.VMEM((width, 3 * local), F32),
        ],
        compiler_params=pltpu.CompilerParams(
            dimension_semantics=("arbitrary",), vmem_limit_bytes=48 * 2**20
        ),
        cost_estimate=pl.CostEstimate(
            flops=16_000_000_000, bytes_accessed=16_000_000, transcendentals=0
        ),
        name="attention_backward",
    )(
        context_grad, queries, keys, values, weights, pk_back, pq_back,
        hidden, w_query, w_key, w_value, table, rel_rows,
    )


def offset_rows(rel_buckets):
    plain = jnp.concatenate([rel_buckets[::-1], rel_buckets[:1]])
    back = plain.reshape(OFFSETS // TILE, TILE)[:, ::-1].reshape(OFFSETS)
    return jnp.stack([plain, back])


def exact_dot(left, right):
    return jnp.dot(left, right, precision=lax.Precision.HIGHEST, preferred_element_type=F32)


def float_dot(left, right):
    return jnp.dot(left, right, preferred_element_type=F32)


def layer_norm(resid, gain, offset):
    average = jnp.mean(resid, axis=-1, keepdims=True)
    centered = resid - average
    variance = jnp.mean(centered * centered, axis=-1, keepdims=True)
    return centered * lax.rsqrt(variance + NORM_EPS) * gain + offset


def exact_gelu(pre_act):
    return jax.nn.gelu(pre_act, approximate=False)


def shards(
    hidden,
    out_grad,
    w_query,
    w_key,
    w_value,
    w_out,
    w_in,
    w_down,
    bucket_table,
    gain_one,
    bias_one,
    gain_two,
    bias_two,
    rel_buckets,
    group_counts,
    key_mask,
):
    local_width = w_query.shape[1]
    rel_rows = offset_rows(rel_buckets)
    query_rows, key_rows, value_rows, weights, context, pk_back, pq_back = forward_attention(
        hidden, w_query, w_key, w_value, bucket_table, rel_rows, group_counts, key_mask
    )
    attn_out = lax.psum(float_dot(context, w_out).astype(jnp.bfloat16), "tensor").astype(
        jnp.float32
    )
    first_norm, norm_one_back = jax.vjp(
        layer_norm, hidden.astype(jnp.float32) + attn_out, gain_one, bias_one
    )
    first_low = first_norm.astype(jnp.bfloat16)
    pre_act = float_dot(first_low, w_in)
    activated_full, gelu_back = jax.vjp(exact_gelu, pre_act)
    activated = activated_full.astype(jnp.bfloat16)
    ffn_out = lax.psum(float_dot(activated, w_down).astype(jnp.bfloat16), "tensor").astype(
        jnp.float32
    )
    second_norm, norm_two_back = jax.vjp(layer_norm, first_norm + ffn_out, gain_two, bias_two)
    output = second_norm.astype(jnp.bfloat16)
    second_grad, grad_gain_two, grad_bias_two = norm_two_back(out_grad.astype(jnp.float32))
    ffn_grad = second_grad.astype(jnp.bfloat16)
    down_local = jnp.einsum("tf,td->fd", activated, ffn_grad, preferred_element_type=jnp.float32)
    act_grad = jnp.einsum("td,fd->tf", ffn_grad, w_down, preferred_element_type=jnp.float32)
    pre_grad = gelu_back(act_grad)[0].astype(jnp.bfloat16)
    in_local = jnp.einsum("tc,tf->cf", first_low, pre_grad, preferred_element_type=jnp.float32)
    back_part = jnp.einsum("tf,cf->tc", pre_grad, w_in, preferred_element_type=jnp.float32)
    first_grad = second_grad + lax.psum(back_part.astype(jnp.bfloat16), "tensor").astype(
        jnp.float32
    )
    resid_grad, grad_gain_one, grad_bias_one = norm_one_back(first_grad)
    attn_grad = resid_grad.astype(jnp.bfloat16)
    out_local = jnp.einsum("tk,td->kd", context, attn_grad, preferred_element_type=jnp.float32)
    context_grad = jnp.einsum(
        "td,kd->tk", attn_grad, w_out, preferred_element_type=jnp.float32
    ).astype(jnp.bfloat16)

    hidden_part, local_grads, pos_grads = backward_attention(
        context_grad, query_rows, key_rows, value_rows, weights, pk_back, pq_back,
        hidden, w_query, w_key, w_value, bucket_table, rel_rows, F32,
    )
    grad_hidden = (
        resid_grad + lax.psum(hidden_part.astype(jnp.bfloat16), "tensor").astype(jnp.float32)
    ).astype(jnp.bfloat16)
    query_local = local_grads[:, :local_width]
    key_local = local_grads[:, local_width : 2 * local_width]
    value_local = local_grads[:, 2 * local_width :]
    key_wide = w_key.astype(jnp.float32)
    query_wide = w_query.astype(jnp.float32)
    table_part = exact_dot(pos_grads[:, :local_width], key_wide.T)
    table_part = table_part + exact_dot(pos_grads[:, local_width:], query_wide.T)
    shares = (
        lax.psum_scatter(query_local, "dp", scatter_dimension=0, tiled=True),
        lax.psum_scatter(key_local, "dp", scatter_dimension=0, tiled=True),
        lax.psum_scatter(value_local, "dp", scatter_dimension=0, tiled=True),
        lax.psum_scatter(out_local, "dp", scatter_dimension=1, tiled=True),
        lax.psum_scatter(in_local, "dp", scatter_dimension=0, tiled=True),
        lax.psum_scatter(down_local, "dp", scatter_dimension=1, tiled=True),
        lax.psum_scatter(grad_gain_one, "dp", scatter_dimension=0, tiled=True),
        lax.psum_scatter(grad_bias_one, "dp", scatter_dimension=0, tiled=True),
        lax.psum_scatter(grad_gain_two, "dp", scatter_dimension=0, tiled=True),
        lax.psum_scatter(grad_bias_two, "dp", scatter_dimension=0, tiled=True),
    )
    gathered = (
        lax.all_gather(shares[0].astype(jnp.bfloat16), "dp", axis=0, tiled=True).astype(
            jnp.float32
        ),
        lax.all_gather(shares[1].astype(jnp.bfloat16), "dp", axis=0, tiled=True).astype(
            jnp.float32
        ),
        lax.all_gather(shares[2].astype(jnp.bfloat16), "dp", axis=0, tiled=True).astype(
            jnp.float32
        ),
        lax.all_gather(shares[3].astype(jnp.bfloat16), "dp", axis=1, tiled=True).astype(
            jnp.float32
        ),
        lax.all_gather(shares[4].astype(jnp.bfloat16), "dp", axis=0, tiled=True).astype(
            jnp.float32
        ),
        lax.all_gather(shares[5].astype(jnp.bfloat16), "dp", axis=1, tiled=True).astype(
            jnp.float32
        ),
        lax.all_gather(shares[6].astype(jnp.bfloat16), "dp", axis=0, tiled=True).astype(
            jnp.float32
        ),
        lax.all_gather(shares[7].astype(jnp.bfloat16), "dp", axis=0, tiled=True).astype(
            jnp.float32
        ),
        lax.all_gather(shares[8].astype(jnp.bfloat16), "dp", axis=0, tiled=True).astype(
            jnp.float32
        ),
        lax.all_gather(shares[9].astype(jnp.bfloat16), "dp", axis=0, tiled=True).astype(
            jnp.float32
        ),
    )
    grad_query = gathered[0]
    grad_key = gathered[1]
    table_share = lax.psum_scatter(table_part, ("dp", "tensor"), scatter_dimension=0, tiled=True)
    grad_table = lax.all_gather(table_share, ("dp", "tensor"), axis=0, tiled=True)
    return (
        output,
        grad_hidden,
        grad_query,
        grad_key,
        gathered[2],
        gathered[3],
        gathered[4],
        gathered[5],
        grad_table,
        gathered[6],
        gathered[7],
        gathered[8],
        gathered[9],
    )


def solution(mesh):
    in_specs = (
        P("dp", None),
        P("dp", None),
        P(None, "tensor"),
        P(None, "tensor"),
        P(None, "tensor"),
        P("tensor", None),
        P(None, "tensor"),
        P("tensor", None),
        P(),
        P(),
        P(),
        P(),
        P(),
        P(),
        P("dp", None),
        P("dp"),
    )
    out_specs = (
        P("dp", None),
        P("dp", None),
        P(None, "tensor"),
        P(None, "tensor"),
        P(None, "tensor"),
        P("tensor", None),
        P(None, "tensor"),
        P("tensor", None),
        P(),
        P(),
        P(),
        P(),
        P(),
    )
    return jax.shard_map(shards, mesh=mesh, in_specs=in_specs, out_specs=out_specs, check_vma=False)
```

```python
import functools
import math

import jax
import jax.numpy as jnp
from jax import lax
from jax.experimental import pallas as pl
from jax.experimental.pallas import tpu as pltpu
from jax.sharding import PartitionSpec as P

NORM_EPS = 1e-07
HEAD_DIM = 64
SEQMAX = 512
TILE = 128
WINDOW = SEQMAX + TILE
OFFSETS = 2 * SEQMAX
NEGATIVE = -1e30
F32 = jnp.float32
BF16 = jnp.bfloat16


def score_factor():
    return 1.0 / math.sqrt(3.0 * HEAD_DIM)


def mm(left, right):
    return jnp.dot(left, right, preferred_element_type=F32)


def mm_nt(left, right):
    return lax.dot_general(left, right, (((1,), (1,)), ((), ())), preferred_element_type=F32)


def mm_tn(left, right):
    return lax.dot_general(left, right, (((0,), (0,)), ((), ())), preferred_element_type=F32)


def starts_of(places, counts_ref):
    long_end = SEQMAX * counts_ref[0, 0]
    mid_end = long_end + SEQMAX // 2 * counts_ref[0, 1]
    in_long = places < long_end
    in_mid = places < mid_end
    anchor = jnp.where(in_long, 0, jnp.where(in_mid, long_end, mid_end))
    shift = jnp.where(in_long, 9, jnp.where(in_mid, 8, 7))
    return anchor + lax.shift_left(lax.shift_right_logical(places - anchor, shift), shift)


def tile_iotas():
    rows = lax.broadcasted_iota(jnp.int32, (TILE, TILE), 0)
    lanes = lax.broadcasted_iota(jnp.int32, (TILE, TILE), 1)
    return rows, lanes


def lane_tiles(wide):
    return [wide[:, c : c + TILE] for c in range(0, wide.shape[1], TILE)]


def skew(wide):
    rows, lanes = tile_iotas()
    keep = lanes <= rows
    turned = [pltpu.roll(part, 1, 1, stride=1, stride_axis=0) for part in lane_tiles(wide)]
    return jnp.concatenate(
        [jnp.where(keep, turned[c], turned[c + 1]) for c in range(len(turned) - 1)], axis=1
    )


def unskew(flipped):
    rows, lanes = tile_iotas()
    late = lanes > rows
    turned = [pltpu.roll(part, 1, 1, stride=1, stride_axis=0) for part in lane_tiles(flipped)]
    zero = jnp.zeros((TILE, TILE), F32)
    turned = [zero] + turned + [zero]
    return jnp.concatenate(
        [jnp.where(late, turned[c], turned[c + 1]) for c in range(len(turned) - 1)], axis=1
    )


def window_of(tile_at):
    low = SEQMAX - TILE - tile_at
    return slice(low, low + WINDOW)


def one_hot_columns(rel_ref, row, buckets):
    ids = lax.broadcasted_iota(jnp.int32, (buckets, OFFSETS), 0)
    return (ids == rel_ref[row : row + 1, :]).astype(BF16)


def split_low(wide):
    high = wide.astype(BF16)
    return high, (wide - high.astype(F32)).astype(BF16)


def forward_kernel(
    hidden_ref, wq_ref, wk_ref, wv_ref, table_ref, rel_ref, counts_ref, mask_ref,
    q_ref, k_ref, v_ref, weights_ref, context_ref, pk_back_ref, pq_back_ref,
    pk_ref, pq_ref, bias_ref, rel_score_ref,
):
    block = pl.program_id(0)
    buckets = table_ref.shape[0]
    heads = wq_ref.shape[1] // HEAD_DIM

    @pl.when(block == 0)
    def tables():
        table = table_ref[...]
        pos_key = lax.dot_general(
            wk_ref[...], table, (((0,), (1,)), ((), ())), preferred_element_type=F32
        ).astype(BF16)
        pos_query = lax.dot_general(
            wq_ref[...], table, (((0,), (1,)), ((), ())), preferred_element_type=F32
        ).astype(BF16)
        plain = one_hot_columns(rel_ref, 0, buckets)
        pk_ref[...] = mm(pos_key, plain).astype(BF16)
        pq_ref[...] = mm(pos_query, plain).astype(BF16)
        back = one_hot_columns(rel_ref, 1, buckets)
        pk_back_ref[...] = mm(pos_key, back).astype(BF16)
        pq_back_ref[...] = mm(pos_query, back).astype(BF16)

    first = block * SEQMAX
    column = starts_of(lax.broadcasted_iota(jnp.int32, (SEQMAX, 1), 0) + first, counts_ref)
    row = starts_of(lax.broadcasted_iota(jnp.int32, (1, SEQMAX), 1) + first, counts_ref)
    row = jnp.where(mask_ref[0] == 1, row, -1)
    bias_ref[...] = jnp.where(column == row, 0.0, NEGATIVE)

    hidden = hidden_ref[...]
    q_ref[...] = mm(hidden, wq_ref[...]).astype(BF16)
    k_ref[...] = mm(hidden, wk_ref[...]).astype(BF16)
    v_ref[...] = mm(hidden, wv_ref[...]).astype(BF16)
    for head in range(heads):
        part = slice(head * HEAD_DIM, (head + 1) * HEAD_DIM)
        queries = q_ref[:, part]
        keys = k_ref[:, part]
        values = v_ref[:, part]
        for at in range(0, SEQMAX, TILE):
            rel = mm(keys[at : at + TILE], pq_ref[part, window_of(at)])
            rel_score_ref[at : at + TILE, :] = skew(rel)
        for at in range(0, SEQMAX, TILE):
            rows = slice(at, at + TILE)
            raw = mm_nt(queries[rows], keys)
            raw = raw + skew(mm(queries[rows], pk_ref[part, window_of(at)]))
            raw = raw + rel_score_ref[:, rows].T
            scaled = raw * score_factor() + bias_ref[rows, :]
            top = jnp.max(scaled, axis=-1, keepdims=True)
            exponent = jnp.exp(scaled - top)
            total = jnp.sum(exponent, axis=-1, keepdims=True)
            weights = exponent * (1.0 / total)
            weights_ref[0, head, rows, :] = weights
            context_ref[rows, part] = mm(weights.astype(BF16), values).astype(BF16)


def forward_attention(hidden, w_query, w_key, w_value, table, rel_rows, counts, key_mask):
    tokens, width = hidden.shape
    local = w_query.shape[1]
    heads = local // HEAD_DIM
    buckets = table.shape[0]
    blocks = tokens // SEQMAX
    whole = lambda *shape: pl.BlockSpec(shape, lambda b: (0,) * len(shape))
    rows = lambda w: pl.BlockSpec((SEQMAX, w), lambda b: (b, 0))
    shape = jax.ShapeDtypeStruct
    return pl.pallas_call(
        forward_kernel,
        grid=(blocks,),
        in_specs=[
            rows(width),
            whole(width, local),
            whole(width, local),
            whole(width, local),
            whole(buckets, width),
            whole(2, OFFSETS),
            pl.BlockSpec(memory_space=pltpu.SMEM),
            pl.BlockSpec((1, 1, SEQMAX), lambda b: (b, 0, 0)),
        ],
        out_specs=[
            rows(local),
            rows(local),
            rows(local),
            pl.BlockSpec((1, heads, SEQMAX, SEQMAX), lambda b: (b, 0, 0, 0)),
            rows(local),
            whole(local, OFFSETS),
            whole(local, OFFSETS),
        ],
        out_shape=[
            shape((tokens, local), BF16),
            shape((tokens, local), BF16),
            shape((tokens, local), BF16),
            shape((blocks, heads, SEQMAX, SEQMAX), F32),
            shape((tokens, local), BF16),
            shape((local, OFFSETS), BF16),
            shape((local, OFFSETS), BF16),
        ],
        scratch_shapes=[
            pltpu.VMEM((local, OFFSETS), BF16),
            pltpu.VMEM((local, OFFSETS), BF16),
            pltpu.VMEM((SEQMAX, SEQMAX), F32),
            pltpu.VMEM((SEQMAX, SEQMAX), F32),
        ],
        compiler_params=pltpu.CompilerParams(
            dimension_semantics=("arbitrary",), vmem_limit_bytes=40 * 2**20
        ),
        cost_estimate=pl.CostEstimate(
            flops=8_000_000_000, bytes_accessed=12_000_000, transcendentals=1_600_000
        ),
        name="attention_forward",
    )(hidden, w_query, w_key, w_value, table, rel_rows, counts, key_mask.reshape(blocks, 1, SEQMAX))


def backward_kernel(
    order_ref, cg_ref, q_ref, k_ref, v_ref, weights_ref, pk_back_ref, pq_back_ref,
    hidden_ref, wq_ref, wk_ref, wv_ref, table_ref, rel_ref,
    part_ref, grads_ref, pos_ref,
    ds_ref, rows_ref, rg_key_ref, rg_query_ref, sum_ref,
):
    block = pl.program_id(0)
    blocks = pl.num_programs(0)
    local = wq_ref.shape[1]
    heads = local // HEAD_DIM
    buckets = table_ref.shape[0]

    @pl.when(block == 0)
    def clear():
        rg_key_ref[...] = jnp.zeros_like(rg_key_ref)
        rg_query_ref[...] = jnp.zeros_like(rg_query_ref)
        sum_ref[...] = jnp.zeros_like(sum_ref)

    tile_rows, tile_lanes = tile_iotas()
    flip = (tile_rows + tile_lanes == TILE - 1).astype(BF16)

    def flipped(low):
        return jnp.concatenate([mm(part, flip) for part in lane_tiles(low)], axis=1)

    for head in range(heads):
        part = slice(head * HEAD_DIM, (head + 1) * HEAD_DIM)
        at_k = slice(local + head * HEAD_DIM, local + (head + 1) * HEAD_DIM)
        at_v = slice(2 * local + head * HEAD_DIM, 2 * local + (head + 1) * HEAD_DIM)
        queries = q_ref[:, part]
        keys = k_ref[:, part]
        values = v_ref[:, part]
        value_grad = jnp.zeros((SEQMAX, HEAD_DIM), F32)
        for at in range(0, SEQMAX, TILE):
            rows = slice(at, at + TILE)
            weights = weights_ref[0, head, rows, :]
            cotangent = cg_ref[order_ref[at // TILE], 0, :, part]
            weight_grad = mm_nt(cotangent, values)
            inner = jnp.sum(weights * weight_grad, axis=-1, keepdims=True)
            score_grad = (weights * (weight_grad - inner) * score_factor()).astype(BF16)
            ds_ref[rows, :] = score_grad
            value_grad = value_grad + mm_tn(weights.astype(BF16), cotangent)
            by_offset = unskew(flipped(score_grad)).astype(BF16)
            window = window_of(at)
            query_grad = mm(score_grad, keys) + mm_nt(by_offset, pk_back_ref[part, window])
            rows_ref[rows, part] = query_grad.astype(BF16)
            rg_key_ref[part, window] += mm_tn(queries[rows], by_offset)
        rows_ref[:, at_v] = value_grad.astype(BF16)
        for at in range(0, SEQMAX, TILE):
            rows = slice(at, at + TILE)
            turned = ds_ref[:, rows].T
            by_offset = unskew(flipped(turned)).astype(BF16)
            window = window_of(at)
            key_grad = mm(turned, queries) + mm_nt(by_offset, pq_back_ref[part, window])
            rows_ref[rows, at_k] = key_grad.astype(BF16)
            rg_query_ref[part, window] += mm_tn(keys[rows], by_offset)
    total = mm_nt(rows_ref[:, :local], wq_ref[...])
    total = total + mm_nt(rows_ref[:, local : 2 * local], wk_ref[...])
    total = total + mm_nt(rows_ref[:, 2 * local :], wv_ref[...])
    for at in range(0, SEQMAX, TILE):
        part_ref[at // TILE, 0] = total[at : at + TILE].astype(BF16)
    sum_ref[...] += mm_tn(hidden_ref[...], rows_ref[...])

    @pl.when(block == blocks - 1)
    def finish():
        back = one_hot_columns(rel_ref, 1, buckets)

        def by_bucket(rg_ref):
            high, low = split_low(rg_ref[...])
            return (mm_nt(high, back) + mm_nt(low, back)).T

        def through_table(grad):
            high, low = split_low(grad)
            return mm_tn(table_ref[...], high) + mm_tn(table_ref[...], low)

        pos_key = by_bucket(rg_key_ref)
        pos_query = by_bucket(rg_query_ref)
        pos_ref[:, :local] = pos_key.astype(pos_ref.dtype)
        pos_ref[:, local:] = pos_query.astype(pos_ref.dtype)
        grads_ref[:, :local] = (sum_ref[:, :local] + through_table(pos_query)).astype(
            grads_ref.dtype
        )
        grads_ref[:, local : 2 * local] = (
            sum_ref[:, local : 2 * local] + through_table(pos_key)
        ).astype(grads_ref.dtype)
        grads_ref[:, 2 * local :] = sum_ref[:, 2 * local :].astype(grads_ref.dtype)


def backward_attention(
    order, context_grad, queries, keys, values, weights, pk_back, pq_back,
    hidden, w_query, w_key, w_value, table, rel_rows, kind,
):
    tokens, width = hidden.shape
    local = w_query.shape[1]
    heads = local // HEAD_DIM
    buckets = table.shape[0]
    blocks = tokens // SEQMAX
    groups = SEQMAX // TILE
    whole = lambda *shape: pl.BlockSpec(shape, lambda b: (0,) * len(shape))
    rows = lambda w: pl.BlockSpec((SEQMAX, w), lambda b: (b, 0))
    shape = jax.ShapeDtypeStruct
    return pl.pallas_call(
        backward_kernel,
        grid=(blocks,),
        in_specs=[
            pl.BlockSpec(memory_space=pltpu.SMEM),
            pl.BlockSpec((groups, 1, TILE, local), lambda b: (0, b, 0, 0)),
            rows(local),
            rows(local),
            rows(local),
            pl.BlockSpec((1, heads, SEQMAX, SEQMAX), lambda b: (b, 0, 0, 0)),
            whole(local, OFFSETS),
            whole(local, OFFSETS),
            rows(width),
            whole(width, local),
            whole(width, local),
            whole(width, local),
            whole(buckets, width),
            whole(2, OFFSETS),
        ],
        out_specs=[
            pl.BlockSpec((groups, 1, TILE, width), lambda b: (0, b, 0, 0)),
            whole(width, 3 * local),
            whole(buckets, 2 * local),
        ],
        out_shape=[
            shape((groups, blocks, TILE, width), BF16),
            shape((width, 3 * local), kind),
            shape((buckets, 2 * local), kind),
        ],
        scratch_shapes=[
            pltpu.VMEM((SEQMAX, SEQMAX), BF16),
            pltpu.VMEM((SEQMAX, 3 * local), BF16),
            pltpu.VMEM((local, OFFSETS), F32),
            pltpu.VMEM((local, OFFSETS), F32),
            pltpu.VMEM((width, 3 * local), F32),
        ],
        compiler_params=pltpu.CompilerParams(
            dimension_semantics=("arbitrary",), vmem_limit_bytes=48 * 2**20
        ),
        cost_estimate=pl.CostEstimate(
            flops=16_000_000_000, bytes_accessed=16_000_000, transcendentals=0
        ),
        name="attention_backward",
    )(
        order, context_grad, queries, keys, values, weights, pk_back, pq_back,
        hidden, w_query, w_key, w_value, table, rel_rows,
    )


def offset_rows(rel_buckets):
    plain = jnp.concatenate([rel_buckets[::-1], rel_buckets[:1]])
    back = plain.reshape(OFFSETS // TILE, TILE)[:, ::-1].reshape(OFFSETS)
    return jnp.stack([plain, back])


CHUNKS = 8
PAD_ROWS = 64


def layer_norm_parts(resid):
    centered = resid - jnp.mean(resid, axis=-1, keepdims=True)
    scale = lax.rsqrt(jnp.mean(centered * centered, axis=-1, keepdims=True) + NORM_EPS)
    return centered * scale, scale


def layer_norm_back(normal, scale, grad, gain):
    inner = grad * gain
    mean = jnp.mean(inner, axis=-1, keepdims=True)
    along = jnp.mean(inner * normal, axis=-1, keepdims=True)
    return scale * (inner - mean - normal * along)


def token_kernel(
    order_ref, context_ref, hidden_ref, out_grad_ref, norms_ref, packed_ref,
    output_ref, context_grad_ref, resid_ref, first_low_ref, act_ref, pre_grad_ref, ffn_grad_ref,
    attn_grad_ref, norm_grads_ref,
    packed_vmem, slope_ref, sems,
):
    groups = packed_vmem.shape[0]
    width = hidden_ref.shape[1]
    hidden_units = act_ref.shape[2]
    local = context_ref.shape[2]
    copies = [
        pltpu.make_async_copy(packed_ref.at[:, g], packed_vmem.at[g], sems.at[g])
        for g in range(groups)
    ]
    for copy in copies:
        copy.start()

    def packed(g):
        return packed_vmem[g].reshape(-1, width)

    def w_in(g):
        return packed(g)[:width]

    def w_down(g):
        return packed(g)[width : width + hidden_units]

    def w_out(g):
        return packed(g)[width + hidden_units : width + hidden_units + local]

    for copy in copies:
        copy.wait()
    gain_one, bias_one = norms_ref[0:1, :], norms_ref[1:2, :]
    gain_two, bias_two = norms_ref[2:3, :], norms_ref[3:4, :]
    resid = hidden_ref[...].astype(F32)
    for g in range(groups):
        resid = resid + mm(context_ref[order_ref[g]], w_out(g)).astype(BF16).astype(F32)
    normal_one, scale_one = layer_norm_parts(resid)
    first_norm = normal_one * gain_one + bias_one
    first_low = first_norm.astype(BF16)
    first_low_ref[...] = first_low
    ffn_out = first_norm
    for g in range(groups):
        pre_act = mm(first_low, w_in(g))
        area = 0.5 * (1.0 + lax.erf(pre_act * math.sqrt(0.5)))
        activated = (pre_act * area).astype(BF16)
        act_ref[g] = activated
        density = jnp.exp(-0.5 * pre_act * pre_act) * (1.0 / math.sqrt(2.0 * math.pi))
        slope_ref[g] = area + pre_act * density
        ffn_out = ffn_out + mm(activated, w_down(g)).astype(BF16).astype(F32)
    normal_two, scale_two = layer_norm_parts(ffn_out)
    output_ref[...] = (normal_two * gain_two + bias_two).astype(BF16)
    out_grad = out_grad_ref[...].astype(F32)
    norm_grads_ref[...] = jnp.zeros_like(norm_grads_ref)
    norm_grads_ref[2:3, :] = jnp.sum(out_grad * normal_two, axis=0, keepdims=True)
    norm_grads_ref[3:4, :] = jnp.sum(out_grad, axis=0, keepdims=True)
    second_grad = layer_norm_back(normal_two, scale_two, out_grad, gain_two)
    ffn_grad = second_grad.astype(BF16)
    ffn_grad_ref[...] = ffn_grad
    first_grad = second_grad
    for g in range(groups):
        pre_grad = (mm_nt(ffn_grad, w_down(g)) * slope_ref[g]).astype(BF16)
        pre_grad_ref[g] = pre_grad
        first_grad = first_grad + mm_nt(pre_grad, w_in(g))
    norm_grads_ref[0:1, :] = jnp.sum(first_grad * normal_one, axis=0, keepdims=True)
    norm_grads_ref[1:2, :] = jnp.sum(first_grad, axis=0, keepdims=True)
    resid_grad = layer_norm_back(normal_one, scale_one, first_grad, gain_one)
    resid_ref[...] = resid_grad
    attn_grad = resid_grad.astype(BF16)
    attn_grad_ref[...] = attn_grad
    for g in range(groups):
        context_grad_ref[g] = mm_nt(attn_grad, w_out(g)).astype(BF16)


def token_layer(order, context, hidden, out_grad, norms, packed):
    chunks, groups, chunk_rows, width = packed.shape
    tokens = hidden.shape[0]
    local = context.shape[2]
    units = chunks * chunk_rows - PAD_ROWS - local - width
    shape = jax.ShapeDtypeStruct
    vmem = pl.BlockSpec(memory_space=pltpu.VMEM)
    return pl.pallas_call(
        token_kernel,
        in_specs=[pl.BlockSpec(memory_space=pltpu.SMEM)]
        + [vmem] * 4
        + [pl.BlockSpec(memory_space=pl.ANY)],
        out_specs=[vmem] * 9,
        out_shape=[
            shape((tokens, width), BF16),
            shape((groups, tokens, local), BF16),
            shape((tokens, width), F32),
            shape((tokens, width), BF16),
            shape((groups, tokens, units), BF16),
            shape((groups, tokens, units), BF16),
            shape((tokens, width), BF16),
            shape((tokens, width), BF16),
            shape((8, width), F32),
        ],
        scratch_shapes=[
            pltpu.VMEM((groups, chunks, chunk_rows, width), BF16),
            pltpu.VMEM((groups, tokens, units), F32),
            pltpu.SemaphoreType.DMA((groups,)),
        ],
        compiler_params=pltpu.CompilerParams(vmem_limit_bytes=48 * 2**20),
        cost_estimate=pl.CostEstimate(
            flops=5_000_000_000, bytes_accessed=18_000_000, transcendentals=1_600_000
        ),
        name="token_layer",
    )(order, context, hidden, out_grad, norms, packed)


def weight_grad_kernel(
    order_ref, context_ref, first_low_ref, act_ref, pre_grad_ref, ffn_grad_ref, attn_grad_ref,
    out_ref,
):
    whole = jnp.concatenate(
        [
            mm_tn(first_low_ref[...], pre_grad_ref[0]),
            mm_tn(act_ref[0], ffn_grad_ref[...]),
            mm_tn(context_ref[0], attn_grad_ref[...]),
            jnp.zeros((PAD_ROWS, first_low_ref.shape[1]), F32),
        ],
        axis=0,
    ).astype(BF16)
    rows = out_ref.shape[2]
    for chunk in range(out_ref.shape[0]):
        out_ref[chunk, 0] = whole[chunk * rows : (chunk + 1) * rows]


def weight_grads(order, context, first_low, act, pre_grad, ffn_grad, attn_grad):
    groups, tokens, units = act.shape
    width = first_low.shape[1]
    local = context.shape[2]
    rows = (width + units + local + PAD_ROWS) // CHUNKS
    whole = lambda *shape: pl.BlockSpec(shape, lambda g, order: (0,) * len(shape))
    group = lambda w: pl.BlockSpec((1, tokens, w), lambda g, order: (g, 0, 0))
    return pl.pallas_call(
        weight_grad_kernel,
        grid_spec=pltpu.PrefetchScalarGridSpec(
            num_scalar_prefetch=1,
            grid=(groups,),
            in_specs=[
                pl.BlockSpec((1, tokens, local), lambda g, order: (order[g], 0, 0)),
                whole(tokens, width),
                group(units),
                group(units),
                whole(tokens, width),
                whole(tokens, width),
            ],
            out_specs=pl.BlockSpec((CHUNKS, 1, rows, width), lambda g, order: (0, g, 0, 0)),
        ),
        out_shape=jax.ShapeDtypeStruct((CHUNKS, groups, rows, width), BF16),
        compiler_params=pltpu.CompilerParams(
            dimension_semantics=("arbitrary",), vmem_limit_bytes=40 * 2**20
        ),
        cost_estimate=pl.CostEstimate(
            flops=2_800_000_000, bytes_accessed=14_000_000, transcendentals=0
        ),
        name="weight_grads",
    )(order, context, first_low, act, pre_grad, ffn_grad, attn_grad)


def place_kernel(order_ref, *refs):
    out_ref = refs[-1]
    for shift, piece_ref in enumerate(refs[:-1]):
        out_ref[:, order_ref[shift]] = piece_ref[...].reshape(out_ref.shape[0], TILE, -1)


def place(order, pieces):
    rows, width = pieces[0].shape
    blocks = rows // TILE
    vmem = pl.BlockSpec(memory_space=pltpu.VMEM)
    out = pl.pallas_call(
        place_kernel,
        in_specs=[pl.BlockSpec(memory_space=pltpu.SMEM)] + [vmem] * len(pieces),
        out_specs=vmem,
        out_shape=jax.ShapeDtypeStruct((blocks, len(pieces), TILE, width), BF16),
        cost_estimate=pl.CostEstimate(flops=0, bytes_accessed=3_000_000, transcendentals=0),
        name="place",
    )(order, *pieces)
    return out.reshape(rows * len(pieces), width)


def send(array, shift, size):
    return lax.ppermute(array, "tensor", [(i, (i + shift) % size) for i in range(size)])


def exchange(array, me, size):
    pick = lambda s: lax.dynamic_index_in_dim(array, (me + s) % size, 0, keepdims=False)
    return [pick(0)] + [send(pick(s), s, size) for s in range(1, size)]


def spread(array, size):
    return [array] + [send(array, s, size) for s in range(1, size)]


def halve(array, axis_index, bits):
    size = 2 ** len(bits)
    for bit in bits:
        half = array.shape[0] // 2
        mine = (axis_index >> bit) & 1
        keep = lax.dynamic_slice_in_dim(array, mine * half, half, 0)
        give = lax.dynamic_slice_in_dim(array, (1 - mine) * half, half, 0)
        pairs = [(i, i ^ (1 << bit)) for i in range(size)]
        got = lax.ppermute(give, "dp", pairs)
        array = (keep.astype(F32) + got.astype(F32)).astype(BF16)
    return array


def double(array, axis_index, bits):
    size = 2 ** len(bits)
    for bit in bits[::-1]:
        pairs = [(i, i ^ (1 << bit)) for i in range(size)]
        got = lax.ppermute(array, "dp", pairs)
        low = (axis_index >> bit) & 1 == 0
        array = jnp.where(
            low, jnp.concatenate([array, got], 0), jnp.concatenate([got, array], 0)
        )
    return array


def shards(
    n_dp,
    n_tensor,
    hidden,
    out_grad,
    w_query,
    w_key,
    w_value,
    w_out,
    w_in,
    w_down,
    bucket_table,
    gain_one,
    bias_one,
    gain_two,
    bias_two,
    rel_buckets,
    group_counts,
    key_mask,
):
    tokens, width = hidden.shape
    local = w_query.shape[1]
    units = w_in.shape[1]
    buckets = bucket_table.shape[0]
    blocks = tokens // SEQMAX
    mine = tokens // n_tensor
    replica = lax.axis_index("dp")
    me = lax.axis_index("tensor")
    order = (me - jnp.arange(n_tensor, dtype=jnp.int32)) % n_tensor
    rel_rows = offset_rows(rel_buckets)

    packed = jnp.concatenate([w_in, w_down, w_out, jnp.zeros((PAD_ROWS, width), BF16)], 0)
    chunk_rows = packed.shape[0] // CHUNKS
    if n_dp == CHUNKS:
        piece = lax.dynamic_slice_in_dim(packed, replica * chunk_rows, chunk_rows, 0)
        packed = lax.all_gather(piece, ("dp", "tensor"), axis=0, tiled=False)
        packed = packed.reshape(CHUNKS, n_tensor, chunk_rows, width)
    else:
        packed = lax.all_gather(packed, "tensor", axis=0, tiled=False)
        packed = packed.reshape(n_tensor, CHUNKS, chunk_rows, width).swapaxes(0, 1)

    def my_rows(array):
        array = array.reshape(blocks, n_tensor, TILE, width)
        return lax.dynamic_index_in_dim(array, me, 1, keepdims=False).reshape(mine, width)

    query_rows, key_rows, value_rows, weights, context, pk_back, pq_back = forward_attention(
        hidden, w_query, w_key, w_value, bucket_table, rel_rows, group_counts, key_mask
    )
    pieces = context.reshape(blocks, n_tensor, TILE, local).swapaxes(0, 1)
    pieces = pieces.reshape(n_tensor, mine, local)
    context = jnp.stack(exchange(pieces, me, n_tensor))
    norms = jnp.stack([gain_one, bias_one, gain_two, bias_two])
    (
        output, context_grad, resid_grad, first_low, act, pre_grad, ffn_grad, attn_grad, norm_grads,
    ) = token_layer(order, context, my_rows(hidden), my_rows(out_grad), norms, packed)
    context_grad = jnp.stack(exchange(context_grad, me, n_tensor))
    context_grad = context_grad.reshape(n_tensor, blocks, TILE, local)
    output = place(order, spread(output, n_tensor))
    grads = weight_grads(order, context, first_low, act, pre_grad, ffn_grad, attn_grad)
    if n_dp == CHUNKS:
        grads = lax.psum_scatter(grads, "dp", scatter_dimension=0, tiled=True)
        grads = lax.psum_scatter(grads[0], "tensor", scatter_dimension=0, tiled=True)
        grads = lax.all_gather(grads[0], "dp", axis=0, tiled=True)
    else:
        grads = grads.swapaxes(0, 1).reshape(n_tensor, CHUNKS * chunk_rows, width)
        grads = lax.psum_scatter(grads, "tensor", scatter_dimension=0, tiled=True)
        grads = lax.psum(grads[0], "dp")

    hidden_part, row_grads, pos_grads = backward_attention(
        order, context_grad, query_rows, key_rows, value_rows, weights, pk_back, pq_back,
        hidden, w_query, w_key, w_value, bucket_table, rel_rows, BF16,
    )
    got = exchange(hidden_part.reshape(n_tensor, mine, width), me, n_tensor)
    grad_hidden = resid_grad
    for piece in got:
        grad_hidden = grad_hidden + piece.astype(F32)
    grad_hidden = place(order, spread(grad_hidden.astype(BF16), n_tensor))

    pos_rows, row_rows = buckets // n_dp, width // n_dp
    norm_cols = 4 * width // n_dp
    pos_grads = pos_grads.reshape(n_dp, pos_rows, 2 * local)
    norm_grads = norm_grads[:4].reshape(n_dp, 1, norm_cols).astype(BF16)
    norm_grads = jnp.pad(norm_grads, ((0, 0), (0, 0), (0, 2 * local - norm_cols)))
    pos_grads = jnp.concatenate([pos_grads, norm_grads], 1)
    pos_grads = jnp.pad(pos_grads, ((0, 0), (0, row_rows - pos_rows - 1), (0, 0)))
    joined = jnp.concatenate([pos_grads.reshape(width, 2 * local), row_grads], 1)
    bits = list(range(n_dp.bit_length() - 1))
    joined = halve(joined, replica, bits)
    table_part = mm_nt(joined[:pos_rows, : 2 * local], jnp.concatenate([w_key, w_query], 1))
    norm_part = jnp.pad(joined[pos_rows : pos_rows + 1, :norm_cols], ((0, 0), (0, width - norm_cols)))
    share = jnp.concatenate([table_part.astype(BF16), norm_part], 0)
    share = jnp.pad(share, ((0, row_rows - pos_rows - 1), (0, 0)))
    shares = jnp.stack(spread(share, n_tensor)).astype(F32)
    in_order = [lax.dynamic_index_in_dim(shares, order[g], 0, False) for g in range(n_tensor)]
    share = sum(in_order).astype(BF16)
    joined = double(jnp.concatenate([share, joined[:, 2 * local :]], 1), replica, bits)
    small = joined[:, :width].reshape(n_dp, row_rows, width).astype(F32)
    grad_table = small[:, :pos_rows].reshape(buckets, width)
    norm_grads = small[:, pos_rows, :norm_cols].reshape(4, width)
    row_grads = joined[:, width:].astype(F32)
    grads = grads.astype(F32)
    return (
        output,
        grad_hidden,
        row_grads[:, :local],
        row_grads[:, local : 2 * local],
        row_grads[:, 2 * local :],
        grads[width + units : width + units + local],
        grads[:width],
        grads[width : width + units],
        grad_table,
        norm_grads[0],
        norm_grads[1],
        norm_grads[2],
        norm_grads[3],
    )


def solution(mesh):
    in_specs = (
        P("dp", None),
        P("dp", None),
        P(None, "tensor"),
        P(None, "tensor"),
        P(None, "tensor"),
        P("tensor", None),
        P(None, "tensor"),
        P("tensor", None),
        P(),
        P(),
        P(),
        P(),
        P(),
        P(),
        P("dp", None),
        P("dp"),
    )
    out_specs = (
        P("dp", None),
        P("dp", None),
        P(None, "tensor"),
        P(None, "tensor"),
        P(None, "tensor"),
        P("tensor", None),
        P(None, "tensor"),
        P("tensor", None),
        P(),
        P(),
        P(),
        P(),
        P(),
    )
    body = functools.partial(shards, mesh.shape["dp"], mesh.shape["tensor"])
    return jax.shard_map(body, mesh=mesh, in_specs=in_specs, out_specs=out_specs, check_vma=False)
```

```python
import functools
import math

import jax
import jax.numpy as jnp
from jax import lax
from jax.experimental import pallas as pl
from jax.experimental.pallas import tpu as pltpu
from jax.sharding import PartitionSpec as P

NORM_EPS = 1e-07
HEAD_DIM = 64
SEQMAX = 512
TILE = 128
WINDOW = SEQMAX + TILE
OFFSETS = 2 * SEQMAX
NEGATIVE = -1e30
CHUNKS = 8
CORE, ACROSS_X, ACROSS_Y = 1, 2, 4
OUT_ROWS = 32
F32 = jnp.float32
BF16 = jnp.bfloat16


def score_factor():
    return 1.0 / math.sqrt(3.0 * HEAD_DIM)


def mm(left, right):
    return jnp.dot(left, right, preferred_element_type=F32)


def mm_nt(left, right):
    return lax.dot_general(left, right, (((1,), (1,)), ((), ())), preferred_element_type=F32)


def mm_tn(left, right):
    return lax.dot_general(left, right, (((0,), (0,)), ((), ())), preferred_element_type=F32)


def starts_of(places, counts_ref):
    long_end = SEQMAX * counts_ref[0, 0]
    mid_end = long_end + SEQMAX // 2 * counts_ref[0, 1]
    in_long = places < long_end
    in_mid = places < mid_end
    anchor = jnp.where(in_long, 0, jnp.where(in_mid, long_end, mid_end))
    shift = jnp.where(in_long, 9, jnp.where(in_mid, 8, 7))
    return anchor + lax.shift_left(lax.shift_right_logical(places - anchor, shift), shift)


def tile_iotas():
    rows = lax.broadcasted_iota(jnp.int32, (TILE, TILE), 0)
    lanes = lax.broadcasted_iota(jnp.int32, (TILE, TILE), 1)
    return rows, lanes


def lane_tiles(wide):
    return [wide[:, c : c + TILE] for c in range(0, wide.shape[1], TILE)]


def skew(wide):
    rows, lanes = tile_iotas()
    keep = lanes <= rows
    turned = [pltpu.roll(part, 1, 1, stride=1, stride_axis=0) for part in lane_tiles(wide)]
    return jnp.concatenate(
        [jnp.where(keep, turned[c], turned[c + 1]) for c in range(len(turned) - 1)], axis=1
    )


def unskew(flipped):
    rows, lanes = tile_iotas()
    late = lanes > rows
    turned = [pltpu.roll(part, 1, 1, stride=1, stride_axis=0) for part in lane_tiles(flipped)]
    zero = jnp.zeros((TILE, TILE), F32)
    turned = [zero] + turned + [zero]
    return jnp.concatenate(
        [jnp.where(late, turned[c], turned[c + 1]) for c in range(len(turned) - 1)], axis=1
    )


def window_of(tile_at):
    low = SEQMAX - TILE - tile_at
    return slice(low, low + WINDOW)


def one_hot_columns(rel_ref, row, buckets):
    ids = lax.broadcasted_iota(jnp.int32, (buckets, OFFSETS), 0)
    return (ids == rel_ref[row : row + 1, :]).astype(BF16)


def split_low(wide):
    high = wide.astype(BF16)
    return high, (wide - high.astype(F32)).astype(BF16)


SCALARS = pl.BlockSpec(memory_space=pltpu.SMEM)
ANYWHERE = pl.BlockSpec(memory_space=pl.ANY)
IN_VMEM = pl.BlockSpec(memory_space=pltpu.VMEM)
Shape = jax.ShapeDtypeStruct


def kernel_call(kernel, name, flops, moved, vmem, **rest):
    return pl.pallas_call(
        kernel,
        compiler_params=pltpu.CompilerParams(vmem_limit_bytes=vmem * 2**20),
        cost_estimate=pl.CostEstimate(flops=flops, bytes_accessed=moved, transcendentals=0),
        name=name,
        **rest,
    )


def tables_kernel(wq_ref, wk_ref, table_ref, rel_ref, pk_ref, pq_ref, pk_back_ref, pq_back_ref):
    table = table_ref[...]
    buckets = table.shape[0]
    turned = (((0,), (1,)), ((), ()))
    pos_key = lax.dot_general(wk_ref[...], table, turned, preferred_element_type=F32).astype(BF16)
    pos_query = lax.dot_general(wq_ref[...], table, turned, preferred_element_type=F32).astype(BF16)
    plain = one_hot_columns(rel_ref, 0, buckets)
    pk_ref[...] = mm(pos_key, plain).astype(BF16)
    pq_ref[...] = mm(pos_query, plain).astype(BF16)
    back = one_hot_columns(rel_ref, 1, buckets)
    pk_back_ref[...] = mm(pos_key, back).astype(BF16)
    pq_back_ref[...] = mm(pos_query, back).astype(BF16)


def position_tables(w_query, w_key, table, rel_rows):
    local = w_query.shape[1]
    return kernel_call(
        tables_kernel,
        "position_tables",
        1_200_000_000,
        4_000_000,
        8,
        in_specs=[IN_VMEM] * 4,
        out_specs=[IN_VMEM] * 4,
        out_shape=[Shape((local, OFFSETS), BF16)] * 4,
    )(w_query, w_key, table, rel_rows)


def forward_kernel(
    block, place_ref, counts_ref, hidden_ref, wq_ref, wk_ref, wv_ref, pk_ref, pq_ref, mask_ref,
    *rest,
):
    q_ref, k_ref, v_ref, weights_ref = rest[-11:-7]
    context_refs = rest[-7:-3]
    context_ref, bias_ref, rel_score_ref = rest[-3:]
    heads = wq_ref.shape[1] // HEAD_DIM
    first = block * SEQMAX
    column = starts_of(lax.broadcasted_iota(jnp.int32, (SEQMAX, 1), 0) + first, counts_ref)
    row = starts_of(lax.broadcasted_iota(jnp.int32, (1, SEQMAX), 1) + first, counts_ref)
    row = jnp.where(mask_ref[block] == 1, row, -1)
    bias_ref[...] = jnp.where(column == row, 0.0, NEGATIVE)
    hidden = hidden_ref[first : first + SEQMAX, :]
    q_ref[...] = mm(hidden, wq_ref[...]).astype(BF16)
    k_ref[...] = mm(hidden, wk_ref[...]).astype(BF16)
    v_ref[...] = mm(hidden, wv_ref[...]).astype(BF16)
    for head in range(heads):
        part = slice(head * HEAD_DIM, (head + 1) * HEAD_DIM)
        queries = q_ref[:, part]
        keys = k_ref[:, part]
        values = v_ref[:, part]
        for at in range(0, SEQMAX, TILE):
            rel = mm(keys[at : at + TILE], pq_ref[part, window_of(at)])
            rel_score_ref[at : at + TILE, :] = skew(rel)
        for at in range(0, SEQMAX, TILE):
            rows = slice(at, at + TILE)
            raw = mm_nt(queries[rows], keys)
            raw = raw + skew(mm(queries[rows], pk_ref[part, window_of(at)]))
            raw = raw + rel_score_ref[:, rows].T
            scaled = raw * score_factor() + bias_ref[rows, :]
            top = jnp.max(scaled, axis=-1, keepdims=True)
            exponent = jnp.exp(scaled - top)
            total = jnp.sum(exponent, axis=-1, keepdims=True)
            weights = (exponent * (1.0 / total)).astype(BF16)
            weights_ref[head, rows, :] = weights
            relative = jnp.bitwise_xor(at // TILE, place_ref[0])
            context_ref[relative, :, part] = mm(weights, values).astype(BF16)
    for relative, ref in enumerate(context_refs):
        for b in range(block):
            ref[b] = rest[relative][b]
        ref[block] = context_ref[relative]


def forward_attention(block, place, counts, hidden, weights, tables, key_mask, context):
    tokens, width = hidden.shape
    local = weights[0].shape[1]
    heads = local // HEAD_DIM
    blocks = tokens // SEQMAX
    groups = SEQMAX // TILE
    rows = Shape((SEQMAX, local), BF16)
    return kernel_call(
        functools.partial(forward_kernel, block),
        f"attention_forward_{block}",
        10_000_000_000,
        5_000_000,
        12,
        in_specs=[SCALARS, SCALARS] + [IN_VMEM] * (7 + len(context)),
        out_specs=[IN_VMEM] * (4 + groups),
        out_shape=[rows] * 3
        + [Shape((heads, SEQMAX, SEQMAX), BF16)]
        + [Shape((block + 1, TILE, local), BF16)] * groups,
        scratch_shapes=[pltpu.VMEM((groups, TILE, local), BF16)]
        + [pltpu.VMEM((SEQMAX, SEQMAX), F32)] * 2,
    )(place, counts, hidden, *weights, *tables, key_mask.reshape(blocks, 1, SEQMAX), *context)


def backward_kernel(block, blocks, place_ref, *refs):
    groups = SEQMAX // TILE
    cg_refs, refs = refs[:groups], refs[groups:]
    q_ref, k_ref, v_ref, weights_ref, pk_back_ref, pq_back_ref, hidden_ref = refs[:7]
    wq_ref, wk_ref, wv_ref, table_ref, rel_ref, norms_ref = refs[7:13]
    refs = refs[13:]
    before, refs = (refs[:3], refs[3:]) if block > 0 else (None, refs)
    local = wq_ref.shape[1]
    heads = local // HEAD_DIM
    buckets = table_ref.shape[0]
    if block < blocks - 1:
        part_refs, refs = refs[:groups], refs[groups:]
        rg_key_ref, rg_query_ref, sum_ref, cg_ref, ds_ref, rows_ref, part_ref = refs
    else:
        part_refs, joined_refs, refs = refs[:groups], refs[groups : groups + 2], refs[groups + 2 :]
        cg_ref, ds_ref, rows_ref, part_ref, rg_key_ref, rg_query_ref, sum_ref, joined_ref = refs
    if before is None:
        rg_key_ref[...] = jnp.zeros_like(rg_key_ref)
        rg_query_ref[...] = jnp.zeros_like(rg_query_ref)
    else:
        rg_key_ref[...] = before[0][...]
        rg_query_ref[...] = before[1][...]
    me = place_ref[0]
    for relative in range(groups):
        cg_ref[jnp.bitwise_xor(me, relative)] = cg_refs[relative][block]

    tile_rows, tile_lanes = tile_iotas()
    flip = (tile_rows + tile_lanes == TILE - 1).astype(BF16)

    def flipped(low):
        return jnp.concatenate([mm(part, flip) for part in lane_tiles(low)], axis=1)

    for head in range(heads):
        part = slice(head * HEAD_DIM, (head + 1) * HEAD_DIM)
        at_k = slice(local + head * HEAD_DIM, local + (head + 1) * HEAD_DIM)
        at_v = slice(2 * local + head * HEAD_DIM, 2 * local + (head + 1) * HEAD_DIM)
        queries = q_ref[:, part]
        keys = k_ref[:, part]
        values = v_ref[:, part]
        value_grad = jnp.zeros((SEQMAX, HEAD_DIM), F32)
        for at in range(0, SEQMAX, TILE):
            rows = slice(at, at + TILE)
            cotangent = cg_ref[at // TILE, :, part]
            low_weights = weights_ref[head, rows, :]
            weights = low_weights.astype(F32)
            weight_grad = mm_nt(cotangent, values)
            inner = jnp.sum(weights * weight_grad, axis=-1, keepdims=True)
            score_grad = (weights * (weight_grad - inner) * score_factor()).astype(BF16)
            ds_ref[rows, :] = score_grad
            value_grad = value_grad + mm_tn(low_weights, cotangent)
            by_offset = unskew(flipped(score_grad)).astype(BF16)
            window = window_of(at)
            query_grad = mm(score_grad, keys) + mm_nt(by_offset, pk_back_ref[part, window])
            rows_ref[rows, part] = query_grad.astype(BF16)
            rg_key_ref[part, window] += mm_tn(queries[rows], by_offset)
        rows_ref[:, at_v] = value_grad.astype(BF16)
        for at in range(0, SEQMAX, TILE):
            rows = slice(at, at + TILE)
            turned = ds_ref[:, rows].T
            by_offset = unskew(flipped(turned)).astype(BF16)
            window = window_of(at)
            key_grad = mm(turned, queries) + mm_nt(by_offset, pq_back_ref[part, window])
            rows_ref[rows, at_k] = key_grad.astype(BF16)
            rg_query_ref[part, window] += mm_tn(keys[rows], by_offset)
    total = mm_nt(rows_ref[:, :local], wq_ref[...])
    total = total + mm_nt(rows_ref[:, local : 2 * local], wk_ref[...])
    total = total + mm_nt(rows_ref[:, 2 * local :], wv_ref[...])
    for at in range(0, SEQMAX, TILE):
        part_ref[jnp.bitwise_xor(at // TILE, me)] = total[at : at + TILE].astype(BF16)
    for relative, ref in enumerate(part_refs):
        ref[...] = part_ref[relative]
    first = block * SEQMAX
    sums = mm_tn(hidden_ref[first : first + SEQMAX, :], rows_ref[...])
    sum_ref[...] = sums if before is None else before[2][...] + sums
    if block < blocks - 1:
        return

    back = one_hot_columns(rel_ref, 1, buckets)

    def by_bucket(rg_ref):
        high, low = split_low(rg_ref[...])
        return (mm_nt(high, back) + mm_nt(low, back)).T

    def through_table(grad):
        high, low = split_low(grad)
        return mm_tn(table_ref[...], high) + mm_tn(table_ref[...], low)

    pos_key = by_bucket(rg_key_ref)
    pos_query = by_bucket(rg_query_ref)
    sum_ref[:, :local] += through_table(pos_query)
    sum_ref[:, local : 2 * local] += through_table(pos_key)
    pos = jnp.concatenate([pos_key, pos_query], axis=1).astype(BF16)
    slots, row_rows, _ = joined_ref.shape
    pos_rows = buckets // slots
    for chunk in range(slots):
        slot = slot_of(jnp.bitwise_xor(chunk, place_ref[1]), (CORE, ACROSS_X, ACROSS_Y))
        joined_ref[slot, :pos_rows, : 2 * local] = pos[chunk * pos_rows : (chunk + 1) * pos_rows]
        extra = jnp.concatenate(
            [
                norms_ref[chunk : chunk + 1, :],
                jnp.zeros((row_rows - pos_rows - 1, 2 * local), F32),
            ],
            axis=0,
        )
        joined_ref[slot, pos_rows:, : 2 * local] = extra.astype(BF16)
        joined_ref[slot, :, 2 * local :] = sum_ref[
            chunk * row_rows : (chunk + 1) * row_rows, :
        ].astype(BF16)
    joined_refs[0][...] = joined_ref[: slots // 2]
    joined_refs[1][...] = joined_ref[slots // 2 :]


def slot_of(relative, order):
    slot = 0
    for position, bit in enumerate(order):
        slot = slot + jnp.minimum(jnp.bitwise_and(relative, bit), 1) * (4 >> position)
    return slot


def backward_attention(
    block, blocks, place, context_grads, rows, weights, tables, hidden, w_rows, table, rel_rows,
    norms, before,
):
    width = hidden.shape[1]
    local = w_rows[0].shape[1]
    heads = local // HEAD_DIM
    buckets = table.shape[0]
    groups = SEQMAX // TILE
    last = block == blocks - 1
    parts = [Shape((TILE, width), BF16)] * groups
    sums = [(local, OFFSETS), (local, OFFSETS), (width, 3 * local)]
    joined = Shape((CHUNKS // 2, width // CHUNKS, 5 * local), BF16)
    scratch = [
        pltpu.VMEM((groups, TILE, local), BF16),
        pltpu.VMEM((SEQMAX, SEQMAX), BF16),
        pltpu.VMEM((SEQMAX, 3 * local), BF16),
        pltpu.VMEM((groups, TILE, width), BF16),
    ]
    if last:
        out_shape = parts + [joined] * 2
        scratch = scratch + [pltpu.VMEM(shape, F32) for shape in sums]
        scratch = scratch + [pltpu.VMEM((CHUNKS,) + joined.shape[1:], BF16)]
    else:
        out_shape = parts + [Shape(shape, F32) for shape in sums]
    return kernel_call(
        functools.partial(backward_kernel, block, blocks),
        f"attention_backward_{block}",
        20_000_000_000,
        8_000_000,
        16,
        in_specs=[SCALARS] + [IN_VMEM] * (groups + 13 + len(before)),
        out_specs=[IN_VMEM] * len(out_shape),
        out_shape=out_shape,
        scratch_shapes=scratch,
    )(place, *context_grads, *rows, weights, *tables, hidden, *w_rows, table, rel_rows, norms, *before)


def offset_rows(rel_buckets):
    plain = jnp.concatenate([rel_buckets[::-1], rel_buckets[:1]])
    back = plain.reshape(OFFSETS // TILE, TILE)[:, ::-1].reshape(OFFSETS)
    return jnp.stack([plain, back])


def layer_norm_parts(resid):
    centered = resid - jnp.mean(resid, axis=-1, keepdims=True)
    scale = lax.rsqrt(jnp.mean(centered * centered, axis=-1, keepdims=True) + NORM_EPS)
    return centered * scale, scale


def layer_norm_back(normal, scale, grad, gain):
    inner = grad * gain
    mean = jnp.mean(inner, axis=-1, keepdims=True)
    along = jnp.mean(inner * normal, axis=-1, keepdims=True)
    return scale * (inner - mean - normal * along)


def token_kernel(place_ref, *refs):
    groups = SEQMAX // TILE
    context_refs, refs = refs[:groups], refs[groups:]
    hidden_ref, out_grad_ref, norms_ref, w_in_ref, w_down_ref, w_out_ref = refs[:6]
    piece_refs, refs = refs[6 : -11 - groups], refs[-11 - groups :]
    (
        output_ref, resid_ref, first_low_ref, act_ref, pre_grad_ref, ffn_grad_ref, attn_grad_ref,
        norm_grads_ref, *context_grad_refs, packed_vmem, slope_ref, sem,
    ) = refs
    width = hidden_ref.shape[1]
    units = act_ref.shape[2]
    local = context_refs[0].shape[1]
    unit_rows, width_rows = units // CHUNKS, width // CHUNKS

    copies = gather_copies(piece_refs, packed_vmem, place_ref[1], sem)
    for copy in copies:
        copy.start()
    for copy in copies:
        copy.wait()

    def packed(shift, first, rows):
        return packed_vmem[shift - 1, :, first : first + rows, :].reshape(CHUNKS * rows, width)

    def w_in(shift):
        return w_in_ref[...] if shift == 0 else packed(shift, 0, width_rows)

    def w_down(shift):
        return w_down_ref[...] if shift == 0 else packed(shift, width_rows, unit_rows)

    def w_out(shift):
        if shift == 0:
            return w_out_ref[...]
        return packed(shift, width_rows + unit_rows, OUT_ROWS)[:local]

    gain_one, bias_one = norms_ref[0:1, :], norms_ref[1:2, :]
    gain_two, bias_two = norms_ref[2:3, :], norms_ref[3:4, :]
    resid = hidden_ref[...].astype(F32)
    for g in range(groups):
        resid = resid + mm(context_refs[g][...], w_out(g)).astype(BF16).astype(F32)
    normal_one, scale_one = layer_norm_parts(resid)
    first_norm = normal_one * gain_one + bias_one
    first_low = first_norm.astype(BF16)
    first_low_ref[...] = first_low
    ffn_out = first_norm
    for g in range(groups):
        pre_act = mm(first_low, w_in(g))
        area = 0.5 * (1.0 + lax.erf(pre_act * math.sqrt(0.5)))
        activated = (pre_act * area).astype(BF16)
        act_ref[g] = activated
        density = jnp.exp(-0.5 * pre_act * pre_act) * (1.0 / math.sqrt(2.0 * math.pi))
        slope_ref[g] = area + pre_act * density
        ffn_out = ffn_out + mm(activated, w_down(g)).astype(BF16).astype(F32)
    normal_two, scale_two = layer_norm_parts(ffn_out)
    output_ref[...] = (normal_two * gain_two + bias_two).astype(BF16)
    out_grad = out_grad_ref[...].astype(F32)
    norm_grads_ref[...] = jnp.zeros_like(norm_grads_ref)
    norm_grads_ref[2:3, :] = jnp.sum(out_grad * normal_two, axis=0, keepdims=True)
    norm_grads_ref[3:4, :] = jnp.sum(out_grad, axis=0, keepdims=True)
    second_grad = layer_norm_back(normal_two, scale_two, out_grad, gain_two)
    ffn_grad = second_grad.astype(BF16)
    ffn_grad_ref[...] = ffn_grad
    first_grad = second_grad
    for g in range(groups):
        pre_grad = (mm_nt(ffn_grad, w_down(g)) * slope_ref[g]).astype(BF16)
        pre_grad_ref[g] = pre_grad
        first_grad = first_grad + mm_nt(pre_grad, w_in(g))
    norm_grads_ref[0:1, :] = jnp.sum(first_grad * normal_one, axis=0, keepdims=True)
    norm_grads_ref[1:2, :] = jnp.sum(first_grad, axis=0, keepdims=True)
    resid_grad = layer_norm_back(normal_one, scale_one, first_grad, gain_one)
    resid_ref[...] = resid_grad
    attn_grad = resid_grad.astype(BF16)
    attn_grad_ref[...] = attn_grad
    for g in range(groups):
        context_grad_refs[g][...] = mm_nt(attn_grad, w_out(g)).astype(BF16)


def gather_copies(piece_refs, packed_vmem, replica, sem):
    copies = []
    for (group, relatives, first, rows), ref in zip(GATHERED, piece_refs):
        for i, relative in enumerate(relatives):
            chunk = jnp.bitwise_xor(replica, relative)
            copies.append(
                pltpu.make_async_copy(
                    ref.at[i],
                    packed_vmem.at[group - 1, chunk, pl.ds(first, rows), :],
                    sem.at[len(copies)],
                )
            )
    return copies


def reached(axes):
    order = (0,)
    for bit in axes:
        order = order + tuple(relative + bit for relative in order)
    return order


def gathered_layout():
    layout = []
    for group, axes in ((1, (ACROSS_Y, ACROSS_X)), (2, (ACROSS_X, ACROSS_Y))):
        for core in (0, CORE):
            layout += [(group, (core, core + axes[0]), 0, 2 * HALF_ROWS)]
            layout += [(group, (core + axes[1], core + sum(axes)), 0, 2 * HALF_ROWS)]
    for first, axes in ((0, (ACROSS_Y, ACROSS_X)), (HALF_ROWS, (ACROSS_X, ACROSS_Y))):
        for core in (0, CORE):
            layout += [(3, (core, core + axes[0]), first, HALF_ROWS)]
            layout += [(3, (core + axes[1], core + sum(axes)), first, HALF_ROWS)]
    return layout


HALF_ROWS = 112
GATHERED = gathered_layout()


def across(array, bit):
    return lax.ppermute(array, "dp", [(i, i ^ bit) for i in range(CHUNKS)])


def widen(held, bit):
    return jnp.concatenate([held, across(held, bit)], 0)


def together(*values):
    return lax.optimization_barrier(values)


def token_layer(place, contexts, hidden, out_grad, norms, w_rows, pieces):
    tokens, width = hidden.shape
    local = contexts[0].shape[1]
    units = w_rows[0].shape[1]
    groups = len(contexts)
    rows = width // CHUNKS + units // CHUNKS + OUT_ROWS
    return kernel_call(
        token_kernel,
        "token_layer",
        15_000_000_000,
        18_000_000,
        24,
        in_specs=[SCALARS]
        + [IN_VMEM] * (groups + 6)
        + [ANYWHERE] * len(pieces),
        out_specs=[IN_VMEM] * (8 + groups),
        out_shape=[
            Shape((tokens, width), BF16),
            Shape((tokens, width), F32),
            Shape((tokens, width), BF16),
            Shape((groups, tokens, units), BF16),
            Shape((groups, tokens, units), BF16),
            Shape((tokens, width), BF16),
            Shape((tokens, width), BF16),
            Shape((8, width), F32),
        ]
        + [Shape((tokens, local), BF16)] * groups,
        scratch_shapes=[
            pltpu.VMEM((groups - 1, CHUNKS, rows, width), BF16),
            pltpu.VMEM((groups, tokens, units), F32),
            pltpu.SemaphoreType.DMA((2 * len(GATHERED),)),
        ],
    )(place, *contexts, hidden, out_grad, norms, *w_rows, *pieces)


def weight_grad_kernel(half, order, place_ref, *refs):
    context_refs, refs = refs[:2], refs[2:]
    first_low_ref, act_ref, pre_grad_ref, ffn_grad_ref, attn_grad_ref = refs[:5]
    keep_ref, give_ref, in_ref, down_ref, last_ref = refs[5:]
    local = context_refs[0].shape[1]
    width_rows = in_ref.shape[0] // CHUNKS
    unit_rows = down_ref.shape[0] // CHUNKS
    last_ref[local:, :] = jnp.zeros((last_ref.shape[0] - local, last_ref.shape[1]), BF16)
    places = reached(order[::-1])
    for j in range(2):
        in_ref[...] = mm_tn(first_low_ref[...], pre_grad_ref[2 * half + j]).astype(BF16)
        down_ref[...] = mm_tn(act_ref[2 * half + j], ffn_grad_ref[...]).astype(BF16)
        last_ref[:local, :] = mm_tn(context_refs[j][...], attn_grad_ref[...]).astype(BF16)
        for core, out_ref in ((0, keep_ref), (CORE, give_ref)):
            for slot, relative in enumerate(places):
                chunk = jnp.bitwise_xor(relative + core, place_ref[1])
                at = pl.multiple_of(chunk * width_rows, 16)
                out_ref[slot, j, :width_rows] = in_ref[pl.ds(at, width_rows), :]
                at = pl.multiple_of(chunk * unit_rows, 16)
                out_ref[slot, j, width_rows : width_rows + unit_rows] = down_ref[
                    pl.ds(at, unit_rows), :
                ]
                at = pl.multiple_of(chunk * OUT_ROWS, 16)
                out_ref[slot, j, width_rows + unit_rows :] = last_ref[pl.ds(at, OUT_ROWS), :]


def weight_grads(half, order, place, contexts, first_low, act, pre_grad, ffn_grad, attn_grad):
    groups, tokens, units = act.shape
    width = first_low.shape[1]
    rows = width // CHUNKS + units // CHUNKS + OUT_ROWS
    return kernel_call(
        functools.partial(weight_grad_kernel, half, order),
        f"weight_grads_{half}",
        4_000_000_000,
        7_000_000,
        12,
        in_specs=[SCALARS] + [IN_VMEM] * 7,
        out_specs=[IN_VMEM] * 2,
        out_shape=[Shape((CHUNKS // 2, 2, rows, width), BF16)] * 2,
        scratch_shapes=[
            pltpu.VMEM((width, width), BF16),
            pltpu.VMEM((units, width), BF16),
            pltpu.VMEM((CHUNKS * OUT_ROWS, width), BF16),
        ],
    )(place, *contexts[2 * half : 2 * half + 2], first_low, act, pre_grad, ffn_grad, attn_grad)


def add(left, right):
    return (left.astype(F32) + right.astype(F32)).astype(BF16)


def give_half(array):
    return array[array.shape[0] // 2 :]


def total_of(arrays):
    return sum(array.astype(F32) for array in arrays).astype(BF16)


def reorder_kernel(place_ref, *refs):
    out_ref = refs[-1]
    groups = out_ref.shape[1]
    blocks = out_ref.shape[0]
    per = len(refs[:-1]) // groups
    for shift in range(groups):
        origin = jnp.bitwise_xor(place_ref[0], shift)
        for b in range(blocks):
            if per == 1:
                out_ref[b, origin] = refs[shift][b * TILE : (b + 1) * TILE, :]
            else:
                out_ref[b, origin] = refs[b * groups + shift][...]


def reorder(place, pieces, blocks):
    width = pieces[0].shape[1]
    groups = SEQMAX // TILE
    out = kernel_call(
        reorder_kernel,
        "reorder",
        0,
        3_000_000,
        8,
        in_specs=[SCALARS] + [IN_VMEM] * len(pieces),
        out_specs=IN_VMEM,
        out_shape=Shape((blocks, groups, TILE, width), BF16),
    )(place, *pieces)
    return out.reshape(blocks * SEQMAX, width)


def unpack_kernel(piece_ref, grad_in_ref, grad_down_ref, grad_out_ref):
    width_rows = grad_in_ref.shape[0] // CHUNKS
    unit_rows = grad_down_ref.shape[0] // CHUNKS
    rows = width_rows + unit_rows
    for chunk in range(CHUNKS):
        piece = piece_ref.at[chunk]
        at = chunk * width_rows
        grad_in_ref[at : at + width_rows, :] = piece[:width_rows, :].astype(F32)
        at = chunk * unit_rows
        grad_down_ref[at : at + unit_rows, :] = piece[width_rows:rows, :].astype(F32)
        at = chunk * OUT_ROWS
        if at < grad_out_ref.shape[0]:
            grad_out_ref[at : at + OUT_ROWS, :] = piece[rows:, :].astype(F32)


def unpack(pieces, width, units, local):
    return kernel_call(
        unpack_kernel,
        "unpack",
        0,
        9_000_000,
        8,
        in_specs=[IN_VMEM],
        out_specs=[IN_VMEM] * 3,
        out_shape=[
            Shape((width, width), F32),
            Shape((units, width), F32),
            Shape((local, width), F32),
        ],
    )(pieces)


def small_kernel(order, place_ref, *refs):
    piece_refs, (q_ref, k_ref, v_ref, table_ref, norm_ref) = refs[:-5], refs[-5:]
    half = len(piece_refs) // 2
    width, local = q_ref.shape
    row_rows, pos_rows = width // CHUNKS, table_ref.shape[0] // CHUNKS
    slot = 0
    for row_ref, small_ref in zip(piece_refs[:half], piece_refs[half:]):
        for i in range(row_ref.shape[0]):
            chunk = jnp.bitwise_xor(place_ref[1], order[slot])
            slot += 1
            at = pl.multiple_of(chunk * row_rows, 8)
            for j, out_ref in enumerate((q_ref, k_ref, v_ref)):
                part = row_ref[i, :, j * local : (j + 1) * local]
                out_ref[pl.ds(at, row_rows), :] = part.astype(F32)
            at = pl.multiple_of(chunk * pos_rows, 8)
            table_ref[pl.ds(at, pos_rows), :] = small_ref[i, :pos_rows, :].astype(F32)
            extra = small_ref[i, pos_rows:, : norm_ref.shape[1]].astype(F32)
            norm_ref[pl.ds(chunk, 1), :] = extra[:1]


def small_unpack(order, place, rows, small, width, local, buckets):
    return kernel_call(
        functools.partial(small_kernel, order),
        "small_unpack",
        0,
        6_000_000,
        8,
        in_specs=[SCALARS] + [IN_VMEM] * (len(rows) + len(small)),
        out_specs=[IN_VMEM] * 5,
        out_shape=[Shape((width, local), F32)] * 3
        + [Shape((buckets, width), F32), Shape((CHUNKS, 4 * width // CHUNKS), F32)],
    )(place, *rows, *small)


def send(array, bits):
    return lax.ppermute(array, "tensor", [(i, i ^ bits) for i in range(SEQMAX // TILE)])


def exchange(pieces):
    return [pieces[0]] + [send(piece, r) for r, piece in enumerate(pieces) if r > 0]


def spread(array):
    near, far = send(array, 1), send(array, 2)
    return [array, near, far, send(far, 1)]


def shards(
    n_dp,
    n_tensor,
    hidden,
    out_grad,
    w_query,
    w_key,
    w_value,
    w_out,
    w_in,
    w_down,
    bucket_table,
    gain_one,
    bias_one,
    gain_two,
    bias_two,
    rel_buckets,
    group_counts,
    key_mask,
):
    tokens, width = hidden.shape
    local = w_query.shape[1]
    units = w_in.shape[1]
    buckets = bucket_table.shape[0]
    blocks = tokens // SEQMAX
    mine = tokens // n_tensor
    by_axis = n_dp == CHUNKS
    me = lax.axis_index("tensor")
    replica = lax.axis_index("dp") if by_axis else jnp.int32(0)
    place = jnp.stack([me, replica]).astype(jnp.int32)
    rel_rows = offset_rows(rel_buckets)
    width_rows, unit_rows = width // CHUNKS, units // CHUNKS
    padded = jnp.pad(w_out, ((0, CHUNKS * OUT_ROWS - local), (0, 0)))

    w_rows = (w_query, w_key, w_value)

    def my_rows(array):
        array = array.reshape(blocks, n_tensor, TILE, width)
        return lax.dynamic_index_in_dim(array, me, 1, keepdims=False).reshape(mine, width)

    def forward(block, start, context):
        *rows, weights, c0, c1, c2, c3 = forward_attention(
            block, start, group_counts, hidden, w_rows, tables[:2], key_mask, context
        )
        return (rows, weights), [c0, c1, c2, c3]

    if by_axis:
        pick = lambda array, rows: lax.dynamic_slice_in_dim(array, replica * rows, rows, 0)
        piece = jnp.concatenate(
            [pick(w_in, width_rows), pick(w_down, unit_rows), pick(padded, OUT_ROWS)], 0
        )
        near, far = send(piece, 1), send(piece, 2)
        tables = position_tables(w_query, w_key, bucket_table, rel_rows)
        kept_0, context = forward(0, place, [])
        near, far, tables, kept_0, context, place = together(
            near, far, tables, kept_0, context, place
        )
        last = send(far, 1)
        near_y, far_x = across(near[None], ACROSS_Y), across(far[None], ACROSS_X)
        kept_1, context = forward(1, place, context)
        near, far, near_y, far_x, last, kept_0, kept_1, context, place = together(
            near, far, near_y, far_x, last, kept_0, kept_1, context, place
        )
        contexts = exchange([piece.reshape(mine, local) for piece in context])
        near = jnp.concatenate([near[None], near_y], 0)
        far = jnp.concatenate([far[None], far_x], 0)
        near_x, far_y = across(near, ACROSS_X), across(far, ACROSS_Y)
        top, low = last[None, :HALF_ROWS], last[None, HALF_ROWS:]
        top_y, low_x = across(top, ACROSS_Y), across(low, ACROSS_X)
        rows, out_rows = my_rows(hidden), my_rows(out_grad)
        (
            near, near_x, far, far_y, top, top_y, low, low_x, contexts, rows, out_rows, kept_0,
            kept_1,
        ) = together(
            near, near_x, far, far_y, top, top_y, low, low_x, contexts, rows, out_rows, kept_0,
            kept_1,
        )
        top = jnp.concatenate([top, top_y], 0)
        low = jnp.concatenate([low, low_x], 0)
        top_x, low_y = across(top, ACROSS_X), across(low, ACROSS_Y)
        gathered = []
        for pair in ((near, near_x), (far, far_y)):
            gathered += [*pair] + [across(array, CORE) for array in pair]
        gathered, top, top_x, low, low_y, contexts, rows, out_rows, kept_0, kept_1 = together(
            gathered, top, top_x, low, low_y, contexts, rows, out_rows, kept_0, kept_1
        )
        for pair in ((top, top_x), (low, low_y)):
            gathered += [*pair] + [across(array, CORE) for array in pair]
    else:
        tables = position_tables(w_query, w_key, bucket_table, rel_rows)
        stacked = jnp.concatenate(
            [
                w_in.reshape(CHUNKS, width_rows, width),
                w_down.reshape(CHUNKS, unit_rows, width),
                padded.reshape(CHUNKS, OUT_ROWS, width),
            ],
            1,
        )
        sent = spread(stacked)
        gathered = [
            jnp.stack([sent[group][chunk, first : first + rows] for chunk in chunks])
            for group, chunks, first, rows in GATHERED
        ]
        kept_0, context = forward(0, place, [])
        kept_1, context = forward(1, place, context)
        contexts = exchange([piece.reshape(mine, local) for piece in context])
        rows, out_rows = my_rows(hidden), my_rows(out_grad)
    norms = jnp.stack([gain_one, bias_one, gain_two, bias_two])
    (
        output, resid_grad, first_low, act, pre_grad, ffn_grad, attn_grad, norm_grads, *back,
    ) = token_layer(place, contexts, rows, out_rows, norms, (w_in, w_down, w_out), gathered)
    norm_grads = norm_grads[:4].reshape(CHUNKS, 4 * width // CHUNKS)

    def backward(block, kept, before):
        p0, p1, p2, p3, *before = backward_attention(
            block, blocks, place, back, *kept, tables[2:], hidden, w_rows, bucket_table, rel_rows,
            norm_grads, before,
        )
        return [p0, p1, p2, p3], before

    half_axes = ((ACROSS_Y, ACROSS_X), (ACROSS_X, ACROSS_Y))
    back = exchange(back)
    halves = [
        weight_grads(half, axes, place, contexts, first_low, act, pre_grad, ffn_grad, attn_grad)
        for half, axes in enumerate(half_axes)
    ]
    back, halves, output, resid_grad, norm_grads, kept_0, kept_1, tables, place = together(
        back, halves, output, resid_grad, norm_grads, kept_0, kept_1, tables, place
    )
    back = [piece.reshape(blocks, TILE, local) for piece in back]
    out_near, out_far = send(output, 1), send(output, 2)
    if by_axis:
        arrived = [across(give, CORE) for keep, give in halves]
    else:
        arrived = []
    parts, before = backward(0, kept_0, ())
    (
        parts, before, arrived, out_near, out_far, halves, output, resid_grad, norm_grads, kept_1,
        tables, place, back,
    ) = together(
        parts, before, arrived, out_near, out_far, halves, output, resid_grad, norm_grads, kept_1,
        tables, place, back,
    )
    parts = [parts[0], send(parts[1], 1), parts[2], send(parts[3], 1)]
    out_last = send(out_far, 1)
    folded = []
    if by_axis:
        for (keep, give), got, axes in zip(halves, arrived, half_axes):
            folded.append(across(add(give_half(keep), give_half(got)), axes[0]))
    parts_1, before = backward(1, kept_1, before)
    parts, parts_1, before, folded, out_last, halves, arrived, resid_grad = together(
        parts, parts_1, before, folded, out_last, halves, arrived, resid_grad
    )
    keep, give = before
    if by_axis:
        thirds = []
        for (held, _), got, first, axes in zip(halves, arrived, folded, half_axes):
            given = total_of([held[1:2], got[1:2], first[1:2]])
            kept = [held[:1], got[:1], first[:1]]
            thirds.append((kept, across(given, axes[1])))
        arrived = across(give, CORE)
    else:
        thirds = []
        joined = lax.psum(jnp.concatenate([keep, give], 0).astype(F32), "dp").astype(BF16)
        arrived = keep
    far_0 = send(add(parts[2], parts[3]), 2)
    near_1 = [send(parts_1[1], 1), send(parts_1[3], 1)]
    (
        parts, parts_1, far_0, near_1, thirds, arrived, keep, give, resid_grad, out_last,
    ) = together(
        parts, parts_1, far_0, near_1, thirds, arrived, keep, give, resid_grad, out_last,
    )
    if by_axis:
        shard = [total_of([*kept, got])[0] for kept, got in thirds]
        shard = jnp.concatenate(shard, 0)
        shard = jnp.stack(
            [lax.dynamic_index_in_dim(shard, me ^ g, 0, False) for g in range(n_tensor)]
        )
        shard = lax.psum_scatter(shard, "tensor", scatter_dimension=0, tiled=True)
    else:
        natural = []
        for (held, given), axes in zip(halves, half_axes):
            chunks = reached(axes[::-1] + (CORE,))
            both = jnp.concatenate([held, given], 0)
            natural += [
                jnp.stack([both[chunks.index(chunk), j] for chunk in range(CHUNKS)])
                for j in range(2)
            ]
        shard = jnp.stack(exchange(natural)).astype(F32)
        shard = lax.psum(sum(shard[r] for r in range(n_tensor)), "dp").astype(BF16)
    def total(block, pieces):
        wide = resid_grad[block * TILE : (block + 1) * TILE]
        for piece in pieces:
            wide = wide + piece.astype(F32)
        return wide.astype(BF16)

    grad_0 = total(0, [parts[0], parts[1], far_0])
    near_0, far_0 = send(grad_0, 1), send(grad_0, 2)
    far_1 = send(add(parts_1[2], near_1[1]), 2)
    if by_axis:
        keep, give = add(keep[:2], arrived[:2]), add(keep[2:], arrived[2:])
        arrived = across(give, ACROSS_X)
    grad_0, near_0, far_0, far_1, near_1, parts_1, arrived, keep, resid_grad = together(
        grad_0, near_0, far_0, far_1, near_1, parts_1, arrived, keep, resid_grad
    )
    last_0 = send(far_0, 1)
    grad_1 = total(1, [parts_1[0], near_1[0], far_1])
    near_1, far_1 = send(grad_1, 1), send(grad_1, 2)
    if by_axis:
        keep, give = add(keep[:1], arrived[:1]), add(keep[1:], arrived[1:])
        arrived = across(give, ACROSS_Y)
    grad_0, near_0, far_0, last_0, grad_1, near_1, far_1, arrived, keep, shard = together(
        grad_0, near_0, far_0, last_0, grad_1, near_1, far_1, arrived, keep, shard
    )
    if by_axis:
        shard = lax.all_gather(shard[0], "dp", axis=0, tiled=False)
    last_1 = send(far_1, 1)
    if by_axis:
        joined = add(keep, arrived)
    pos_rows = buckets // CHUNKS
    slots = joined.shape[0]
    w_table = jnp.concatenate([w_key, w_query], 1)
    table_part = mm_nt(joined[:, :pos_rows, : 2 * local].reshape(slots * pos_rows, -1), w_table)
    table_part = table_part.astype(BF16).reshape(slots, pos_rows, width)
    norm_part = jnp.pad(
        joined[:, pos_rows : pos_rows + 16, : 2 * local],
        ((0, 0), (0, 0), (0, width - 2 * local)),
    )
    small = jnp.concatenate([table_part, norm_part], 1)
    row_grads = joined[:, :, 2 * local :]
    small_near = send(small, 1)
    rows_y = across(row_grads, ACROSS_Y) if by_axis else row_grads
    (
        grad_0, near_0, far_0, last_0, grad_1, near_1, far_1, last_1, small, small_near, row_grads,
        rows_y,
    ) = together(
        grad_0, near_0, far_0, last_0, grad_1, near_1, far_1, last_1, small, small_near, row_grads,
        rows_y,
    )
    small = add(small, small_near)
    small_far = send(small, 2)
    if by_axis:
        row_grads = jnp.concatenate([row_grads, rows_y], 0)
        rows_x = across(row_grads, ACROSS_X)
        small, small_far, row_grads, rows_x = together(small, small_far, row_grads, rows_x)
        small = add(small, small_far)
        row_grads = jnp.concatenate([row_grads, rows_x], 0)
        rows_core = across(row_grads, CORE)
        small_y = across(small, ACROSS_Y)
        small, small_y, row_grads, rows_core = together(small, small_y, row_grads, rows_core)
        small = jnp.concatenate([small, small_y], 0)
        small = widen(small, ACROSS_X)
        row_grads, small = [row_grads, rows_core], [small, across(small, CORE)]
    else:
        row_grads, small = [row_grads], [add(small, small_far)]
    order = reached((ACROSS_Y, ACROSS_X, CORE))
    grad_query, grad_key, grad_value, grad_table, norm_grads = small_unpack(
        order, place, row_grads, small, width, local, buckets
    )
    norm_grads = norm_grads.reshape(4, width)
    grad_in, grad_down, grad_out = unpack(shard, width, units, local)
    return (
        reorder(place, [output, out_near, out_far, out_last], blocks),
        reorder(place, [grad_0, near_0, far_0, last_0, grad_1, near_1, far_1, last_1], blocks),
        grad_query,
        grad_key,
        grad_value,
        grad_out,
        grad_in,
        grad_down,
        grad_table,
        norm_grads[0],
        norm_grads[1],
        norm_grads[2],
        norm_grads[3],
    )


def solution(mesh):
    in_specs = (
        P("dp", None),
        P("dp", None),
        P(None, "tensor"),
        P(None, "tensor"),
        P(None, "tensor"),
        P("tensor", None),
        P(None, "tensor"),
        P("tensor", None),
        P(),
        P(),
        P(),
        P(),
        P(),
        P(),
        P("dp", None),
        P("dp"),
    )
    out_specs = (
        P("dp", None),
        P("dp", None),
        P(None, "tensor"),
        P(None, "tensor"),
        P(None, "tensor"),
        P("tensor", None),
        P(None, "tensor"),
        P("tensor", None),
        P(),
        P(),
        P(),
        P(),
        P(),
    )
    body = functools.partial(shards, mesh.shape["dp"], mesh.shape["tensor"])
    return jax.shard_map(body, mesh=mesh, in_specs=in_specs, out_specs=out_specs, check_vma=False)
```

```python
import functools
import math

import jax
import jax.numpy as jnp
from jax import lax
from jax.experimental import pallas as pl
from jax.experimental.pallas import tpu as pltpu
from jax.sharding import PartitionSpec as P

NORM_EPS = 1e-07
HEAD_DIM = 64
SEQMAX = 512
TILE = 128
WINDOW = SEQMAX + TILE
OFFSETS = 2 * SEQMAX
NEGATIVE = -1e30
CHUNKS = 8
CORE, ACROSS_X, ACROSS_Y = 1, 2, 4
OUT_ROWS = 32
SMALL_ROWS = 8
F32 = jnp.float32
BF16 = jnp.bfloat16


def score_factor():
    return 1.0 / math.sqrt(3.0 * HEAD_DIM)


def mm(left, right):
    return jnp.dot(left, right, preferred_element_type=F32)


def mm_nt(left, right):
    return lax.dot_general(left, right, (((1,), (1,)), ((), ())), preferred_element_type=F32)


def mm_tn(left, right):
    return lax.dot_general(left, right, (((0,), (0,)), ((), ())), preferred_element_type=F32)


def starts_of(places, counts_ref):
    long_end = SEQMAX * counts_ref[0, 0]
    mid_end = long_end + SEQMAX // 2 * counts_ref[0, 1]
    in_long = places < long_end
    in_mid = places < mid_end
    anchor = jnp.where(in_long, 0, jnp.where(in_mid, long_end, mid_end))
    shift = jnp.where(in_long, 9, jnp.where(in_mid, 8, 7))
    return anchor + lax.shift_left(lax.shift_right_logical(places - anchor, shift), shift)


def tile_iotas():
    rows = lax.broadcasted_iota(jnp.int32, (TILE, TILE), 0)
    lanes = lax.broadcasted_iota(jnp.int32, (TILE, TILE), 1)
    return rows, lanes


def lane_tiles(wide):
    return [wide[:, c : c + TILE] for c in range(0, wide.shape[1], TILE)]


def skew(wide):
    rows, lanes = tile_iotas()
    keep = lanes <= rows
    turned = [pltpu.roll(part, 1, 1, stride=1, stride_axis=0) for part in lane_tiles(wide)]
    return jnp.concatenate(
        [jnp.where(keep, turned[c], turned[c + 1]) for c in range(len(turned) - 1)], axis=1
    )


def unskew(flipped):
    rows, lanes = tile_iotas()
    late = lanes > rows
    turned = [pltpu.roll(part, 1, 1, stride=1, stride_axis=0) for part in lane_tiles(flipped)]
    zero = jnp.zeros((TILE, TILE), F32)
    turned = [zero] + turned + [zero]
    return jnp.concatenate(
        [jnp.where(late, turned[c], turned[c + 1]) for c in range(len(turned) - 1)], axis=1
    )


def window_of(tile_at):
    low = SEQMAX - TILE - tile_at
    return slice(low, low + WINDOW)


def one_hot_columns(rel_ref, row, buckets):
    ids = lax.broadcasted_iota(jnp.int32, (buckets, OFFSETS), 0)
    return (ids == rel_ref[row : row + 1, :]).astype(BF16)


def split_low(wide):
    high = wide.astype(BF16)
    return high, (wide - high.astype(F32)).astype(BF16)


SCALARS = pl.BlockSpec(memory_space=pltpu.SMEM)
ANYWHERE = pl.BlockSpec(memory_space=pl.ANY)
IN_HBM = pl.BlockSpec(memory_space=pltpu.HBM)
IN_VMEM = pl.BlockSpec(memory_space=pltpu.VMEM)
Shape = jax.ShapeDtypeStruct


def in_hbm(*arrays):
    return [pltpu.with_memory_space_constraint(array, pltpu.HBM) for array in arrays]


def hbm_shape(shape, kind):
    return pltpu.HBM(shape, kind)


def kernel_call(kernel, name, flops, moved, vmem, **rest):
    return pl.pallas_call(
        kernel,
        compiler_params=pltpu.CompilerParams(vmem_limit_bytes=vmem * 2**20),
        cost_estimate=pl.CostEstimate(flops=flops, bytes_accessed=moved, transcendentals=0),
        name=name,
        **rest,
    )


def start_copies(pairs, sems):
    copies = [
        pltpu.make_async_copy(source, target, sems.at[i]) for i, (source, target) in enumerate(pairs)
    ]
    for copy in copies:
        copy.start()
    return copies


def wait_copies(copies):
    for copy in copies:
        copy.wait()


def prepare_kernel(
    wq_ref, wk_ref, wv_ref, table_ref, rel_ref, hidden_ref, pk_ref, pq_ref, q_ref, k_ref, v_ref,
    pk_back_out, pq_back_out, q_out, k_out, v_out, pk_back, pq_back, sems,
):
    table = table_ref[...]
    buckets = table.shape[0]
    pos_key = mm_nt(wk_ref[...], table).astype(BF16)
    pos_query = mm_nt(wq_ref[...], table).astype(BF16)
    plain = one_hot_columns(rel_ref, 0, buckets)
    pk_ref[...] = mm(pos_key, plain).astype(BF16)
    pq_ref[...] = mm(pos_query, plain).astype(BF16)
    back = one_hot_columns(rel_ref, 1, buckets)
    pk_back[...] = mm(pos_key, back).astype(BF16)
    pq_back[...] = mm(pos_query, back).astype(BF16)
    copies = start_copies([(pk_back, pk_back_out), (pq_back, pq_back_out)], sems)
    hidden = hidden_ref[...]
    for i, (ref, w_ref, out) in enumerate(
        ((q_ref, wq_ref, q_out), (k_ref, wk_ref, k_out), (v_ref, wv_ref, v_out))
    ):
        ref[...] = mm_nt(hidden, w_ref[...]).astype(BF16)
        copies += start_copies([(ref, out)], sems.at[pl.ds(2 + i, 1)])
    wait_copies(copies)


def prepare(w_query, w_key, w_value, table, rel_rows, hidden):
    local = w_query.shape[0]
    tokens = hidden.shape[0]
    table_kind = ((local, OFFSETS), BF16)
    row_kind = ((tokens, local), BF16)
    out = kernel_call(
        prepare_kernel,
        "prepare",
        4_000_000_000,
        6_000_000,
        10,
        in_specs=[IN_VMEM] * 6,
        out_specs=[IN_VMEM] * 5 + [IN_HBM] * 5,
        out_shape=[Shape(*table_kind)] * 2
        + [Shape(*row_kind)] * 3
        + [hbm_shape(*table_kind)] * 2
        + [hbm_shape(*row_kind)] * 3,
        scratch_shapes=[pltpu.VMEM(*table_kind)] * 2 + [pltpu.SemaphoreType.DMA((5,))],
    )(w_query, w_key, w_value, table, rel_rows, hidden)
    return out[:5], out[5:]


def forward_kernel(
    block, place_ref, counts_ref, pk_ref, pq_ref, q_ref, k_ref, v_ref, mask_ref, *rest
):
    before, rest = rest[: 4 if block else 0], rest[4 if block else 0 :]
    weights_out, context_refs, rest = rest[0], rest[1:5], rest[5:]
    context_ref, bias_ref, rel_score_ref, weights_ref, sems_out = rest
    heads = q_ref.shape[1] // HEAD_DIM
    first = block * SEQMAX
    here = slice(first, first + SEQMAX)
    column = starts_of(lax.broadcasted_iota(jnp.int32, (SEQMAX, 1), 0) + first, counts_ref)
    row = starts_of(lax.broadcasted_iota(jnp.int32, (1, SEQMAX), 1) + first, counts_ref)
    row = jnp.where(mask_ref[block] == 1, row, -1)
    bias_ref[...] = jnp.where(column == row, 0.0, NEGATIVE)
    copies = []
    for head in range(heads):
        part = slice(head * HEAD_DIM, (head + 1) * HEAD_DIM)
        queries = q_ref[here, part]
        keys = k_ref[here, part]
        values = v_ref[here, part]
        for at in range(0, SEQMAX, TILE):
            rel = mm(keys[at : at + TILE], pq_ref[part, window_of(at)])
            rel_score_ref[at : at + TILE, :] = skew(rel)
        for at in range(0, SEQMAX, TILE):
            rows = slice(at, at + TILE)
            raw = mm_nt(queries[rows], keys)
            raw = raw + skew(mm(queries[rows], pk_ref[part, window_of(at)]))
            raw = raw + rel_score_ref[:, rows].T
            scaled = raw * score_factor() + bias_ref[rows, :]
            top = jnp.max(scaled, axis=-1, keepdims=True)
            exponent = jnp.exp(scaled - top)
            total = jnp.sum(exponent, axis=-1, keepdims=True)
            weights = (exponent * (1.0 / total)).astype(BF16)
            weights_ref[head, rows, :] = weights
            relative = jnp.bitwise_xor(at // TILE, place_ref[0])
            context_ref[relative, :, part] = mm(weights, values).astype(BF16)
        copies += start_copies(
            [(weights_ref.at[head], weights_out.at[head])], sems_out.at[pl.ds(head, 1)]
        )
    for relative, ref in enumerate(context_refs):
        for b in range(block):
            ref[b] = before[relative][b]
        ref[block] = context_ref[relative]
    wait_copies(copies)


def forward_attention(block, place, counts, tables, rows, key_mask, context):
    tokens, local = rows[0].shape
    heads = local // HEAD_DIM
    blocks = tokens // SEQMAX
    groups = SEQMAX // TILE
    return kernel_call(
        functools.partial(forward_kernel, block),
        f"attention_forward_{block}",
        10_000_000_000,
        5_000_000,
        12,
        in_specs=[SCALARS] * 2 + [IN_VMEM] * (6 + len(context)),
        out_specs=[IN_HBM] + [IN_VMEM] * groups,
        out_shape=[hbm_shape((heads, SEQMAX, SEQMAX), BF16)]
        + [Shape((block + 1, TILE, local), BF16)] * groups,
        scratch_shapes=[pltpu.VMEM((groups, TILE, local), BF16)]
        + [pltpu.VMEM((SEQMAX, SEQMAX), F32)] * 2
        + [pltpu.VMEM((heads, SEQMAX, SEQMAX), BF16), pltpu.SemaphoreType.DMA((heads,))],
    )(place, counts, *tables, *rows, key_mask.reshape(blocks, 1, SEQMAX), *context)


def backward_kernel(block, blocks, place_ref, *refs):
    groups = SEQMAX // TILE
    cg_refs, refs = refs[:groups], refs[groups:]
    q_hbm, k_hbm, v_hbm, weights_hbm, pk_hbm, pq_hbm, hidden_hbm = refs[:7]
    w_hbms, table_hbm, rel_ref, norms_ref = refs[7:10], *refs[10:13]
    refs = refs[13:]
    before, refs = (refs[:3], refs[3:]) if block > 0 else (None, refs)
    q_ref, k_ref, v_ref, weights_ref, pk_back_ref, pq_back_ref, hidden_ref = refs[-12:-5]
    wq_ref, wk_ref, wv_ref, table_ref, sems = refs[-5:]
    refs = refs[:-12]
    local = wq_ref.shape[0]
    heads = local // HEAD_DIM
    buckets = table_ref.shape[0]
    if block < blocks - 1:
        part_refs, refs = refs[:3], refs[3:]
        rg_key_ref, rg_query_ref, sum_ref, cg_ref, ds_ref, rows_ref, part_ref = refs
    else:
        part_refs, joined_refs, refs = refs[:3], refs[3:5], refs[5:]
        cg_ref, ds_ref, rows_ref, part_ref, rg_key_ref, rg_query_ref, sum_ref, joined_ref = refs
    first = block * SEQMAX
    copies = start_copies(
        [
            (q_hbm.at[pl.ds(first, SEQMAX), :], q_ref),
            (k_hbm.at[pl.ds(first, SEQMAX), :], k_ref),
            (v_hbm.at[pl.ds(first, SEQMAX), :], v_ref),
            (weights_hbm, weights_ref),
            (pk_hbm, pk_back_ref),
            (pq_hbm, pq_back_ref),
            (hidden_hbm.at[pl.ds(first, SEQMAX), :], hidden_ref),
            (w_hbms[0], wq_ref),
            (w_hbms[1], wk_ref),
            (w_hbms[2], wv_ref),
        ]
        + ([(table_hbm, table_ref)] if block == blocks - 1 else []),
        sems,
    )
    if before is None:
        rg_key_ref[...] = jnp.zeros_like(rg_key_ref)
        rg_query_ref[...] = jnp.zeros_like(rg_query_ref)
    else:
        rg_key_ref[...] = before[0][...]
        rg_query_ref[...] = before[1][...]
    me = place_ref[0]
    for relative in range(groups):
        cg_ref[jnp.bitwise_xor(me, relative)] = cg_refs[relative][block]
    wait_copies(copies[:6])

    tile_rows, tile_lanes = tile_iotas()
    flip = (tile_rows + tile_lanes == TILE - 1).astype(BF16)

    def flipped(low):
        return jnp.concatenate([mm(part, flip) for part in lane_tiles(low)], axis=1)

    for head in range(heads):
        part = slice(head * HEAD_DIM, (head + 1) * HEAD_DIM)
        at_k = slice(local + head * HEAD_DIM, local + (head + 1) * HEAD_DIM)
        at_v = slice(2 * local + head * HEAD_DIM, 2 * local + (head + 1) * HEAD_DIM)
        queries = q_ref[:, part]
        keys = k_ref[:, part]
        values = v_ref[:, part]
        value_grad = jnp.zeros((SEQMAX, HEAD_DIM), F32)
        for at in range(0, SEQMAX, TILE):
            rows = slice(at, at + TILE)
            cotangent = cg_ref[at // TILE, :, part]
            low_weights = weights_ref[head, rows, :]
            weights = low_weights.astype(F32)
            weight_grad = mm_nt(cotangent, values)
            inner = jnp.sum(weights * weight_grad, axis=-1, keepdims=True)
            score_grad = (weights * (weight_grad - inner) * score_factor()).astype(BF16)
            ds_ref[rows, :] = score_grad
            value_grad = value_grad + mm_tn(low_weights, cotangent)
            by_offset = unskew(flipped(score_grad)).astype(BF16)
            window = window_of(at)
            query_grad = mm(score_grad, keys) + mm_nt(by_offset, pk_back_ref[part, window])
            rows_ref[rows, part] = query_grad.astype(BF16)
            rg_key_ref[part, window] += mm_tn(queries[rows], by_offset)
        rows_ref[:, at_v] = value_grad.astype(BF16)
        for at in range(0, SEQMAX, TILE):
            rows = slice(at, at + TILE)
            turned = ds_ref[:, rows].T
            by_offset = unskew(flipped(turned)).astype(BF16)
            window = window_of(at)
            key_grad = mm(turned, queries) + mm_nt(by_offset, pq_back_ref[part, window])
            rows_ref[rows, at_k] = key_grad.astype(BF16)
            rg_query_ref[part, window] += mm_tn(keys[rows], by_offset)
    wait_copies(copies[6:])
    total = mm(rows_ref[:, :local], wq_ref[...])
    total = total + mm(rows_ref[:, local : 2 * local], wk_ref[...])
    total = total + mm(rows_ref[:, 2 * local :], wv_ref[...])
    for at in range(0, SEQMAX, TILE):
        part_ref[jnp.bitwise_xor(at // TILE, me)] = total[at : at + TILE].astype(BF16)
    part_refs[0][...] = part_ref[0]
    part_refs[1][:TILE, :] = part_ref[1]
    part_refs[1][TILE:, :] = part_ref[3]
    part_refs[2][...] = part_ref[2]
    sums = mm_tn(rows_ref[...], hidden_ref[...])
    sum_ref[...] = sums if before is None else before[2][...] + sums
    if block < blocks - 1:
        return

    back = one_hot_columns(rel_ref, 1, buckets)

    def by_bucket(rg_ref):
        high, low = split_low(rg_ref[...])
        return (mm_nt(high, back) + mm_nt(low, back)).T

    def through_table(grad):
        high, low = split_low(grad)
        return mm_tn(high, table_ref[...]) + mm_tn(low, table_ref[...])

    pos_key = by_bucket(rg_key_ref)
    pos_query = by_bucket(rg_query_ref)
    sum_ref[:local, :] += through_table(pos_query)
    sum_ref[local : 2 * local, :] += through_table(pos_key)
    pos = jnp.concatenate([pos_key, pos_query], axis=1).astype(BF16)
    slots = joined_ref.shape[0]
    row_rows, pos_rows = 3 * local // slots, buckets // slots // 2
    for chunk in range(slots):
        slot = slot_of(jnp.bitwise_xor(chunk, place_ref[1]), (CORE, ACROSS_X, ACROSS_Y))
        at = 2 * chunk * pos_rows
        low = [norms_ref[chunk : chunk + 1, :], jnp.zeros((SMALL_ROWS - 1, 2 * local), F32)]
        low = jnp.concatenate(low, axis=0)
        pieces = [
            sum_ref[chunk * row_rows : (chunk + 1) * row_rows, :].astype(BF16),
            jnp.concatenate([pos[at : at + pos_rows], pos[at + pos_rows : at + 2 * pos_rows]], 1),
            jnp.concatenate([low, jnp.zeros_like(low)], axis=1).astype(BF16),
        ]
        joined_ref[slot] = jnp.concatenate(pieces, axis=0)
    joined_refs[0][...] = joined_ref[: slots // 2]
    joined_refs[1][...] = joined_ref[slots // 2 :]


def slot_of(relative, order):
    slot = 0
    for position, bit in enumerate(order):
        slot = slot + jnp.minimum(jnp.bitwise_and(relative, bit), 1) * (4 >> position)
    return slot


def backward_attention(
    block, blocks, place, context_grads, kept, weights, tables, hidden, w_rows, table, rel_rows,
    norms, before,
):
    width = hidden.shape[1]
    local = w_rows[0].shape[0]
    heads = local // HEAD_DIM
    buckets = table.shape[0]
    groups = SEQMAX // TILE
    last = block == blocks - 1
    parts = [Shape((rows, width), BF16) for rows in (TILE, 2 * TILE, TILE)]
    sums = [(local, OFFSETS), (local, OFFSETS), (3 * local, width)]
    joined_rows = 3 * local // CHUNKS + buckets // CHUNKS // 2 + SMALL_ROWS
    joined = Shape((CHUNKS // 2, joined_rows, width), BF16)
    scratch = [
        pltpu.VMEM((groups, TILE, local), BF16),
        pltpu.VMEM((SEQMAX, SEQMAX), BF16),
        pltpu.VMEM((SEQMAX, 3 * local), BF16),
        pltpu.VMEM((groups, TILE, width), BF16),
    ]
    if last:
        out_shape = parts + [joined] * 2
        scratch = scratch + [pltpu.VMEM(shape, F32) for shape in sums]
        scratch = scratch + [pltpu.VMEM((CHUNKS,) + joined.shape[1:], BF16)]
    else:
        out_shape = parts + [Shape(shape, F32) for shape in sums]
    scratch = scratch + [pltpu.VMEM((SEQMAX, local), BF16)] * 3
    scratch = scratch + [pltpu.VMEM((heads, SEQMAX, SEQMAX), BF16)]
    scratch = scratch + [pltpu.VMEM((local, OFFSETS), BF16)] * 2
    scratch = scratch + [pltpu.VMEM((SEQMAX, width), BF16)]
    scratch = scratch + [pltpu.VMEM((local, width), BF16)] * 3
    scratch = scratch + [pltpu.VMEM((buckets, width), BF16), pltpu.SemaphoreType.DMA((11,))]
    return kernel_call(
        functools.partial(backward_kernel, block, blocks),
        f"attention_backward_{block}",
        20_000_000_000,
        8_000_000,
        24,
        in_specs=[SCALARS]
        + [IN_VMEM] * groups
        + [IN_HBM] * 11
        + [IN_VMEM] * (2 + len(before)),
        out_specs=[IN_VMEM] * len(out_shape),
        out_shape=out_shape,
        scratch_shapes=scratch,
    )(
        place,
        *context_grads,
        *in_hbm(*kept, weights, *tables, hidden, *w_rows, table),
        rel_rows,
        norms,
        *before,
    )


def offset_rows(rel_buckets):
    plain = jnp.concatenate([rel_buckets[::-1], rel_buckets[:1]])
    back = plain.reshape(OFFSETS // TILE, TILE)[:, ::-1].reshape(OFFSETS)
    return jnp.stack([plain, back])


def layer_norm_parts(resid):
    centered = resid - jnp.mean(resid, axis=-1, keepdims=True)
    scale = lax.rsqrt(jnp.mean(centered * centered, axis=-1, keepdims=True) + NORM_EPS)
    return centered * scale, scale


def layer_norm_back(normal, scale, grad, gain):
    inner = grad * gain
    mean = jnp.mean(inner, axis=-1, keepdims=True)
    along = jnp.mean(inner * normal, axis=-1, keepdims=True)
    return scale * (inner - mean - normal * along)


def token_kernel(place_ref, *refs):
    groups = SEQMAX // TILE
    context_refs, refs = refs[:groups], refs[groups:]
    hidden_ref, out_grad_ref, norms_ref, w_in_ref, w_down_ref, w_out_ref = refs[:6]
    piece_refs, refs = refs[6 : -14 - groups], refs[-14 - groups :]
    (
        output_ref, resid_ref, first_low_ref, act_out, pre_grad_out, ffn_grad_ref, attn_grad_ref,
        norm_grads_ref, *context_grad_refs, packed_vmem, slope_ref, sem, act_ref, pre_grad_ref,
        sems_out,
    ) = refs
    sent = []
    width = hidden_ref.shape[1]
    units = act_ref.shape[2]
    local = context_refs[0].shape[1]
    unit_rows, width_rows = units // CHUNKS, width // CHUNKS

    copies = gather_copies(piece_refs, packed_vmem, place_ref[1], sem)
    for copy in copies:
        copy.start()
    for copy in copies:
        copy.wait()

    def packed(shift, first, rows):
        return packed_vmem[shift - 1, :, first : first + rows, :].reshape(CHUNKS * rows, width)

    def w_in(shift):
        return w_in_ref[...] if shift == 0 else packed(shift, 0, width_rows)

    def w_down(shift):
        return w_down_ref[...] if shift == 0 else packed(shift, width_rows, unit_rows)

    def w_out(shift):
        if shift == 0:
            return w_out_ref[...]
        return packed(shift, width_rows + unit_rows, OUT_ROWS)[:local]

    gain_one, bias_one = norms_ref[0:1, :], norms_ref[1:2, :]
    gain_two, bias_two = norms_ref[2:3, :], norms_ref[3:4, :]
    resid = hidden_ref[...].astype(F32)
    for g in range(groups):
        resid = resid + mm(context_refs[g][...], w_out(g)).astype(BF16).astype(F32)
    normal_one, scale_one = layer_norm_parts(resid)
    first_norm = normal_one * gain_one + bias_one
    first_low = first_norm.astype(BF16)
    first_low_ref[...] = first_low
    ffn_out = first_norm
    for g in range(groups):
        pre_act = mm(first_low, w_in(g))
        area = 0.5 * (1.0 + lax.erf(pre_act * math.sqrt(0.5)))
        activated = (pre_act * area).astype(BF16)
        act_ref[g] = activated
        sent += start_copies([(act_ref.at[g], act_out.at[g])], sems_out.at[pl.ds(g, 1)])
        density = jnp.exp(-0.5 * pre_act * pre_act) * (1.0 / math.sqrt(2.0 * math.pi))
        slope_ref[g] = area + pre_act * density
        ffn_out = ffn_out + mm(activated, w_down(g)).astype(BF16).astype(F32)
    normal_two, scale_two = layer_norm_parts(ffn_out)
    output_ref[...] = (normal_two * gain_two + bias_two).astype(BF16)
    out_grad = out_grad_ref[...].astype(F32)
    norm_grads_ref[...] = jnp.zeros_like(norm_grads_ref)
    norm_grads_ref[2:3, :] = jnp.sum(out_grad * normal_two, axis=0, keepdims=True)
    norm_grads_ref[3:4, :] = jnp.sum(out_grad, axis=0, keepdims=True)
    second_grad = layer_norm_back(normal_two, scale_two, out_grad, gain_two)
    ffn_grad = second_grad.astype(BF16)
    ffn_grad_ref[...] = ffn_grad
    first_grad = second_grad
    for g in range(groups):
        pre_grad = (mm_nt(ffn_grad, w_down(g)) * slope_ref[g]).astype(BF16)
        pre_grad_ref[g] = pre_grad
        sent += start_copies(
            [(pre_grad_ref.at[g], pre_grad_out.at[g])], sems_out.at[pl.ds(groups + g, 1)]
        )
        first_grad = first_grad + mm_nt(pre_grad, w_in(g))
    norm_grads_ref[0:1, :] = jnp.sum(first_grad * normal_one, axis=0, keepdims=True)
    norm_grads_ref[1:2, :] = jnp.sum(first_grad, axis=0, keepdims=True)
    resid_grad = layer_norm_back(normal_one, scale_one, first_grad, gain_one)
    resid_ref[...] = resid_grad
    attn_grad = resid_grad.astype(BF16)
    attn_grad_ref[...] = attn_grad
    for g in range(groups):
        context_grad_refs[g][...] = mm_nt(attn_grad, w_out(g)).astype(BF16)
    wait_copies(sent)


def gather_copies(piece_refs, packed_vmem, replica, sem):
    copies = []
    for (group, relatives, first, rows), ref in zip(GATHERED, piece_refs):
        for i, relative in enumerate(relatives):
            chunk = jnp.bitwise_xor(replica, relative)
            copies.append(
                pltpu.make_async_copy(
                    ref.at[i],
                    packed_vmem.at[group - 1, chunk, pl.ds(first[i] if group == 3 else first, rows), :],
                    sem.at[len(copies)],
                )
            )
    return copies


def reached(axes):
    order = (0,)
    for bit in axes:
        order = order + tuple(relative + bit for relative in order)
    return order


def gathered_layout():
    layout = []
    for group, axes in ((1, (ACROSS_Y, ACROSS_X)), (2, (ACROSS_X, ACROSS_Y))):
        for core in (0, CORE):
            layout += [(group, (core, core + axes[0]), 0, 2 * HALF_ROWS)]
            layout += [(group, (core + axes[1], core + sum(axes)), 0, 2 * HALF_ROWS)]
    halves = ((0, (ACROSS_Y, ACROSS_X)), (HALF_ROWS, (ACROSS_X, ACROSS_Y)))
    for core in (0, CORE):
        both = tuple((core + r, first) for first, axes in halves for r in reached(axes))
        layout += [(3, tuple(r for r, first in both), tuple(first for r, first in both), HALF_ROWS)]
    return layout


ROW_ORDER = reached((ACROSS_Y, ACROSS_X, CORE))
HALF_ROWS = 112
GATHERED = gathered_layout()


def across(array, bit):
    return lax.ppermute(array, "dp", [(i, i ^ bit) for i in range(CHUNKS)])


def nearby(arrays):
    ways = (ACROSS_Y, ACROSS_X, ACROSS_Y + ACROSS_X)
    return [arrays[0]] + [across(array, way) for array, way in zip(arrays[1:], ways)]


def together(*values):
    return lax.optimization_barrier(values)


def token_layer(place, contexts, hidden, out_grad, norms, w_rows, pieces):
    tokens, width = hidden.shape
    local = contexts[0].shape[1]
    units = w_rows[0].shape[1]
    groups = len(contexts)
    rows = width // CHUNKS + units // CHUNKS + OUT_ROWS
    return kernel_call(
        token_kernel,
        "token_layer",
        15_000_000_000,
        18_000_000,
        24,
        in_specs=[SCALARS]
        + [IN_VMEM] * (groups + 6)
        + [ANYWHERE] * len(pieces),
        out_specs=[IN_VMEM] * 3 + [IN_HBM] * 2 + [IN_VMEM] * (3 + groups),
        out_shape=[
            Shape((tokens, width), BF16),
            Shape((tokens, width), F32),
            Shape((tokens, width), BF16),
            hbm_shape((groups, tokens, units), BF16),
            hbm_shape((groups, tokens, units), BF16),
            Shape((tokens, width), BF16),
            Shape((tokens, width), BF16),
            Shape((8, width), F32),
        ]
        + [Shape((tokens, local), BF16)] * groups,
        scratch_shapes=[
            pltpu.VMEM((groups - 1, CHUNKS, rows, width), BF16),
            pltpu.VMEM((groups, tokens, units), F32),
            pltpu.SemaphoreType.DMA((32,)),
            pltpu.VMEM((groups, tokens, units), BF16),
            pltpu.VMEM((groups, tokens, units), BF16),
            pltpu.SemaphoreType.DMA((2 * groups,)),
        ],
    )(place, *contexts, hidden, out_grad, norms, *w_rows, *pieces)


def weight_grad_kernel(half, place_ref, *refs):
    context_refs, refs = refs[:2], refs[2:]
    first_low_ref, act_hbm, pre_grad_hbm, ffn_grad_ref, attn_grad_ref, *out_refs = refs[:7]
    in_ref, down_ref, last_ref, sorted_ref, sems, act_ref, pre_grad_ref, sems_in = refs[7:]
    arriving = start_copies(
        [
            (source.at[2 * half + j], target.at[j])
            for j in range(2)
            for source, target in ((pre_grad_hbm, pre_grad_ref), (act_hbm, act_ref))
        ],
        sems_in,
    )
    local = context_refs[0].shape[1]
    width_rows = in_ref.shape[0] // CHUNKS
    unit_rows = down_ref.shape[0] // CHUNKS
    rows = width_rows + unit_rows
    last_ref[local:, :] = jnp.zeros((last_ref.shape[0] - local, last_ref.shape[1]), BF16)
    copies = []
    for j, axes in enumerate(PART_AXES):
        last_ref[:local, :] = mm_tn(context_refs[j][...], attn_grad_ref[...]).astype(BF16)
        wait_copies(arriving[2 * j : 2 * j + 2])
        in_ref[...] = mm_tn(first_low_ref[...], pre_grad_ref[j]).astype(BF16)
        down_ref[...] = mm_tn(act_ref[j], ffn_grad_ref[...]).astype(BF16)
        for side, core in ((1, CORE), (0, 0)):
            for slot, relative in enumerate(reached(axes[::-1])):
                chunk = jnp.bitwise_xor(relative + core, place_ref[1])
                at = pl.multiple_of(chunk * width_rows, 16)
                sorted_ref[side, j, slot, :width_rows] = in_ref[pl.ds(at, width_rows), :]
                at = pl.multiple_of(chunk * unit_rows, 16)
                sorted_ref[side, j, slot, width_rows:rows] = down_ref[pl.ds(at, unit_rows), :]
                at = pl.multiple_of(chunk * OUT_ROWS, 16)
                sorted_ref[side, j, slot, rows:] = last_ref[pl.ds(at, OUT_ROWS), :]
            copies += start_copies(
                [(sorted_ref.at[side, j], out_refs[side].at[j])], sems.at[pl.ds(2 * side + j, 1)]
            )
    wait_copies(copies)


PART_AXES = ((ACROSS_Y, ACROSS_X), (ACROSS_X, ACROSS_Y))


def weight_grads(half, place, contexts, first_low, act, pre_grad, ffn_grad, attn_grad):
    units = act.shape[2]
    width = first_low.shape[1]
    rows = width // CHUNKS + units // CHUNKS + OUT_ROWS
    return kernel_call(
        functools.partial(weight_grad_kernel, half),
        f"weight_grads_{half}",
        4_000_000_000,
        7_000_000,
        15,
        in_specs=[SCALARS] + [IN_VMEM] * 3 + [IN_HBM] * 2 + [IN_VMEM] * 2,
        out_specs=[IN_HBM] * 2,
        out_shape=[hbm_shape((2, CHUNKS // 2, rows, width), BF16)] * 2,
        scratch_shapes=[
            pltpu.VMEM((width, width), BF16),
            pltpu.VMEM((units, width), BF16),
            pltpu.VMEM((CHUNKS * OUT_ROWS, width), BF16),
            pltpu.VMEM((2, 2, CHUNKS // 2, rows, width), BF16),
            pltpu.SemaphoreType.DMA((4,)),
            pltpu.VMEM((2, act.shape[1], units), BF16),
            pltpu.VMEM((2, act.shape[1], units), BF16),
            pltpu.SemaphoreType.DMA((4,)),
        ],
    )(
        place,
        *contexts[2 * half : 2 * half + 2],
        first_low,
        *in_hbm(act, pre_grad),
        ffn_grad,
        attn_grad,
    )


def add(left, right):
    return (left.astype(F32) + right.astype(F32)).astype(BF16)


def total_of(arrays):
    return sum(array.astype(F32) for array in arrays).astype(BF16)


def reorder_kernel(place_ref, *refs):
    out_ref = refs[-1]
    groups = out_ref.shape[1]
    blocks = out_ref.shape[0]
    per = len(refs[:-1]) // groups
    for shift in range(groups):
        origin = jnp.bitwise_xor(place_ref[0], shift)
        for b in range(blocks):
            if per == 1:
                out_ref[b, origin] = refs[shift][b * TILE : (b + 1) * TILE, :]
            else:
                out_ref[b, origin] = refs[b * groups + shift][...]


def reorder(place, pieces, blocks):
    width = pieces[0].shape[1]
    groups = SEQMAX // TILE
    out = kernel_call(
        reorder_kernel,
        "reorder",
        0,
        3_000_000,
        8,
        in_specs=[SCALARS] + [IN_VMEM] * len(pieces),
        out_specs=IN_VMEM,
        out_shape=Shape((blocks, groups, TILE, width), BF16),
    )(place, *pieces)
    return out.reshape(blocks * SEQMAX, width)


def unpack_kernel(place_ref, *refs):
    piece_refs, refs = refs[:CHUNKS], refs[CHUNKS:]
    grad_in_ref, grad_down_ref, grad_out_ref, q_ref, k_ref, v_ref, table_ref = refs[:7]
    norm_refs, all_ref, norms_ref = refs[7:11], *refs[11:]
    local = q_ref.shape[0]
    width_rows = grad_in_ref.shape[0] // CHUNKS
    unit_rows = grad_down_ref.shape[0] // CHUNKS
    table_rows = table_ref.shape[0] // CHUNKS
    row_rows = all_ref.shape[0] // CHUNKS
    columns = norms_ref.shape[1]
    out_at = width_rows + unit_rows
    table_at = out_at + OUT_ROWS
    norm_at = table_at + table_rows
    rows_at = norm_at + SMALL_ROWS
    for relative, ref in zip(ROW_ORDER, piece_refs):
        chunk = jnp.bitwise_xor(place_ref[1], relative)
        at = pl.multiple_of(chunk * width_rows, 8)
        grad_in_ref[pl.ds(at, width_rows), :] = ref[:width_rows, :].astype(F32)
        at = pl.multiple_of(chunk * unit_rows, 8)
        grad_down_ref[pl.ds(at, unit_rows), :] = ref[width_rows:out_at, :].astype(F32)
        at = pl.multiple_of(chunk * table_rows, 8)
        table_ref[pl.ds(at, table_rows), :] = ref[table_at:norm_at, :].astype(F32)
        norms_ref[pl.ds(chunk, 1), :] = ref[norm_at:rows_at, :columns].astype(F32)[:1]
        at = pl.multiple_of(chunk * row_rows, 8)
        all_ref[pl.ds(at, row_rows), :] = ref[rows_at:, :].astype(F32)

        @pl.when(chunk * OUT_ROWS < grad_out_ref.shape[0])
        def out_rows(chunk=chunk, ref=ref):
            at = pl.multiple_of(chunk * OUT_ROWS, 8)
            grad_out_ref[pl.ds(at, OUT_ROWS), :] = ref[out_at:table_at, :].astype(F32)

    for i, ref in enumerate((q_ref, k_ref, v_ref)):
        ref[...] = all_ref[i * local : (i + 1) * local, :]
    for i, ref in enumerate(norm_refs):
        ref[:columns] = norms_ref[2 * i, :]
        ref[columns:] = norms_ref[2 * i + 1, :]


def unpack(place, pieces, width, units, local, buckets):
    return kernel_call(
        unpack_kernel,
        "unpack",
        0,
        14_000_000,
        10,
        in_specs=[SCALARS] + [IN_VMEM] * CHUNKS,
        out_specs=[IN_VMEM] * 11,
        out_shape=[Shape((width, width), F32), Shape((units, width), F32)]
        + [Shape((local, width), F32)] * 4
        + [Shape((buckets, width), F32)]
        + [Shape((width,), F32)] * 4,
        scratch_shapes=[
            pltpu.VMEM((3 * local, width), F32),
            pltpu.VMEM((CHUNKS, 4 * width // CHUNKS), F32),
        ],
    )(place, *pieces)


def send(array, bits):
    return lax.ppermute(array, "tensor", [(i, i ^ bits) for i in range(SEQMAX // TILE)])


def exchange(pieces):
    return [pieces[0]] + [send(piece, r) for r, piece in enumerate(pieces) if r > 0]


def spread(array):
    near, far = send(array, 1), send(array, 2)
    return [array, near, far, send(far, 1)]


def shards(
    n_dp,
    n_tensor,
    hidden,
    out_grad,
    w_query,
    w_key,
    w_value,
    w_out,
    w_in,
    w_down,
    bucket_table,
    gain_one,
    bias_one,
    gain_two,
    bias_two,
    rel_buckets,
    group_counts,
    key_mask,
):
    tokens, width = hidden.shape
    local = w_query.shape[1]
    units = w_in.shape[1]
    buckets = bucket_table.shape[0]
    blocks = tokens // SEQMAX
    mine = tokens // n_tensor
    by_axis = n_dp == CHUNKS
    me = lax.axis_index("tensor")
    replica = lax.axis_index("dp") if by_axis else jnp.int32(0)
    place = jnp.stack([me, replica]).astype(jnp.int32)
    rel_rows = offset_rows(rel_buckets)
    width_rows, unit_rows = width // CHUNKS, units // CHUNKS
    padded = jnp.pad(w_out, ((0, CHUNKS * OUT_ROWS - local), (0, 0)))

    w_rows = (w_query.T, w_key.T, w_value.T)

    def my_rows(array):
        array = array.reshape(blocks, n_tensor, TILE, width)
        return lax.dynamic_index_in_dim(array, me, 1, keepdims=False).reshape(mine, width)

    def forward(block, context):
        weights, *context = forward_attention(
            block, place, group_counts, tables, rows, key_mask, context
        )
        return weights, context

    if by_axis:
        pick = lambda array, rows: lax.dynamic_slice_in_dim(array, replica * rows, rows, 0)
        piece = jnp.concatenate(
            [pick(w_in, width_rows), pick(w_down, unit_rows), pick(padded, OUT_ROWS)], 0
        )
        near, far = send(piece, 1), send(piece, 2)
        (*tables, q, k, v), saved = prepare(*w_rows, bucket_table, rel_rows, hidden)
        rows = (q, k, v)
        my_hidden, my_out_grad = my_rows(hidden), my_rows(out_grad)
        near, far, tables, rows, saved, my_hidden, my_out_grad = together(
            near, far, tables, rows, saved, my_hidden, my_out_grad
        )
        last = send(far, 1)
        near_y, far_x = across(near[None], ACROSS_Y), across(far[None], ACROSS_X)
        kept_0, context = forward(0, [])
        near, far, near_y, far_x, last, kept_0, context, tables, rows = together(
            near, far, near_y, far_x, last, kept_0, context, tables, rows
        )
        near = jnp.concatenate([near[None], near_y], 0)
        far = jnp.concatenate([far[None], far_x], 0)
        near_x, far_y = across(near, ACROSS_X), across(far, ACROSS_Y)
        near_core = across(near, CORE)
        top, low = last[None, :HALF_ROWS], last[None, HALF_ROWS:]
        top_y, low_x = across(top, ACROSS_Y), across(low, ACROSS_X)
        kept_1, context = forward(1, context)
        (
            near, near_x, near_core, far, far_y, top, top_y, low, low_x, context, kept_0, kept_1,
        ) = together(
            near, near_x, near_core, far, far_y, top, top_y, low, low_x, context, kept_0, kept_1,
        )
        contexts = exchange([piece.reshape(mine, local) for piece in context])
        top = jnp.concatenate([top, top_y], 0)
        low = jnp.concatenate([low, low_x], 0)
        top_x, low_y = across(top, ACROSS_X), across(low, ACROSS_Y)
        near, near_x, near_core, far, far_y, top, top_x, low, low_y, contexts, kept_0, kept_1 = (
            together(
                near, near_x, near_core, far, far_y, top, top_x, low, low_y, contexts, kept_0,
                kept_1,
            )
        )
        both = jnp.concatenate([top, top_x, low, low_y], 0)
        gathered = [near, near_x, near_core, across(near_x, CORE)]
        gathered += [far, far_y, across(far, CORE), across(far_y, CORE)]
        gathered += [both, across(both, CORE)]
    else:
        (*tables, q, k, v), saved = prepare(*w_rows, bucket_table, rel_rows, hidden)
        rows = (q, k, v)
        stacked = jnp.concatenate(
            [
                w_in.reshape(CHUNKS, width_rows, width),
                w_down.reshape(CHUNKS, unit_rows, width),
                padded.reshape(CHUNKS, OUT_ROWS, width),
            ],
            1,
        )
        sent = spread(stacked)
        gathered = [
            jnp.stack(
                [
                    sent[group][chunk, at : at + rows]
                    for chunk, at in zip(chunks, first if group == 3 else (first,) * len(chunks))
                ]
            )
            for group, chunks, first, rows in GATHERED
        ]
        kept_0, context = forward(0, [])
        kept_1, context = forward(1, context)
        contexts = exchange([piece.reshape(mine, local) for piece in context])
        my_hidden, my_out_grad = my_rows(hidden), my_rows(out_grad)
    *tables, q, k, v = saved
    norms = jnp.stack([gain_one, bias_one, gain_two, bias_two])
    (
        output, resid_grad, first_low, act, pre_grad, ffn_grad, attn_grad, norm_grads, *back,
    ) = token_layer(
        place, contexts, my_hidden, my_out_grad, norms, (w_in, w_down, w_out), gathered
    )
    norm_grads = norm_grads[:4].reshape(CHUNKS, 4 * width // CHUNKS)

    def backward(block, kept, before):
        own, near, far, *before = backward_attention(
            block, blocks, place, back, (q, k, v), kept, tables, hidden, w_rows, bucket_table, rel_rows,
            norm_grads, before,
        )
        return [own, near, far], before

    sources = (first_low, act, pre_grad, ffn_grad, attn_grad)
    keep_1, give_1 = weight_grads(1, place, contexts, *sources)
    back, keep_1, give_1, contexts, sources, output, resid_grad, norm_grads, kept_0, kept_1 = (
        together(
            back, keep_1, give_1, contexts, sources, output, resid_grad, norm_grads, kept_0, kept_1
        )
    )
    back = exchange(back)
    core_1 = across(give_1, CORE) if by_axis else give_1
    keep_0, give_0 = weight_grads(0, place, contexts, *sources)
    (
        back, core_1, keep_0, give_0, keep_1, output, resid_grad, norm_grads, kept_0, kept_1,
        tables, place,
    ) = together(
        back, core_1, keep_0, give_0, keep_1, output, resid_grad, norm_grads, kept_0, kept_1,
        tables, place,
    )
    back = [piece.reshape(blocks, TILE, local) for piece in back]

    def first_stage(keep, got):
        sums = [add(keep[j, 2:], got[j, 2:]) for j in range(2)]
        return [across(part, axes[0]) for part, axes in zip(sums, PART_AXES)]

    def second_stage(terms):
        kept, got = [], []
        for j, axes in enumerate(PART_AXES):
            given = [total_of([a[j, 1:2], b[j, 1:2], c[j][1:2]]) for a, b, c in terms]
            kept.append([[a[j, 0], b[j, 0], c[j][0]] for a, b, c in terms])
            got.append(across(jnp.concatenate(given, 0), axes[1]))
        return kept, got

    stage_1, core_0 = [], give_0
    if by_axis:
        stage_1 = first_stage(keep_1, core_1)
        core_0 = across(give_0, CORE)
    out_near, out_far = send(output, 1), send(output, 2)
    parts, before = backward(0, kept_0, ())
    (
        parts, before, stage_1, core_0, core_1, keep_0, keep_1, out_near, out_far, output,
        resid_grad, norm_grads, kept_1, tables, place, back,
    ) = together(
        parts, before, stage_1, core_0, core_1, keep_0, keep_1, out_near, out_far, output,
        resid_grad, norm_grads, kept_1, tables, place, back,
    )
    stage_0 = first_stage(keep_0, core_0) if by_axis else []
    parts = [parts[0], send(parts[1], 1), parts[2]]
    out_last = send(out_far, 1)
    parts_1, before = backward(1, kept_1, before)
    (
        parts, parts_1, before, stage_0, stage_1, core_0, core_1, keep_0, keep_1, out_last,
        resid_grad,
    ) = together(
        parts, parts_1, before, stage_0, stage_1, core_0, core_1, keep_0, keep_1, out_last,
        resid_grad,
    )
    keep, give = before
    thirds, arrived = [], keep
    if not by_axis:
        joined = lax.psum(jnp.concatenate([keep, give], 0).astype(F32), "dp").astype(BF16)
    if by_axis:
        thirds = second_stage(((keep_0, core_0, stage_0), (keep_1, core_1, stage_1)))
        arrived = across(give, CORE)
    far_0 = send(add(parts[2], parts[1][TILE:]), 2)
    near_1 = send(parts_1[1], 1)
    (
        parts, parts_1, far_0, near_1, thirds, arrived, keep, give, resid_grad, out_last,
    ) = together(
        parts, parts_1, far_0, near_1, thirds, arrived, keep, give, resid_grad, out_last,
    )

    def total(block, pieces):
        wide = resid_grad[block * TILE : (block + 1) * TILE]
        for piece in pieces:
            wide = wide + piece.astype(F32)
        return wide.astype(BF16)

    def joint(arrays, way):
        rows = [array.shape[0] for array in arrays]
        got = send(jnp.concatenate(arrays, 0), way)
        return [got[sum(rows[:i]) : sum(rows[: i + 1])] for i in range(len(rows))]

    grad_0 = total(0, [parts[0], parts[1][:TILE], far_0])
    sum_1 = add(parts_1[2], near_1[TILE:])
    output = reorder(place, [output, out_near, out_far, out_last], blocks)
    shard, near_0 = [], [grad_0]
    if by_axis:
        for half in range(2):
            for j in range(2):
                shard.append(total_of([*thirds[0][j][half], thirds[1][j][half]]))
        near_0 = near_0 + [shard[3]]
        sums = add(keep, arrived)
        arrived = nearby([sums[i : i + 1] for i in range(CHUNKS // 2)])
    near_0 = joint(near_0, 1)
    far_0, far_1 = joint([grad_0, sum_1], 2)
    grad_0, near_0, far_0, far_1, near_1, parts_1, arrived, resid_grad, output, shard = together(
        grad_0, near_0, far_0, far_1, near_1, parts_1, arrived, resid_grad, output, shard
    )
    grad_1 = total(1, [parts_1[0], near_1[:TILE], far_1])
    if by_axis:
        joined = total_of(arrived)
    row_rows, pos_rows = 3 * local // CHUNKS, buckets // CHUNKS // 2
    slots = joined.shape[0]
    row_grads = joined[:, :row_rows]
    pos = joined[:, row_rows : row_rows + pos_rows]
    pos = jnp.concatenate([pos[:, :, : 2 * local], pos[:, :, 2 * local :]], 1)
    w_table = jnp.concatenate([w_rows[1], w_rows[0]], 0)
    table_part = mm(pos.reshape(slots * 2 * pos_rows, 2 * local), w_table)
    table_part = table_part.astype(BF16).reshape(slots, 2 * pos_rows, width)
    small = jnp.concatenate([table_part, joined[:, row_rows + pos_rows :]], 1)
    small_rows = small.shape[1]
    small = small.reshape(slots * small_rows, width)
    small = [small, None, None, send(small, 3)]
    shard_far = []
    if by_axis:
        *shard_1, small[1] = joint([shard[1], small[0]], 1)
        *shard_2, small[2] = joint([add(shard[2], near_0[1]), small[0]], 2)
        shard_far = shard_1 + shard_2
    else:
        small[1], small[2] = send(small[0], 1), send(small[0], 2)
    grad_0, near_0, far_0, grad_1, row_grads, small, shard, shard_far = together(
        grad_0, near_0, far_0, grad_1, row_grads, small, shard, shard_far
    )
    near_1, last_0 = joint([grad_1, far_0], 1)
    far_1 = send(grad_1, 2)
    small = [part.astype(F32) for part in small]
    small = ((small[0] + small[1]) + (small[2] + small[3])).astype(BF16)
    if by_axis:
        shard = total_of([shard[0], *shard_far])
        pieces = nearby([jnp.concatenate([shard, small, row_grads[0]], 0)] * 4)
        grad_0, near_0, far_0, last_0, grad_1, near_1, far_1, pieces = together(
            grad_0, near_0, far_0, last_0, grad_1, near_1, far_1, pieces
        )
        pieces = pieces + [across(piece, CORE) for piece in pieces]
    else:
        natural = []
        for keep, give in ((keep_0, give_0), (keep_1, give_1)):
            for j, axes in enumerate(PART_AXES):
                chunks = reached(axes[::-1] + (CORE,))
                both = jnp.concatenate([keep[j], give[j]], 0)
                natural.append(jnp.stack([both[chunks.index(c)] for c in range(CHUNKS)]))
        shard = jnp.stack(exchange(natural)).astype(F32)
        shard = lax.psum(sum(shard[r] for r in range(n_tensor)), "dp").astype(BF16)
        small = small.reshape(slots, small_rows, width)
        pieces = [
            jnp.concatenate([shard[chunk], small[slot], row_grads[slot]], 0)
            for slot, chunk in enumerate(ROW_ORDER)
        ]
    last_1 = send(far_1, 1)
    if by_axis:
        last_1, pieces = together(last_1, pieces)
    grad_hidden = reorder(
        place, [grad_0, near_0[0], far_0, last_0, grad_1, near_1, far_1, last_1], blocks
    )
    (
        grad_in, grad_down, grad_out, grad_query, grad_key, grad_value, grad_table, *norm_grads,
    ) = unpack(place, pieces, width, units, local, buckets)
    return (
        output,
        grad_hidden,
        grad_query.T,
        grad_key.T,
        grad_value.T,
        grad_out,
        grad_in,
        grad_down,
        grad_table,
        *norm_grads,
    )


def solution(mesh):
    in_specs = (
        P("dp", None),
        P("dp", None),
        P(None, "tensor"),
        P(None, "tensor"),
        P(None, "tensor"),
        P("tensor", None),
        P(None, "tensor"),
        P("tensor", None),
        P(),
        P(),
        P(),
        P(),
        P(),
        P(),
        P("dp", None),
        P("dp"),
    )
    out_specs = (
        P("dp", None),
        P("dp", None),
        P(None, "tensor"),
        P(None, "tensor"),
        P(None, "tensor"),
        P("tensor", None),
        P(None, "tensor"),
        P("tensor", None),
        P(),
        P(),
        P(),
        P(),
        P(),
    )
    body = functools.partial(shards, mesh.shape["dp"], mesh.shape["tensor"])
    return jax.shard_map(body, mesh=mesh, in_specs=in_specs, out_specs=out_specs, check_vma=False)
```

```python
import functools
import math

import jax
import jax.numpy as jnp
from jax import lax
from jax.experimental import pallas as pl
from jax.experimental.pallas import tpu as pltpu
from jax.sharding import PartitionSpec as P

NORM_EPS = 1e-07
HEAD_DIM = 64
SEQMAX = 512
TILE = 128
WINDOW = SEQMAX + TILE
OFFSETS = 2 * SEQMAX
NEGATIVE = -1e30
CHUNKS = 8
CORE, ACROSS_X, ACROSS_Y = 1, 2, 4
OUT_ROWS = 32
SMALL_ROWS = 8
F32 = jnp.float32
BF16 = jnp.bfloat16


def score_factor():
    return 1.0 / math.sqrt(3.0 * HEAD_DIM)


def mm(left, right):
    return jnp.dot(left, right, preferred_element_type=F32)


def mm_nt(left, right):
    return lax.dot_general(left, right, (((1,), (1,)), ((), ())), preferred_element_type=F32)


def mm_tn(left, right):
    return lax.dot_general(left, right, (((0,), (0,)), ((), ())), preferred_element_type=F32)


def starts_of(places, counts_ref):
    long_end = SEQMAX * counts_ref[0, 0]
    mid_end = long_end + SEQMAX // 2 * counts_ref[0, 1]
    in_long = places < long_end
    in_mid = places < mid_end
    anchor = jnp.where(in_long, 0, jnp.where(in_mid, long_end, mid_end))
    shift = jnp.where(in_long, 9, jnp.where(in_mid, 8, 7))
    return anchor + lax.shift_left(lax.shift_right_logical(places - anchor, shift), shift)


def tile_iotas():
    rows = lax.broadcasted_iota(jnp.int32, (TILE, TILE), 0)
    lanes = lax.broadcasted_iota(jnp.int32, (TILE, TILE), 1)
    return rows, lanes


def lane_tiles(wide):
    return [wide[:, c : c + TILE] for c in range(0, wide.shape[1], TILE)]


def skew(wide):
    rows, lanes = tile_iotas()
    keep = lanes <= rows
    turned = [pltpu.roll(part, 1, 1, stride=1, stride_axis=0) for part in lane_tiles(wide)]
    return jnp.concatenate(
        [jnp.where(keep, turned[c], turned[c + 1]) for c in range(len(turned) - 1)], axis=1
    )


def unskew(flipped):
    rows, lanes = tile_iotas()
    late = lanes > rows
    turned = [pltpu.roll(part, 1, 1, stride=1, stride_axis=0) for part in lane_tiles(flipped)]
    zero = jnp.zeros((TILE, TILE), F32)
    turned = [zero] + turned + [zero]
    return jnp.concatenate(
        [jnp.where(late, turned[c], turned[c + 1]) for c in range(len(turned) - 1)], axis=1
    )


def window_of(tile_at):
    low = SEQMAX - TILE - tile_at
    return slice(low, low + WINDOW)


def one_hot_columns(rel_ref, row, buckets):
    ids = lax.broadcasted_iota(jnp.int32, (buckets, OFFSETS), 0)
    return (ids == rel_ref[row : row + 1, :]).astype(BF16)


def split_low(wide):
    high = wide.astype(BF16)
    return high, (wide - high.astype(F32)).astype(BF16)


SCALARS = pl.BlockSpec(memory_space=pltpu.SMEM)
ANYWHERE = pl.BlockSpec(memory_space=pl.ANY)
IN_HBM = pl.BlockSpec(memory_space=pltpu.HBM)
IN_VMEM = pl.BlockSpec(memory_space=pltpu.VMEM)
Shape = jax.ShapeDtypeStruct


def in_hbm(*arrays):
    return [pltpu.with_memory_space_constraint(array, pltpu.HBM) for array in arrays]


def hbm_shape(shape, kind):
    return pltpu.HBM(shape, kind)


def kernel_call(kernel, name, flops, moved, vmem, **rest):
    return pl.pallas_call(
        kernel,
        compiler_params=pltpu.CompilerParams(vmem_limit_bytes=vmem * 2**20),
        cost_estimate=pl.CostEstimate(flops=flops, bytes_accessed=moved, transcendentals=0),
        name=name,
        **rest,
    )


PART_AXES = ((ACROSS_Y, ACROSS_X), (ACROSS_X, ACROSS_Y))


def start_copies(pairs, sems):
    copies = [
        pltpu.make_async_copy(source, target, sems.at[i]) for i, (source, target) in enumerate(pairs)
    ]
    for copy in copies:
        copy.start()
    return copies


def wait_copies(copies):
    for copy in copies:
        copy.wait()


def prepare_kernel(
    wq_ref, wk_ref, wv_ref, table_ref, rel_ref, hidden_ref, pk_ref, pq_ref, q_ref, k_ref, v_ref,
    pk_back_out, pq_back_out, q_out, k_out, v_out, pk_back, pq_back, sems,
):
    table = table_ref[...]
    buckets = table.shape[0]
    pos_key = mm_nt(wk_ref[...], table).astype(BF16)
    pos_query = mm_nt(wq_ref[...], table).astype(BF16)
    plain = one_hot_columns(rel_ref, 0, buckets)
    pk_ref[...] = mm(pos_key, plain).astype(BF16)
    pq_ref[...] = mm(pos_query, plain).astype(BF16)
    back = one_hot_columns(rel_ref, 1, buckets)
    pk_back[...] = mm(pos_key, back).astype(BF16)
    pq_back[...] = mm(pos_query, back).astype(BF16)
    copies = start_copies([(pk_back, pk_back_out), (pq_back, pq_back_out)], sems)
    hidden = hidden_ref[...]
    for i, (ref, w_ref, out) in enumerate(
        ((q_ref, wq_ref, q_out), (k_ref, wk_ref, k_out), (v_ref, wv_ref, v_out))
    ):
        ref[...] = mm_nt(hidden, w_ref[...]).astype(BF16)
        copies += start_copies([(ref, out)], sems.at[pl.ds(2 + i, 1)])
    wait_copies(copies)


def prepare(w_query, w_key, w_value, table, rel_rows, hidden):
    local = w_query.shape[0]
    tokens = hidden.shape[0]
    table_kind = ((local, OFFSETS), BF16)
    row_kind = ((tokens, local), BF16)
    out = kernel_call(
        prepare_kernel,
        "prepare",
        4_000_000_000,
        6_000_000,
        10,
        in_specs=[IN_VMEM] * 6,
        out_specs=[IN_VMEM] * 5 + [IN_HBM] * 5,
        out_shape=[Shape(*table_kind)] * 2
        + [Shape(*row_kind)] * 3
        + [hbm_shape(*table_kind)] * 2
        + [hbm_shape(*row_kind)] * 3,
        scratch_shapes=[pltpu.VMEM(*table_kind)] * 2 + [pltpu.SemaphoreType.DMA((5,))],
    )(w_query, w_key, w_value, table, rel_rows, hidden)
    return out[:5], out[5:]


def forward_kernel(
    block, place_ref, counts_ref, pk_ref, pq_ref, q_ref, k_ref, v_ref, mask_ref, *rest
):
    before, rest = rest[: 3 if block else 0], rest[3 if block else 0 :]
    weights_out, context_refs, rest = rest[0], rest[1:4], rest[4:]
    context_ref, bias_ref, rel_score_ref, weights_ref, sems_out = rest
    heads = q_ref.shape[1] // HEAD_DIM
    first = block * SEQMAX
    here = slice(first, first + SEQMAX)
    column = starts_of(lax.broadcasted_iota(jnp.int32, (SEQMAX, 1), 0) + first, counts_ref)
    row = starts_of(lax.broadcasted_iota(jnp.int32, (1, SEQMAX), 1) + first, counts_ref)
    row = jnp.where(mask_ref[block] == 1, row, -1)
    bias_ref[...] = jnp.where(column == row, 0.0, NEGATIVE)
    copies = []
    for head in range(heads):
        part = slice(head * HEAD_DIM, (head + 1) * HEAD_DIM)
        queries = q_ref[here, part]
        keys = k_ref[here, part]
        values = v_ref[here, part]
        for at in range(0, SEQMAX, TILE):
            rel = mm(keys[at : at + TILE], pq_ref[part, window_of(at)])
            rel_score_ref[at : at + TILE, :] = skew(rel)
        for at in range(0, SEQMAX, TILE):
            rows = slice(at, at + TILE)
            raw = mm_nt(queries[rows], keys)
            raw = raw + skew(mm(queries[rows], pk_ref[part, window_of(at)]))
            raw = raw + rel_score_ref[:, rows].T
            scaled = raw * score_factor() + bias_ref[rows, :]
            top = jnp.max(scaled, axis=-1, keepdims=True)
            exponent = jnp.exp(scaled - top)
            total = jnp.sum(exponent, axis=-1, keepdims=True)
            weights = (exponent * (1.0 / total)).astype(BF16)
            weights_ref[head, rows, :] = weights
            relative = jnp.bitwise_xor(at // TILE, place_ref[0])
            context_ref[relative, :, part] = mm(weights, values).astype(BF16)
        copies += start_copies(
            [(weights_ref.at[head], weights_out.at[head])], sems_out.at[pl.ds(head, 1)]
        )
    at = 0
    for n, ref in enumerate(context_refs):
        for r in range(ref.shape[0]):
            for b in range(block):
                ref[r, b * TILE : (b + 1) * TILE] = before[n][r, b * TILE : (b + 1) * TILE]
            ref[r, block * TILE : (block + 1) * TILE] = context_ref[at]
            at += 1
    wait_copies(copies)


def forward_attention(block, place, counts, tables, rows, key_mask, context):
    tokens, local = rows[0].shape
    heads = local // HEAD_DIM
    blocks = tokens // SEQMAX
    groups = SEQMAX // TILE
    return kernel_call(
        functools.partial(forward_kernel, block),
        f"attention_forward_{block}",
        10_000_000_000,
        5_000_000,
        12,
        in_specs=[SCALARS] * 2 + [IN_VMEM] * (6 + len(context)),
        out_specs=[IN_HBM] + [IN_VMEM] * 3,
        out_shape=[hbm_shape((heads, SEQMAX, SEQMAX), BF16)]
        + [Shape((n, (block + 1) * TILE, local), BF16) for n in (1, 1, 2)],
        scratch_shapes=[pltpu.VMEM((groups, TILE, local), BF16)]
        + [pltpu.VMEM((SEQMAX, SEQMAX), F32)] * 2
        + [pltpu.VMEM((heads, SEQMAX, SEQMAX), BF16), pltpu.SemaphoreType.DMA((heads,))],
    )(place, counts, *tables, *rows, key_mask.reshape(blocks, 1, SEQMAX), *context)


def backward_kernel(block, blocks, place_ref, *refs):
    groups = SEQMAX // TILE
    cg_refs, refs = refs[:groups], refs[groups:]
    q_hbm, k_hbm, v_hbm, weights_hbm, pk_hbm, pq_hbm, hidden_hbm = refs[:7]
    w_hbms, table_hbm, rel_ref, norms_ref = refs[7:10], *refs[10:13]
    refs = refs[13:]
    before, refs = (refs[:3], refs[3:]) if block > 0 else (None, refs)
    q_ref, k_ref, v_ref, weights_ref, pk_back_ref, pq_back_ref, hidden_ref = refs[-12:-5]
    wq_ref, wk_ref, wv_ref, table_ref, sems = refs[-5:]
    refs = refs[:-12]
    local = wq_ref.shape[0]
    heads = local // HEAD_DIM
    buckets = table_ref.shape[0]
    if block < blocks - 1:
        part_refs, refs = refs[:3], refs[3:]
        rg_key_ref, rg_query_ref, sum_ref, cg_ref, ds_ref, rows_ref, part_ref = refs
    else:
        part_refs, joined_refs, refs = refs[:3], refs[3:5], refs[5:]
        cg_ref, ds_ref, rows_ref, part_ref, rg_key_ref, rg_query_ref, sum_ref, joined_ref = refs
    first = block * SEQMAX
    copies = start_copies(
        [
            (q_hbm.at[pl.ds(first, SEQMAX), :], q_ref),
            (k_hbm.at[pl.ds(first, SEQMAX), :], k_ref),
            (v_hbm.at[pl.ds(first, SEQMAX), :], v_ref),
            (weights_hbm, weights_ref),
            (pk_hbm, pk_back_ref),
            (pq_hbm, pq_back_ref),
            (hidden_hbm.at[pl.ds(first, SEQMAX), :], hidden_ref),
            (w_hbms[0], wq_ref),
            (w_hbms[1], wk_ref),
            (w_hbms[2], wv_ref),
        ]
        + ([(table_hbm, table_ref)] if block == blocks - 1 else []),
        sems,
    )
    if before is None:
        rg_key_ref[...] = jnp.zeros_like(rg_key_ref)
        rg_query_ref[...] = jnp.zeros_like(rg_query_ref)
    else:
        rg_key_ref[...] = before[0][...]
        rg_query_ref[...] = before[1][...]
    me = place_ref[0]
    for relative in range(groups):
        cg_ref[jnp.bitwise_xor(me, relative)] = cg_refs[relative][block]
    wait_copies(copies[:6])

    tile_rows, tile_lanes = tile_iotas()
    flip = (tile_rows + tile_lanes == TILE - 1).astype(BF16)

    def flipped(low):
        return jnp.concatenate([mm(part, flip) for part in lane_tiles(low)], axis=1)

    for head in range(heads):
        part = slice(head * HEAD_DIM, (head + 1) * HEAD_DIM)
        at_k = slice(local + head * HEAD_DIM, local + (head + 1) * HEAD_DIM)
        at_v = slice(2 * local + head * HEAD_DIM, 2 * local + (head + 1) * HEAD_DIM)
        queries = q_ref[:, part]
        keys = k_ref[:, part]
        values = v_ref[:, part]
        value_grad = jnp.zeros((SEQMAX, HEAD_DIM), F32)
        for at in range(0, SEQMAX, TILE):
            rows = slice(at, at + TILE)
            cotangent = cg_ref[at // TILE, :, part]
            low_weights = weights_ref[head, rows, :]
            weights = low_weights.astype(F32)
            weight_grad = mm_nt(cotangent, values)
            inner = jnp.sum(weights * weight_grad, axis=-1, keepdims=True)
            score_grad = (weights * (weight_grad - inner) * score_factor()).astype(BF16)
            ds_ref[rows, :] = score_grad
            value_grad = value_grad + mm_tn(low_weights, cotangent)
            by_offset = unskew(flipped(score_grad)).astype(BF16)
            window = window_of(at)
            query_grad = mm(score_grad, keys) + mm_nt(by_offset, pk_back_ref[part, window])
            rows_ref[rows, part] = query_grad.astype(BF16)
            rg_key_ref[part, window] += mm_tn(queries[rows], by_offset)
        rows_ref[:, at_v] = value_grad.astype(BF16)
        for at in range(0, SEQMAX, TILE):
            rows = slice(at, at + TILE)
            turned = ds_ref[:, rows].T
            by_offset = unskew(flipped(turned)).astype(BF16)
            window = window_of(at)
            key_grad = mm(turned, queries) + mm_nt(by_offset, pq_back_ref[part, window])
            rows_ref[rows, at_k] = key_grad.astype(BF16)
            rg_query_ref[part, window] += mm_tn(keys[rows], by_offset)
    wait_copies(copies[6:])
    total = mm(rows_ref[:, :local], wq_ref[...])
    total = total + mm(rows_ref[:, local : 2 * local], wk_ref[...])
    total = total + mm(rows_ref[:, 2 * local :], wv_ref[...])
    for at in range(0, SEQMAX, TILE):
        part_ref[jnp.bitwise_xor(at // TILE, me)] = total[at : at + TILE].astype(BF16)
    part_refs[0][...] = part_ref[0]
    part_refs[1][:TILE, :] = part_ref[1]
    part_refs[1][TILE:, :] = part_ref[3]
    part_refs[2][...] = part_ref[2]
    sums = mm_tn(rows_ref[...], hidden_ref[...])
    sum_ref[...] = sums if before is None else before[2][...] + sums
    if block < blocks - 1:
        return

    back = one_hot_columns(rel_ref, 1, buckets)

    def by_bucket(rg_ref):
        high, low = split_low(rg_ref[...])
        return (mm_nt(high, back) + mm_nt(low, back)).T

    def through_table(grad):
        high, low = split_low(grad)
        return mm_tn(high, table_ref[...]) + mm_tn(low, table_ref[...])

    pos_key = by_bucket(rg_key_ref)
    pos_query = by_bucket(rg_query_ref)
    sum_ref[:local, :] += through_table(pos_query)
    sum_ref[local : 2 * local, :] += through_table(pos_key)
    pos = jnp.concatenate([pos_key, pos_query], axis=1).astype(BF16)
    slots = joined_ref.shape[0]
    row_rows, pos_rows = 3 * local // slots, buckets // slots // 2
    for chunk in range(slots):
        slot = slot_of(jnp.bitwise_xor(chunk, place_ref[1]), (CORE, ACROSS_X, ACROSS_Y))
        at = 2 * chunk * pos_rows
        low = [norms_ref[chunk : chunk + 1, :], jnp.zeros((SMALL_ROWS - 1, 2 * local), F32)]
        low = jnp.concatenate(low, axis=0)
        pieces = [
            sum_ref[chunk * row_rows : (chunk + 1) * row_rows, :].astype(BF16),
            jnp.concatenate([pos[at : at + pos_rows], pos[at + pos_rows : at + 2 * pos_rows]], 1),
            jnp.concatenate([low, jnp.zeros_like(low)], axis=1).astype(BF16),
        ]
        joined_ref[slot] = jnp.concatenate(pieces, axis=0)
    joined_refs[0][...] = joined_ref[: slots // 2]
    joined_refs[1][...] = joined_ref[slots // 2 :]


def slot_of(relative, order):
    slot = 0
    for position, bit in enumerate(order):
        slot = slot + jnp.minimum(jnp.bitwise_and(relative, bit), 1) * (4 >> position)
    return slot


def backward_attention(
    block, blocks, place, context_grads, kept, weights, tables, hidden, w_rows, table, rel_rows,
    norms, before,
):
    width = hidden.shape[1]
    local = w_rows[0].shape[0]
    heads = local // HEAD_DIM
    buckets = table.shape[0]
    groups = SEQMAX // TILE
    last = block == blocks - 1
    parts = [Shape((rows, width), BF16) for rows in (TILE, 2 * TILE, TILE)]
    sums = [(local, OFFSETS), (local, OFFSETS), (3 * local, width)]
    joined_rows = 3 * local // CHUNKS + buckets // CHUNKS // 2 + SMALL_ROWS
    joined = Shape((CHUNKS // 2, joined_rows, width), BF16)
    scratch = [
        pltpu.VMEM((groups, TILE, local), BF16),
        pltpu.VMEM((SEQMAX, SEQMAX), BF16),
        pltpu.VMEM((SEQMAX, 3 * local), BF16),
        pltpu.VMEM((groups, TILE, width), BF16),
    ]
    if last:
        out_shape = parts + [joined] * 2
        scratch = scratch + [pltpu.VMEM(shape, F32) for shape in sums]
        scratch = scratch + [pltpu.VMEM((CHUNKS,) + joined.shape[1:], BF16)]
    else:
        out_shape = parts + [Shape(shape, F32) for shape in sums]
    scratch = scratch + [pltpu.VMEM((SEQMAX, local), BF16)] * 3
    scratch = scratch + [pltpu.VMEM((heads, SEQMAX, SEQMAX), BF16)]
    scratch = scratch + [pltpu.VMEM((local, OFFSETS), BF16)] * 2
    scratch = scratch + [pltpu.VMEM((SEQMAX, width), BF16)]
    scratch = scratch + [pltpu.VMEM((local, width), BF16)] * 3
    scratch = scratch + [pltpu.VMEM((buckets, width), BF16), pltpu.SemaphoreType.DMA((11,))]
    return kernel_call(
        functools.partial(backward_kernel, block, blocks),
        f"attention_backward_{block}",
        20_000_000_000,
        8_000_000,
        24,
        in_specs=[SCALARS]
        + [IN_VMEM] * groups
        + [IN_HBM] * 11
        + [IN_VMEM] * (2 + len(before)),
        out_specs=[IN_VMEM] * len(out_shape),
        out_shape=out_shape,
        scratch_shapes=scratch,
    )(
        place,
        *context_grads,
        *in_hbm(*kept, weights, *tables, hidden, *w_rows, table),
        rel_rows,
        norms,
        *before,
    )


def offset_rows(rel_buckets):
    plain = jnp.concatenate([rel_buckets[::-1], rel_buckets[:1]])
    back = plain.reshape(OFFSETS // TILE, TILE)[:, ::-1].reshape(OFFSETS)
    return jnp.stack([plain, back])


def layer_norm_parts(resid):
    centered = resid - jnp.mean(resid, axis=-1, keepdims=True)
    scale = lax.rsqrt(jnp.mean(centered * centered, axis=-1, keepdims=True) + NORM_EPS)
    return centered * scale, scale


def layer_norm_back(normal, scale, grad, gain):
    inner = grad * gain
    mean = jnp.mean(inner, axis=-1, keepdims=True)
    along = jnp.mean(inner * normal, axis=-1, keepdims=True)
    return scale * (inner - mean - normal * along)


def piece_kernel(place_ref, w_in_hbm, w_down_hbm, w_out_hbm, piece_ref, sems):
    replica = place_ref[1]
    width_rows, unit_rows = w_in_hbm.shape[0] // CHUNKS, w_down_hbm.shape[0] // CHUNKS
    rows = width_rows + unit_rows
    local = w_out_hbm.shape[0]
    at = pl.multiple_of(replica * width_rows, 16)
    down_at = pl.multiple_of(replica * unit_rows, 16)
    copies = start_copies(
        [
            (w_in_hbm.at[pl.ds(at, width_rows), :], piece_ref.at[pl.ds(0, width_rows), :]),
            (w_down_hbm.at[pl.ds(down_at, unit_rows), :], piece_ref.at[pl.ds(width_rows, unit_rows), :]),
        ],
        sems,
    )
    holds = replica * OUT_ROWS < local

    @pl.when(holds)
    def copy_out():
        out_at = pl.multiple_of(replica * OUT_ROWS, 16)
        wait_copies(
            start_copies(
                [(w_out_hbm.at[pl.ds(out_at, OUT_ROWS), :], piece_ref.at[pl.ds(rows, OUT_ROWS), :])],
                sems.at[pl.ds(2, 1)],
            )
        )

    @pl.when(jnp.logical_not(holds))
    def blank():
        piece_ref[rows:, :] = jnp.zeros((OUT_ROWS, piece_ref.shape[1]), BF16)

    wait_copies(copies)


def own_piece(place, w_in, w_down, w_out):
    width = w_down.shape[1]
    rows = w_in.shape[0] // CHUNKS + w_down.shape[0] // CHUNKS + OUT_ROWS
    return kernel_call(
        piece_kernel,
        "own_piece",
        0,
        700_000,
        4,
        in_specs=[SCALARS] + [IN_HBM] * 3,
        out_specs=IN_VMEM,
        out_shape=Shape((rows, width), BF16),
        scratch_shapes=[pltpu.SemaphoreType.DMA((3,))],
    )(place, *in_hbm(w_in, w_down, w_out))


def token_kernel(place_ref, *refs):
    groups = SEQMAX // TILE
    context_refs, refs = refs[:groups], refs[groups:]
    hidden_ref, out_grad_ref, norms_ref, w_in_ref, w_down_ref, w_out_ref = refs[:6]
    piece_refs, refs = refs[6 : 6 + len(GATHERED)], refs[6 + len(GATHERED) :]
    (
        output_ref, resid_ref, first_low_ref, act_out, pre_grad_out, ffn_grad_ref, attn_grad_ref,
        norm_grads_ref, *refs,
    ) = refs
    context_grad_refs, late_refs, refs = refs[:groups], refs[groups : groups + 2], refs[groups + 2 :]
    packed_vmem, out_vmem, slope_ref, sem, act_ref, pre_grad_ref, sems_out, *late_scratch = refs
    sent = []
    width = hidden_ref.shape[1]
    units = act_ref.shape[2]
    local = context_refs[0].shape[1]
    unit_rows, width_rows = units // CHUNKS, width // CHUNKS
    half = groups // 2

    out_copies, copies = gather_copies(piece_refs, packed_vmem, out_vmem, place_ref[1], sem)
    for copy in out_copies + copies:
        copy.start()
    for copy in out_copies:
        copy.wait()

    def packed(shift, first, rows):
        return packed_vmem[shift - 1, :, first : first + rows, :].reshape(CHUNKS * rows, width)

    def w_in(shift):
        return w_in_ref[...] if shift == 0 else packed(shift, 0, width_rows)

    def w_down(shift):
        return w_down_ref[...] if shift == 0 else packed(shift, width_rows, unit_rows)

    def w_out(shift):
        if shift == 0:
            return w_out_ref[...]
        return out_vmem[shift - 1].reshape(CHUNKS * OUT_ROWS, width)[:local]

    gain_one, bias_one = norms_ref[0:1, :], norms_ref[1:2, :]
    gain_two, bias_two = norms_ref[2:3, :], norms_ref[3:4, :]
    resid = hidden_ref[...].astype(F32)
    for g in range(groups):
        resid = resid + mm(context_refs[g][...], w_out(g)).astype(BF16).astype(F32)
    normal_one, scale_one = layer_norm_parts(resid)
    first_norm = normal_one * gain_one + bias_one
    first_low = first_norm.astype(BF16)
    first_low_ref[...] = first_low
    ffn_out = first_norm
    for g in range(groups):
        if g == 1:
            wait_copies(copies)
        pre_act = mm(first_low, w_in(g))
        area = 0.5 * (1.0 + lax.erf(pre_act * math.sqrt(0.5)))
        activated = (pre_act * area).astype(BF16)
        act_ref[g] = activated
        if g < half:
            sent += start_copies([(act_ref.at[g], act_out.at[g])], sems_out.at[pl.ds(g, 1)])
        density = jnp.exp(-0.5 * pre_act * pre_act) * (1.0 / math.sqrt(2.0 * math.pi))
        slope_ref[g] = area + pre_act * density
        ffn_out = ffn_out + mm(activated, w_down(g)).astype(BF16).astype(F32)
    normal_two, scale_two = layer_norm_parts(ffn_out)
    output_ref[...] = (normal_two * gain_two + bias_two).astype(BF16)
    out_grad = out_grad_ref[...].astype(F32)
    norm_grads_ref[...] = jnp.zeros_like(norm_grads_ref)
    norm_grads_ref[2:3, :] = jnp.sum(out_grad * normal_two, axis=0, keepdims=True)
    norm_grads_ref[3:4, :] = jnp.sum(out_grad, axis=0, keepdims=True)
    second_grad = layer_norm_back(normal_two, scale_two, out_grad, gain_two)
    ffn_grad = second_grad.astype(BF16)
    ffn_grad_ref[...] = ffn_grad
    first_grad = second_grad
    for g in range(groups):
        pre_grad = (mm_nt(ffn_grad, w_down(g)) * slope_ref[g]).astype(BF16)
        pre_grad_ref[g] = pre_grad
        if g < half:
            sent += start_copies(
                [(pre_grad_ref.at[g], pre_grad_out.at[g])], sems_out.at[pl.ds(half + g, 1)]
            )
        first_grad = first_grad + mm_nt(pre_grad, w_in(g))
    norm_grads_ref[0:1, :] = jnp.sum(first_grad * normal_one, axis=0, keepdims=True)
    norm_grads_ref[1:2, :] = jnp.sum(first_grad, axis=0, keepdims=True)
    resid_grad = layer_norm_back(normal_one, scale_one, first_grad, gain_one)
    resid_ref[...] = resid_grad
    attn_grad = resid_grad.astype(BF16)
    attn_grad_ref[...] = attn_grad
    for g in range(groups):
        context_grad_refs[g][...] = mm_nt(attn_grad, w_out(g)).astype(BF16)
    sorted_weight_grads(
        place_ref,
        [ref[...] for ref in context_refs[half:]],
        first_low,
        lambda j: act_ref[half + j],
        lambda j: pre_grad_ref[half + j],
        ffn_grad,
        attn_grad,
        late_refs,
        late_scratch,
    )
    wait_copies(sent)


def gather_copies(piece_refs, packed_vmem, out_vmem, replica, sem):
    out_copies, copies = [], []
    kept = packed_vmem.shape[2]
    for (group, relatives, firsts, rows), ref in zip(GATHERED, piece_refs):
        for i, relative in enumerate(relatives):
            chunk = jnp.bitwise_xor(replica, relative)
            first = firsts[i]
            main = min(first + rows, kept) - first
            copies.append(
                pltpu.make_async_copy(
                    ref.at[i, pl.ds(0, main), :],
                    packed_vmem.at[group - 1, chunk, pl.ds(first, main), :],
                    sem.at[len(copies)],
                )
            )
            if main < rows:
                out_copies.append(
                    pltpu.make_async_copy(
                        ref.at[i, pl.ds(main, rows - main), :],
                        out_vmem.at[group - 1, chunk],
                        sem.at[32 + len(out_copies)],
                    )
                )
    return out_copies, copies


def reached(axes):
    order = (0,)
    for bit in axes:
        order = order + tuple(relative + bit for relative in order)
    return order


def gathered_layout():
    layout = []
    for group, axes in ((1, (ACROSS_Y, ACROSS_X)), (2, (ACROSS_X, ACROSS_Y))):
        for core in (0, CORE):
            layout += [(group, (core, core + axes[0]), (0, 0), 2 * HALF_ROWS)]
            layout += [(group, (core + axes[1], core + sum(axes)), (0, 0), 2 * HALF_ROWS)]
    halves = ((0, (ACROSS_Y, ACROSS_X)), (HALF_ROWS, (ACROSS_X, ACROSS_Y)))
    for core in (0, CORE):
        both = tuple((core + r, first) for first, axes in halves for r in reached(axes))
        layout += [(3, tuple(r for r, first in both), tuple(first for r, first in both), HALF_ROWS)]
    return layout


ROW_ORDER = reached((ACROSS_Y, ACROSS_X, CORE))
HALF_ROWS = 112
GATHERED = gathered_layout()


def across(array, bit):
    return lax.ppermute(array, "dp", [(i, i ^ bit) for i in range(CHUNKS)])


def nearby(arrays):
    ways = (ACROSS_Y, ACROSS_X, ACROSS_Y + ACROSS_X)
    return [arrays[0]] + [across(array, way) for array, way in zip(arrays[1:], ways)]


def together(*values):
    return lax.optimization_barrier(values)


def token_layer(place, contexts, hidden, out_grad, norms, w_rows, pieces):
    tokens, width = hidden.shape
    local = contexts[0].shape[1]
    units = w_rows[0].shape[1]
    groups = len(contexts)
    rows = width // CHUNKS + units // CHUNKS + OUT_ROWS
    return kernel_call(
        token_kernel,
        "token_layer",
        15_000_000_000,
        18_000_000,
        40,
        in_specs=[SCALARS]
        + [IN_VMEM] * (groups + 6)
        + [ANYWHERE] * len(pieces),
        out_specs=[IN_VMEM] * 3 + [IN_HBM] * 2 + [IN_VMEM] * (3 + groups) + [IN_HBM] * 2,
        out_shape=[
            Shape((tokens, width), BF16),
            Shape((tokens, width), F32),
            Shape((tokens, width), BF16),
            hbm_shape((groups // 2, tokens, units), BF16),
            hbm_shape((groups // 2, tokens, units), BF16),
            Shape((tokens, width), BF16),
            Shape((tokens, width), BF16),
            Shape((8, width), F32),
        ]
        + [Shape((tokens, local), BF16)] * groups
        + [hbm_shape((2, CHUNKS // 2, rows, width), BF16)] * 2,
        scratch_shapes=[
            pltpu.VMEM((groups - 1, CHUNKS, rows - OUT_ROWS, width), BF16),
            pltpu.VMEM((groups - 1, CHUNKS, OUT_ROWS, width), BF16),
            pltpu.VMEM((groups, tokens, units), F32),
            pltpu.SemaphoreType.DMA((56,)),
            pltpu.VMEM((groups, tokens, units), BF16),
            pltpu.VMEM((groups, tokens, units), BF16),
            pltpu.SemaphoreType.DMA((groups,)),
        ]
        + weight_grad_scratch(width, units, rows),
    )(place, *contexts, hidden, out_grad, norms, *w_rows, *pieces)


def sorted_weight_grads(
    place_ref, contexts, first_low, act_of, pre_grad_of, ffn_grad, attn_grad, out_refs, scratch
):
    in_ref, down_ref, last_ref, sorted_ref, sems = scratch
    local = contexts[0].shape[1]
    width_rows = in_ref.shape[0] // CHUNKS
    unit_rows = down_ref.shape[0] // CHUNKS
    rows = width_rows + unit_rows
    last_ref[local:, :] = jnp.zeros((last_ref.shape[0] - local, last_ref.shape[1]), BF16)
    copies = []
    for j, axes in enumerate(PART_AXES):
        last_ref[:local, :] = mm_tn(contexts[j], attn_grad).astype(BF16)
        in_ref[...] = mm_tn(first_low, pre_grad_of(j)).astype(BF16)
        down_ref[...] = mm_tn(act_of(j), ffn_grad).astype(BF16)
        for side, core in ((1, CORE), (0, 0)):
            for slot, relative in enumerate(reached(axes[::-1])):
                chunk = jnp.bitwise_xor(relative + core, place_ref[1])
                at = pl.multiple_of(chunk * width_rows, 16)
                sorted_ref[side, j, slot, :width_rows] = in_ref[pl.ds(at, width_rows), :]
                at = pl.multiple_of(chunk * unit_rows, 16)
                sorted_ref[side, j, slot, width_rows:rows] = down_ref[pl.ds(at, unit_rows), :]
                at = pl.multiple_of(chunk * OUT_ROWS, 16)
                sorted_ref[side, j, slot, rows:] = last_ref[pl.ds(at, OUT_ROWS), :]
            copies += start_copies(
                [(sorted_ref.at[side, j], out_refs[side].at[j])], sems.at[pl.ds(2 * side + j, 1)]
            )
    wait_copies(copies)


def weight_grad_scratch(width, units, rows):
    return [
        pltpu.VMEM((width, width), BF16),
        pltpu.VMEM((units, width), BF16),
        pltpu.VMEM((CHUNKS * OUT_ROWS, width), BF16),
        pltpu.VMEM((2, 2, CHUNKS // 2, rows, width), BF16),
        pltpu.SemaphoreType.DMA((4,)),
    ]


def weight_grad_kernel(place_ref, *refs):
    context_refs, refs = refs[:2], refs[2:]
    first_low_ref, act_hbm, pre_grad_hbm, ffn_grad_ref, attn_grad_ref, *out_refs = refs[:7]
    scratch, (act_ref, pre_grad_ref, sems_in) = refs[7:12], refs[12:]
    arriving = start_copies(
        [
            (source.at[j], target.at[j])
            for j in range(2)
            for source, target in ((pre_grad_hbm, pre_grad_ref), (act_hbm, act_ref))
        ],
        sems_in,
    )

    def act_of(j):
        arriving[2 * j + 1].wait()
        return act_ref[j]

    def pre_grad_of(j):
        arriving[2 * j].wait()
        return pre_grad_ref[j]

    sorted_weight_grads(
        place_ref,
        [ref[...] for ref in context_refs],
        first_low_ref[...],
        act_of,
        pre_grad_of,
        ffn_grad_ref[...],
        attn_grad_ref[...],
        out_refs,
        scratch,
    )


def weight_grads(place, contexts, first_low, act, pre_grad, ffn_grad, attn_grad):
    tokens, units = act.shape[1:]
    width = first_low.shape[1]
    rows = width // CHUNKS + units // CHUNKS + OUT_ROWS
    return kernel_call(
        weight_grad_kernel,
        "weight_grads",
        4_000_000_000,
        7_000_000,
        15,
        in_specs=[SCALARS] + [IN_VMEM] * 3 + [IN_HBM] * 2 + [IN_VMEM] * 2,
        out_specs=[IN_HBM] * 2,
        out_shape=[hbm_shape((2, CHUNKS // 2, rows, width), BF16)] * 2,
        scratch_shapes=weight_grad_scratch(width, units, rows)
        + [
            pltpu.VMEM((2, tokens, units), BF16),
            pltpu.VMEM((2, tokens, units), BF16),
            pltpu.SemaphoreType.DMA((4,)),
        ],
    )(place, *contexts[:2], first_low, *in_hbm(act, pre_grad), ffn_grad, attn_grad)


def add(left, right):
    return (left.astype(F32) + right.astype(F32)).astype(BF16)


def total_of(arrays):
    return sum(array.astype(F32) for array in arrays).astype(BF16)


def reorder_kernel(place_ref, *refs):
    out_ref = refs[-1]
    groups = out_ref.shape[1]
    blocks = out_ref.shape[0]
    per = len(refs[:-1]) // groups
    for shift in range(groups):
        origin = jnp.bitwise_xor(place_ref[0], shift)
        for b in range(blocks):
            if per == 1:
                out_ref[b, origin] = refs[shift][b * TILE : (b + 1) * TILE, :]
            else:
                out_ref[b, origin] = refs[b * groups + shift][...]


def reorder(place, pieces, blocks):
    width = pieces[0].shape[1]
    groups = SEQMAX // TILE
    out = kernel_call(
        reorder_kernel,
        "reorder",
        0,
        3_000_000,
        8,
        in_specs=[SCALARS] + [IN_VMEM] * len(pieces),
        out_specs=IN_VMEM,
        out_shape=Shape((blocks, groups, TILE, width), BF16),
    )(place, *pieces)
    return out.reshape(blocks * SEQMAX, width)


def unpack_kernel(place_ref, *refs):
    piece_refs, refs = refs[:CHUNKS], refs[CHUNKS:]
    grad_in_ref, grad_down_ref, grad_out_ref, q_ref, k_ref, v_ref, table_ref = refs[:7]
    norm_refs, all_ref, norms_ref = refs[7:11], *refs[11:]
    local = q_ref.shape[0]
    width_rows = grad_in_ref.shape[0] // CHUNKS
    unit_rows = grad_down_ref.shape[0] // CHUNKS
    table_rows = table_ref.shape[0] // CHUNKS
    row_rows = all_ref.shape[0] // CHUNKS
    columns = norms_ref.shape[1]
    out_at = width_rows + unit_rows
    table_at = out_at + OUT_ROWS
    norm_at = table_at + table_rows
    rows_at = norm_at + SMALL_ROWS
    for relative, ref in zip(ROW_ORDER, piece_refs):
        chunk = jnp.bitwise_xor(place_ref[1], relative)
        at = pl.multiple_of(chunk * width_rows, 8)
        grad_in_ref[pl.ds(at, width_rows), :] = ref[:width_rows, :].astype(F32)
        at = pl.multiple_of(chunk * unit_rows, 8)
        grad_down_ref[pl.ds(at, unit_rows), :] = ref[width_rows:out_at, :].astype(F32)
        at = pl.multiple_of(chunk * table_rows, 8)
        table_ref[pl.ds(at, table_rows), :] = ref[table_at:norm_at, :].astype(F32)
        norms_ref[pl.ds(chunk, 1), :] = ref[norm_at:rows_at, :columns].astype(F32)[:1]
        at = pl.multiple_of(chunk * row_rows, 8)
        all_ref[pl.ds(at, row_rows), :] = ref[rows_at:, :].astype(F32)

        @pl.when(chunk * OUT_ROWS < grad_out_ref.shape[0])
        def out_rows(chunk=chunk, ref=ref):
            at = pl.multiple_of(chunk * OUT_ROWS, 8)
            grad_out_ref[pl.ds(at, OUT_ROWS), :] = ref[out_at:table_at, :].astype(F32)

    for i, ref in enumerate((q_ref, k_ref, v_ref)):
        ref[...] = all_ref[i * local : (i + 1) * local, :]
    for i, ref in enumerate(norm_refs):
        ref[:columns] = norms_ref[2 * i, :]
        ref[columns:] = norms_ref[2 * i + 1, :]


def unpack(place, pieces, width, units, local, buckets):
    return kernel_call(
        unpack_kernel,
        "unpack",
        0,
        14_000_000,
        10,
        in_specs=[SCALARS] + [IN_VMEM] * CHUNKS,
        out_specs=[IN_VMEM] * 11,
        out_shape=[Shape((width, width), F32), Shape((units, width), F32)]
        + [Shape((local, width), F32)] * 4
        + [Shape((buckets, width), F32)]
        + [Shape((width,), F32)] * 4,
        scratch_shapes=[
            pltpu.VMEM((3 * local, width), F32),
            pltpu.VMEM((CHUNKS, 4 * width // CHUNKS), F32),
        ],
    )(place, *pieces)


def send(array, bits):
    return lax.ppermute(array, "tensor", [(i, i ^ bits) for i in range(SEQMAX // TILE)])


def exchange(pieces):
    return [pieces[0]] + [send(piece, r) for r, piece in enumerate(pieces) if r > 0]


def second_exchange(context, got):
    near = send(jnp.concatenate([context[1], got[1:]], 0), 1)
    return [context[0][0], near[0], got[0], near[1]]


def spread(array):
    near, far = send(array, 1), send(array, 2)
    return [array, near, far, send(far, 1)]


def shards(
    n_dp,
    n_tensor,
    hidden,
    out_grad,
    w_query,
    w_key,
    w_value,
    w_out,
    w_in,
    w_down,
    bucket_table,
    gain_one,
    bias_one,
    gain_two,
    bias_two,
    rel_buckets,
    group_counts,
    key_mask,
):
    tokens, width = hidden.shape
    local = w_query.shape[1]
    units = w_in.shape[1]
    buckets = bucket_table.shape[0]
    blocks = tokens // SEQMAX
    mine = tokens // n_tensor
    by_axis = n_dp == CHUNKS
    me = lax.axis_index("tensor")
    replica = lax.axis_index("dp") if by_axis else jnp.int32(0)
    place = jnp.stack([me, replica]).astype(jnp.int32)
    rel_rows = offset_rows(rel_buckets)
    width_rows, unit_rows = width // CHUNKS, units // CHUNKS
    padded = jnp.pad(w_out, ((0, CHUNKS * OUT_ROWS - local), (0, 0)))

    w_rows = (w_query.T, w_key.T, w_value.T)

    def my_rows(array):
        array = array.reshape(blocks, n_tensor, TILE, width)
        return lax.dynamic_index_in_dim(array, me, 1, keepdims=False).reshape(mine, width)

    def forward(block, context):
        weights, *context = forward_attention(
            block, place, group_counts, tables, rows, key_mask, context
        )
        return weights, context

    if by_axis:
        piece = own_piece(place, w_in, w_down, w_out)
        near, far = send(piece, 1), send(piece, 2)
        (*tables, q, k, v), saved = prepare(*w_rows, bucket_table, rel_rows, hidden)
        rows = (q, k, v)
        my_hidden, my_out_grad = my_rows(hidden), my_rows(out_grad)
        near, far, tables, rows, saved, my_hidden, my_out_grad = together(
            near, far, tables, rows, saved, my_hidden, my_out_grad
        )
        last = send(far, 1)
        near_y, far_x = across(near[None], ACROSS_Y), across(far[None], ACROSS_X)
        kept_0, context = forward(0, [])
        near, far, near_y, far_x, last, kept_0, context, tables, rows = together(
            near, far, near_y, far_x, last, kept_0, context, tables, rows
        )
        near = jnp.concatenate([near[None], near_y], 0)
        far = jnp.concatenate([far[None], far_x], 0)
        near_x, far_y = across(near, ACROSS_X), across(far, ACROSS_Y)
        top, low = last[None, :HALF_ROWS], last[None, HALF_ROWS:]
        top_y, low_x = across(top, ACROSS_Y), across(low, ACROSS_X)
        kept_1, context = forward(1, context)
        got = send(context[2], 2)
        near, near_x, far, far_y, top, top_y, low, low_x, context, got, kept_0, kept_1 = together(
            near, near_x, far, far_y, top, top_y, low, low_x, context, got, kept_0, kept_1
        )
        contexts = second_exchange(context, got)
        top = jnp.concatenate([top, top_y], 0)
        low = jnp.concatenate([low, low_x], 0)
        top_x, low_y = across(top, ACROSS_X), across(low, ACROSS_Y)
        cores = [across(near, CORE), across(near_x, CORE)]
        near, near_x, cores, far, far_y, top, top_x, low, low_y, contexts, kept_0, kept_1 = (
            together(
                near, near_x, cores, far, far_y, top, top_x, low, low_y, contexts, kept_0, kept_1
            )
        )
        both = jnp.concatenate([top, top_x, low, low_y], 0)
        gathered = [near, near_x, *cores]
        gathered += [far, far_y, across(far, CORE), across(far_y, CORE)]
        gathered += [both, across(both, CORE)]
    else:
        (*tables, q, k, v), saved = prepare(*w_rows, bucket_table, rel_rows, hidden)
        rows = (q, k, v)
        stacked = jnp.concatenate(
            [
                w_in.reshape(CHUNKS, width_rows, width),
                w_down.reshape(CHUNKS, unit_rows, width),
                padded.reshape(CHUNKS, OUT_ROWS, width),
            ],
            1,
        )
        sent = spread(stacked)
        gathered = [
            jnp.stack(
                [
                    sent[group][chunk, at : at + rows]
                    for chunk, at in zip(chunks, first)
                ]
            )
            for group, chunks, first, rows in GATHERED
        ]
        kept_0, context = forward(0, [])
        kept_1, context = forward(1, context)
        contexts = second_exchange(context, send(context[2], 2))
        my_hidden, my_out_grad = my_rows(hidden), my_rows(out_grad)
    *tables, q, k, v = saved
    norms = jnp.stack([gain_one, bias_one, gain_two, bias_two])
    (
        output, resid_grad, first_low, act, pre_grad, ffn_grad, attn_grad, norm_grads, *back,
        late_keep, late_give,
    ) = token_layer(
        place, contexts, my_hidden, my_out_grad, norms, (w_in, w_down, w_out), gathered
    )
    norm_grads = norm_grads[:4].reshape(CHUNKS, 4 * width // CHUNKS)

    def backward(block, kept, before):
        own, near, far, *before = backward_attention(
            block, blocks, place, back, (q, k, v), kept, tables, hidden, w_rows, bucket_table, rel_rows,
            norm_grads, before,
        )
        return [own, near, far], before

    keep_1, give_1 = late_keep, late_give
    back = exchange(back)
    core_1 = across(give_1, CORE) if by_axis else give_1
    keep_0, give_0 = weight_grads(
        place, contexts, first_low, act, pre_grad, ffn_grad, attn_grad
    )

    def first_sums(keep, got):
        return [add(keep[j, 2:], got[j, 2:]) for j in range(2)]

    sums_1 = first_sums(keep_1, core_1) if by_axis else []
    (
        back, core_1, sums_1, keep_0, give_0, keep_1, output, resid_grad, norm_grads, kept_0,
        kept_1, tables, place,
    ) = together(
        back, core_1, sums_1, keep_0, give_0, keep_1, output, resid_grad, norm_grads, kept_0,
        kept_1, tables, place,
    )
    back = [piece.reshape(blocks, TILE, local) for piece in back]

    def first_stage(sums):
        return [across(part, axes[0]) for part, axes in zip(sums, PART_AXES)]

    def second_stage(terms):
        kept, got = [], []
        for j, axes in enumerate(PART_AXES):
            given = [total_of([a[j, 1:2], b[j, 1:2], c[j][1:2]]) for a, b, c in terms]
            kept.append([[a[j, 0], b[j, 0], c[j][0]] for a, b, c in terms])
            got.append(across(jnp.concatenate(given, 0), axes[1]))
        return kept, got

    stage_1, core_0 = [], give_0
    if by_axis:
        stage_1 = first_stage(sums_1)
        core_0 = across(give_0, CORE)
    out_near, out_far = send(output, 1), send(output, 2)
    parts, before = backward(0, kept_0, ())
    (
        parts, before, stage_1, core_0, core_1, keep_0, keep_1, out_near, out_far, output,
        resid_grad, norm_grads, kept_1, tables, place, back,
    ) = together(
        parts, before, stage_1, core_0, core_1, keep_0, keep_1, out_near, out_far, output,
        resid_grad, norm_grads, kept_1, tables, place, back,
    )
    stage_0 = first_stage(first_sums(keep_0, core_0)) if by_axis else []
    parts = [parts[0], send(parts[1], 1), parts[2]]
    out_last = send(out_far, 1)
    parts_1, before = backward(1, kept_1, before)
    (
        parts, parts_1, before, stage_0, stage_1, core_0, core_1, keep_0, keep_1, out_last,
        resid_grad,
    ) = together(
        parts, parts_1, before, stage_0, stage_1, core_0, core_1, keep_0, keep_1, out_last,
        resid_grad,
    )
    def total(block, pieces):
        wide = resid_grad[block * TILE : (block + 1) * TILE]
        for piece in pieces:
            wide = wide + piece.astype(F32)
        return wide.astype(BF16)

    keep, give = before
    thirds, sums = [], keep
    if not by_axis:
        joined = lax.psum(jnp.concatenate([keep, give], 0).astype(F32), "dp").astype(BF16)
    if by_axis:
        thirds = second_stage(((keep_0, core_0, stage_0), (keep_1, core_1, stage_1)))
        sums = add(keep, across(give, CORE))
    far_0 = send(add(parts[2], parts[1][TILE:]), 2)
    near_1 = send(parts_1[1], 1)
    grad_0 = total(0, [parts[0], parts[1][:TILE], far_0])
    sum_1 = add(parts_1[2], near_1[TILE:])
    grad_0, sum_1, parts_1, near_1, thirds, sums, resid_grad, out_last = together(
        grad_0, sum_1, parts_1, near_1, thirds, sums, resid_grad, out_last
    )

    def joint(arrays, way):
        rows = [array.shape[0] for array in arrays]
        got = send(jnp.concatenate(arrays, 0), way)
        return [got[sum(rows[:i]) : sum(rows[: i + 1])] for i in range(len(rows))]

    output = reorder(place, [output, out_near, out_far, out_last], blocks)
    shard, near_0 = [], [grad_0]
    if by_axis:
        for half in range(2):
            for j in range(2):
                shard.append(total_of([*thirds[0][j][half], thirds[1][j][half]]))
        near_0 = near_0 + [shard[3]]
        joined = total_of(nearby([sums[i : i + 1] for i in range(CHUNKS // 2)]))
    near_0 = joint(near_0, 1)
    far_0, far_1 = joint([grad_0, sum_1], 2)
    row_rows, pos_rows = 3 * local // CHUNKS, buckets // CHUNKS // 2
    slots = joined.shape[0]
    row_grads = joined[:, :row_rows]
    pos = joined[:, row_rows : row_rows + pos_rows]
    pos = jnp.concatenate([pos[:, :, : 2 * local], pos[:, :, 2 * local :]], 1)
    w_table = jnp.concatenate([w_rows[1], w_rows[0]], 0)
    table_part = mm(pos.reshape(slots * 2 * pos_rows, 2 * local), w_table)
    table_part = table_part.astype(BF16).reshape(slots, 2 * pos_rows, width)
    small = jnp.concatenate([table_part, joined[:, row_rows + pos_rows :]], 1)
    small_rows = small.shape[1]
    small = small.reshape(slots * small_rows, width)
    grad_0, near_0, far_0, far_1, near_1, parts_1, resid_grad, output, shard, small, row_grads = (
        together(
            grad_0, near_0, far_0, far_1, near_1, parts_1, resid_grad, output, shard, small,
            row_grads,
        )
    )
    grad_1 = total(1, [parts_1[0], near_1[:TILE], far_1])
    small = [small, None, None, send(small, 3)]
    shard_far = []
    if by_axis:
        *shard_1, small[1] = joint([shard[1], small[0]], 1)
        *shard_2, small[2] = joint([add(shard[2], near_0[1]), small[0]], 2)
        shard_far = shard_1 + shard_2
    else:
        small[1], small[2] = send(small[0], 1), send(small[0], 2)
    grad_0, near_0, far_0, grad_1, row_grads, small, shard, shard_far = together(
        grad_0, near_0, far_0, grad_1, row_grads, small, shard, shard_far
    )
    near_1, last_0 = joint([grad_1, far_0], 1)
    far_1 = send(grad_1, 2)
    small = [part.astype(F32) for part in small]
    small = ((small[0] + small[1]) + (small[2] + small[3])).astype(BF16)
    if by_axis:
        shard = total_of([shard[0], *shard_far])
        pieces = nearby([jnp.concatenate([shard, small, row_grads[0]], 0)] * 4)
        grad_0, near_0, far_0, last_0, grad_1, near_1, far_1, pieces = together(
            grad_0, near_0, far_0, last_0, grad_1, near_1, far_1, pieces
        )
        pieces = pieces + [across(piece, CORE) for piece in pieces]
    else:
        natural = []
        for keep, give in ((keep_0, give_0), (keep_1, give_1)):
            for j, axes in enumerate(PART_AXES):
                chunks = reached(axes[::-1] + (CORE,))
                both = jnp.concatenate([keep[j], give[j]], 0)
                natural.append(jnp.stack([both[chunks.index(c)] for c in range(CHUNKS)]))
        shard = jnp.stack(exchange(natural)).astype(F32)
        shard = lax.psum(sum(shard[r] for r in range(n_tensor)), "dp").astype(BF16)
        small = small.reshape(slots, small_rows, width)
        pieces = [
            jnp.concatenate([shard[chunk], small[slot], row_grads[slot]], 0)
            for slot, chunk in enumerate(ROW_ORDER)
        ]
    last_1 = send(far_1, 1)
    if by_axis:
        last_1, pieces = together(last_1, pieces)
    grad_hidden = reorder(
        place, [grad_0, near_0[0], far_0, last_0, grad_1, near_1, far_1, last_1], blocks
    )
    (
        grad_in, grad_down, grad_out, grad_query, grad_key, grad_value, grad_table, *norm_grads,
    ) = unpack(place, pieces, width, units, local, buckets)
    return (
        output,
        grad_hidden,
        grad_query.T,
        grad_key.T,
        grad_value.T,
        grad_out,
        grad_in,
        grad_down,
        grad_table,
        *norm_grads,
    )


def solution(mesh):
    in_specs = (
        P("dp", None),
        P("dp", None),
        P(None, "tensor"),
        P(None, "tensor"),
        P(None, "tensor"),
        P("tensor", None),
        P(None, "tensor"),
        P("tensor", None),
        P(),
        P(),
        P(),
        P(),
        P(),
        P(),
        P("dp", None),
        P("dp"),
    )
    out_specs = (
        P("dp", None),
        P("dp", None),
        P(None, "tensor"),
        P(None, "tensor"),
        P(None, "tensor"),
        P("tensor", None),
        P(None, "tensor"),
        P("tensor", None),
        P(),
        P(),
        P(),
        P(),
        P(),
    )
    body = functools.partial(shards, mesh.shape["dp"], mesh.shape["tensor"])
    return jax.shard_map(body, mesh=mesh, in_specs=in_specs, out_specs=out_specs, check_vma=False)
```

```python
import functools
import math

import jax
import jax.numpy as jnp
from jax import lax
from jax.experimental import pallas as pl
from jax.experimental.pallas import tpu as pltpu
from jax.sharding import PartitionSpec as P

NORM_EPS = 1e-07
HEAD_DIM = 64
SEQMAX = 512
TILE = 128
WINDOW = SEQMAX + TILE
OFFSETS = 2 * SEQMAX
NEGATIVE = -1e30
CHUNKS = 8
CORE, ACROSS_X, ACROSS_Y = 1, 2, 4
OUT_ROWS = 32
SMALL_ROWS = 16
F32 = jnp.float32
BF16 = jnp.bfloat16


def score_factor():
    return 1.0 / math.sqrt(3.0 * HEAD_DIM)


def mm(left, right):
    return jnp.dot(left, right, preferred_element_type=F32)


def mm_nt(left, right):
    return lax.dot_general(left, right, (((1,), (1,)), ((), ())), preferred_element_type=F32)


def mm_tn(left, right):
    return lax.dot_general(left, right, (((0,), (0,)), ((), ())), preferred_element_type=F32)


def starts_of(places, counts_ref):
    long_end = SEQMAX * counts_ref[0, 0]
    mid_end = long_end + SEQMAX // 2 * counts_ref[0, 1]
    in_long = places < long_end
    in_mid = places < mid_end
    anchor = jnp.where(in_long, 0, jnp.where(in_mid, long_end, mid_end))
    shift = jnp.where(in_long, 9, jnp.where(in_mid, 8, 7))
    return anchor + lax.shift_left(lax.shift_right_logical(places - anchor, shift), shift)


def tile_iotas():
    rows = lax.broadcasted_iota(jnp.int32, (TILE, TILE), 0)
    lanes = lax.broadcasted_iota(jnp.int32, (TILE, TILE), 1)
    return rows, lanes


def lane_tiles(wide):
    return [wide[:, c : c + TILE] for c in range(0, wide.shape[1], TILE)]


def skew(wide):
    rows, lanes = tile_iotas()
    keep = lanes <= rows
    turned = [pltpu.roll(part, 1, 1, stride=1, stride_axis=0) for part in lane_tiles(wide)]
    return jnp.concatenate(
        [jnp.where(keep, turned[c], turned[c + 1]) for c in range(len(turned) - 1)], axis=1
    )


def unskew(flipped):
    rows, lanes = tile_iotas()
    late = lanes > rows
    turned = [pltpu.roll(part, 1, 1, stride=1, stride_axis=0) for part in lane_tiles(flipped)]
    zero = jnp.zeros((TILE, TILE), F32)
    turned = [zero] + turned + [zero]
    return jnp.concatenate(
        [jnp.where(late, turned[c], turned[c + 1]) for c in range(len(turned) - 1)], axis=1
    )


def window_of(tile_at):
    low = SEQMAX - TILE - tile_at
    return slice(low, low + WINDOW)


def one_hot_columns(rel_ref, row, buckets):
    ids = lax.broadcasted_iota(jnp.int32, (buckets, OFFSETS), 0)
    return (ids == rel_ref[row : row + 1, :]).astype(BF16)


def split_low(wide):
    high = wide.astype(BF16)
    return high, (wide - high.astype(F32)).astype(BF16)


SCALARS = pl.BlockSpec(memory_space=pltpu.SMEM)
ANYWHERE = pl.BlockSpec(memory_space=pl.ANY)
IN_HBM = pl.BlockSpec(memory_space=pltpu.HBM)
IN_VMEM = pl.BlockSpec(memory_space=pltpu.VMEM)
Shape = jax.ShapeDtypeStruct


def in_hbm(*arrays):
    return [pltpu.with_memory_space_constraint(array, pltpu.HBM) for array in arrays]


def hbm_shape(shape, kind):
    return pltpu.HBM(shape, kind)


def kernel_call(kernel, name, flops, moved, vmem, **rest):
    return pl.pallas_call(
        kernel,
        compiler_params=pltpu.CompilerParams(vmem_limit_bytes=vmem * 2**20),
        cost_estimate=pl.CostEstimate(flops=flops, bytes_accessed=moved, transcendentals=0),
        name=name,
        **rest,
    )


PART_AXES = ((ACROSS_Y, ACROSS_X), (ACROSS_X, ACROSS_Y))


def start_copies(pairs, sems):
    copies = [
        pltpu.make_async_copy(source, target, sems.at[i]) for i, (source, target) in enumerate(pairs)
    ]
    for copy in copies:
        copy.start()
    return copies


def wait_copies(copies):
    for copy in copies:
        copy.wait()


def prepare_kernel(
    wq_ref, wk_ref, wv_ref, table_ref, rel_ref, hidden_ref, pk_ref, pq_ref, q_ref, k_ref, v_ref,
    pk_back_out, pq_back_out, q_out, k_out, v_out, pk_back, pq_back, sems,
):
    table = table_ref[...]
    buckets = table.shape[0]
    pos_key = mm_nt(wk_ref[...], table).astype(BF16)
    pos_query = mm_nt(wq_ref[...], table).astype(BF16)
    plain = one_hot_columns(rel_ref, 0, buckets)
    pk_ref[...] = mm(pos_key, plain).astype(BF16)
    pq_ref[...] = mm(pos_query, plain).astype(BF16)
    back = one_hot_columns(rel_ref, 1, buckets)
    pk_back[...] = mm(pos_key, back).astype(BF16)
    pq_back[...] = mm(pos_query, back).astype(BF16)
    copies = start_copies([(pk_back, pk_back_out), (pq_back, pq_back_out)], sems)
    hidden = hidden_ref[...]
    for i, (ref, w_ref, out) in enumerate(
        ((q_ref, wq_ref, q_out), (k_ref, wk_ref, k_out), (v_ref, wv_ref, v_out))
    ):
        ref[...] = mm_nt(hidden, w_ref[...]).astype(BF16)
        copies += start_copies([(ref, out)], sems.at[pl.ds(2 + i, 1)])
    wait_copies(copies)


def prepare(w_query, w_key, w_value, table, rel_rows, hidden):
    local = w_query.shape[0]
    tokens = hidden.shape[0]
    table_kind = ((local, OFFSETS), BF16)
    row_kind = ((tokens, local), BF16)
    out = kernel_call(
        prepare_kernel,
        "prepare",
        4_000_000_000,
        6_000_000,
        10,
        in_specs=[IN_VMEM] * 6,
        out_specs=[IN_VMEM] * 5 + [IN_HBM] * 5,
        out_shape=[Shape(*table_kind)] * 2
        + [Shape(*row_kind)] * 3
        + [hbm_shape(*table_kind)] * 2
        + [hbm_shape(*row_kind)] * 3,
        scratch_shapes=[pltpu.VMEM(*table_kind)] * 2 + [pltpu.SemaphoreType.DMA((5,))],
    )(w_query, w_key, w_value, table, rel_rows, hidden)
    return out[:5], out[5:]


def forward_kernel(
    block, place_ref, counts_ref, pk_ref, pq_ref, q_ref, k_ref, v_ref, mask_ref, *rest
):
    before, rest = rest[: 3 if block else 0], rest[3 if block else 0 :]
    weights_out, context_refs, rest = rest[0], rest[1:4], rest[4:]
    context_ref, bias_ref, rel_score_ref, weights_ref, sems_out = rest
    heads = q_ref.shape[1] // HEAD_DIM
    first = block * SEQMAX
    here = slice(first, first + SEQMAX)
    column = starts_of(lax.broadcasted_iota(jnp.int32, (SEQMAX, 1), 0) + first, counts_ref)
    row = starts_of(lax.broadcasted_iota(jnp.int32, (1, SEQMAX), 1) + first, counts_ref)
    row = jnp.where(mask_ref[block] == 1, row, -1)
    bias_ref[...] = jnp.where(column == row, 0.0, NEGATIVE)
    copies = []
    for head in range(heads):
        part = slice(head * HEAD_DIM, (head + 1) * HEAD_DIM)
        queries = q_ref[here, part]
        keys = k_ref[here, part]
        values = v_ref[here, part]
        for at in range(0, SEQMAX, TILE):
            rel = mm(keys[at : at + TILE], pq_ref[part, window_of(at)])
            rel_score_ref[at : at + TILE, :] = skew(rel)
        for at in range(0, SEQMAX, TILE):
            rows = slice(at, at + TILE)
            raw = mm_nt(queries[rows], keys)
            raw = raw + skew(mm(queries[rows], pk_ref[part, window_of(at)]))
            raw = raw + rel_score_ref[:, rows].T
            scaled = raw * score_factor() + bias_ref[rows, :]
            top = jnp.max(scaled, axis=-1, keepdims=True)
            exponent = jnp.exp(scaled - top)
            total = jnp.sum(exponent, axis=-1, keepdims=True)
            weights = (exponent * (1.0 / total)).astype(BF16)
            weights_ref[head, rows, :] = weights
            relative = jnp.bitwise_xor(at // TILE, place_ref[0])
            context_ref[relative, :, part] = mm(weights, values).astype(BF16)
        copies += start_copies(
            [(weights_ref.at[head], weights_out.at[head])], sems_out.at[pl.ds(head, 1)]
        )
    at = 0
    for n, ref in enumerate(context_refs):
        for r in range(ref.shape[0]):
            for b in range(block):
                ref[r, b * TILE : (b + 1) * TILE] = before[n][r, b * TILE : (b + 1) * TILE]
            ref[r, block * TILE : (block + 1) * TILE] = context_ref[at]
            at += 1
    wait_copies(copies)


def forward_attention(block, place, counts, tables, rows, key_mask, context):
    tokens, local = rows[0].shape
    heads = local // HEAD_DIM
    blocks = tokens // SEQMAX
    groups = SEQMAX // TILE
    return kernel_call(
        functools.partial(forward_kernel, block),
        f"attention_forward_{block}",
        10_000_000_000,
        5_000_000,
        12,
        in_specs=[SCALARS] * 2 + [IN_VMEM] * (6 + len(context)),
        out_specs=[IN_HBM] + [IN_VMEM] * 3,
        out_shape=[hbm_shape((heads, SEQMAX, SEQMAX), BF16)]
        + [Shape((n, (block + 1) * TILE, local), BF16) for n in (1, 1, 2)],
        scratch_shapes=[pltpu.VMEM((groups, TILE, local), BF16)]
        + [pltpu.VMEM((SEQMAX, SEQMAX), F32)] * 2
        + [pltpu.VMEM((heads, SEQMAX, SEQMAX), BF16), pltpu.SemaphoreType.DMA((heads,))],
    )(place, counts, *tables, *rows, key_mask.reshape(blocks, 1, SEQMAX), *context)


def backward_kernel(block, blocks, place_ref, *refs):
    groups = SEQMAX // TILE
    cg_refs, refs = refs[:groups], refs[groups:]
    q_hbm, k_hbm, v_hbm, weights_hbm, pk_hbm, pq_hbm, hidden_hbm = refs[:7]
    w_hbms, table_hbm, rel_ref, norms_ref = refs[7:10], *refs[10:13]
    refs = refs[13:]
    before, refs = (refs[:3], refs[3:]) if block > 0 else (None, refs)
    q_ref, k_ref, v_ref, weights_ref, pk_back_ref, pq_back_ref, hidden_ref = refs[-12:-5]
    wq_ref, wk_ref, wv_ref, table_ref, sems = refs[-5:]
    refs = refs[:-12]
    local = wq_ref.shape[0]
    heads = local // HEAD_DIM
    buckets = table_ref.shape[0]
    if block < blocks - 1:
        part_refs, refs = refs[:3], refs[3:]
        rg_key_ref, rg_query_ref, sum_ref, cg_ref, ds_ref, rows_ref, part_ref = refs
    else:
        part_refs, joined_refs, refs = refs[:3], refs[3:5], refs[5:]
        cg_ref, ds_ref, rows_ref, part_ref, rg_key_ref, rg_query_ref, sum_ref, joined_ref = refs
    first = block * SEQMAX
    copies = start_copies(
        [
            (q_hbm.at[pl.ds(first, SEQMAX), :], q_ref),
            (k_hbm.at[pl.ds(first, SEQMAX), :], k_ref),
            (v_hbm.at[pl.ds(first, SEQMAX), :], v_ref),
            (weights_hbm, weights_ref),
            (pk_hbm, pk_back_ref),
            (pq_hbm, pq_back_ref),
            (hidden_hbm.at[pl.ds(first, SEQMAX), :], hidden_ref),
            (w_hbms[0], wq_ref),
            (w_hbms[1], wk_ref),
            (w_hbms[2], wv_ref),
        ]
        + ([(table_hbm, table_ref)] if block == blocks - 1 else []),
        sems,
    )
    if before is None:
        rg_key_ref[...] = jnp.zeros_like(rg_key_ref)
        rg_query_ref[...] = jnp.zeros_like(rg_query_ref)
    else:
        rg_key_ref[...] = before[0][...]
        rg_query_ref[...] = before[1][...]
    me = place_ref[0]
    for relative in range(groups):
        cg_ref[jnp.bitwise_xor(me, relative)] = cg_refs[relative][block]
    wait_copies(copies[:6])

    tile_rows, tile_lanes = tile_iotas()
    flip = (tile_rows + tile_lanes == TILE - 1).astype(BF16)

    def flipped(low):
        return jnp.concatenate([mm(part, flip) for part in lane_tiles(low)], axis=1)

    for head in range(heads):
        part = slice(head * HEAD_DIM, (head + 1) * HEAD_DIM)
        at_k = slice(local + head * HEAD_DIM, local + (head + 1) * HEAD_DIM)
        at_v = slice(2 * local + head * HEAD_DIM, 2 * local + (head + 1) * HEAD_DIM)
        queries = q_ref[:, part]
        keys = k_ref[:, part]
        values = v_ref[:, part]
        value_grad = jnp.zeros((SEQMAX, HEAD_DIM), F32)
        for at in range(0, SEQMAX, TILE):
            rows = slice(at, at + TILE)
            cotangent = cg_ref[at // TILE, :, part]
            low_weights = weights_ref[head, rows, :]
            weights = low_weights.astype(F32)
            weight_grad = mm_nt(cotangent, values)
            inner = jnp.sum(weights * weight_grad, axis=-1, keepdims=True)
            score_grad = (weights * (weight_grad - inner) * score_factor()).astype(BF16)
            ds_ref[rows, :] = score_grad
            value_grad = value_grad + mm_tn(low_weights, cotangent)
            by_offset = unskew(flipped(score_grad)).astype(BF16)
            window = window_of(at)
            query_grad = mm(score_grad, keys) + mm_nt(by_offset, pk_back_ref[part, window])
            rows_ref[rows, part] = query_grad.astype(BF16)
            rg_key_ref[part, window] += mm_tn(queries[rows], by_offset)
        rows_ref[:, at_v] = value_grad.astype(BF16)
        for at in range(0, SEQMAX, TILE):
            rows = slice(at, at + TILE)
            turned = ds_ref[:, rows].T
            by_offset = unskew(flipped(turned)).astype(BF16)
            window = window_of(at)
            key_grad = mm(turned, queries) + mm_nt(by_offset, pq_back_ref[part, window])
            rows_ref[rows, at_k] = key_grad.astype(BF16)
            rg_query_ref[part, window] += mm_tn(keys[rows], by_offset)
    wait_copies(copies[6:])
    total = mm(rows_ref[:, :local], wq_ref[...])
    total = total + mm(rows_ref[:, local : 2 * local], wk_ref[...])
    total = total + mm(rows_ref[:, 2 * local :], wv_ref[...])
    for at in range(0, SEQMAX, TILE):
        part_ref[jnp.bitwise_xor(at // TILE, me)] = total[at : at + TILE].astype(BF16)
    part_refs[0][...] = part_ref[0]
    part_refs[1][:TILE, :] = part_ref[1]
    part_refs[1][TILE:, :] = part_ref[3]
    part_refs[2][...] = part_ref[2]
    sums = mm_tn(rows_ref[...], hidden_ref[...])
    sum_ref[...] = sums if before is None else before[2][...] + sums
    if block < blocks - 1:
        return

    back = one_hot_columns(rel_ref, 1, buckets)

    def by_bucket(rg_ref):
        high, low = split_low(rg_ref[...])
        return (mm_nt(high, back) + mm_nt(low, back)).T

    def through_table(grad):
        high, low = split_low(grad)
        return mm_tn(high, table_ref[...]) + mm_tn(low, table_ref[...])

    pos_key = by_bucket(rg_key_ref)
    pos_query = by_bucket(rg_query_ref)
    sum_ref[:local, :] += through_table(pos_query)
    sum_ref[local : 2 * local, :] += through_table(pos_key)
    pos = jnp.concatenate([pos_key, pos_query], axis=1).astype(BF16)
    slots = joined_ref.shape[0]
    row_rows, pos_rows = 3 * local // slots, buckets // slots // 2
    for chunk in range(slots):
        slot = slot_of(jnp.bitwise_xor(chunk, place_ref[1]), (CORE, ACROSS_X, ACROSS_Y))
        at = 2 * chunk * pos_rows
        low = [norms_ref[chunk : chunk + 1, :], jnp.zeros((SMALL_ROWS - 1, 2 * local), F32)]
        low = jnp.concatenate(low, axis=0)
        pieces = [
            jnp.concatenate([pos[at : at + pos_rows], pos[at + pos_rows : at + 2 * pos_rows]], 1),
            jnp.concatenate([low, jnp.zeros_like(low)], axis=1).astype(BF16),
            sum_ref[chunk * row_rows : (chunk + 1) * row_rows, :].astype(BF16),
        ]
        joined_ref[slot] = jnp.concatenate(pieces, axis=0)
    joined_refs[0][...] = joined_ref[: slots // 2]
    joined_refs[1][...] = joined_ref[slots // 2 :]


def slot_of(relative, order):
    slot = 0
    for position, bit in enumerate(order):
        slot = slot + jnp.minimum(jnp.bitwise_and(relative, bit), 1) * (4 >> position)
    return slot


def backward_attention(
    block, blocks, place, context_grads, kept, weights, tables, hidden, w_rows, table, rel_rows,
    norms, before,
):
    width = hidden.shape[1]
    local = w_rows[0].shape[0]
    heads = local // HEAD_DIM
    buckets = table.shape[0]
    groups = SEQMAX // TILE
    last = block == blocks - 1
    parts = [Shape((rows, width), BF16) for rows in (TILE, 2 * TILE, TILE)]
    sums = [(local, OFFSETS), (local, OFFSETS), (3 * local, width)]
    joined_rows = 3 * local // CHUNKS + buckets // CHUNKS // 2 + SMALL_ROWS
    joined = Shape((CHUNKS // 2, joined_rows, width), BF16)
    scratch = [
        pltpu.VMEM((groups, TILE, local), BF16),
        pltpu.VMEM((SEQMAX, SEQMAX), BF16),
        pltpu.VMEM((SEQMAX, 3 * local), BF16),
        pltpu.VMEM((groups, TILE, width), BF16),
    ]
    if last:
        out_shape = parts + [joined] * 2
        scratch = scratch + [pltpu.VMEM(shape, F32) for shape in sums]
        scratch = scratch + [pltpu.VMEM((CHUNKS,) + joined.shape[1:], BF16)]
    else:
        out_shape = parts + [Shape(shape, F32) for shape in sums]
    scratch = scratch + [pltpu.VMEM((SEQMAX, local), BF16)] * 3
    scratch = scratch + [pltpu.VMEM((heads, SEQMAX, SEQMAX), BF16)]
    scratch = scratch + [pltpu.VMEM((local, OFFSETS), BF16)] * 2
    scratch = scratch + [pltpu.VMEM((SEQMAX, width), BF16)]
    scratch = scratch + [pltpu.VMEM((local, width), BF16)] * 3
    scratch = scratch + [pltpu.VMEM((buckets, width), BF16), pltpu.SemaphoreType.DMA((11,))]
    return kernel_call(
        functools.partial(backward_kernel, block, blocks),
        f"attention_backward_{block}",
        20_000_000_000,
        8_000_000,
        24,
        in_specs=[SCALARS]
        + [IN_VMEM] * groups
        + [IN_HBM] * 11
        + [IN_VMEM] * (2 + len(before)),
        out_specs=[IN_VMEM] * len(out_shape),
        out_shape=out_shape,
        scratch_shapes=scratch,
    )(
        place,
        *context_grads,
        *in_hbm(*kept, weights, *tables, hidden, *w_rows, table),
        rel_rows,
        norms,
        *before,
    )


def offset_rows(rel_buckets):
    plain = jnp.concatenate([rel_buckets[::-1], rel_buckets[:1]])
    back = plain.reshape(OFFSETS // TILE, TILE)[:, ::-1].reshape(OFFSETS)
    return jnp.stack([plain, back])


def layer_norm_parts(resid):
    centered = resid - jnp.mean(resid, axis=-1, keepdims=True)
    scale = lax.rsqrt(jnp.mean(centered * centered, axis=-1, keepdims=True) + NORM_EPS)
    return centered * scale, scale


def layer_norm_back(normal, scale, grad, gain):
    inner = grad * gain
    mean = jnp.mean(inner, axis=-1, keepdims=True)
    along = jnp.mean(inner * normal, axis=-1, keepdims=True)
    return scale * (inner - mean - normal * along)


def piece_kernel(place_ref, w_in_hbm, w_down_hbm, w_out_hbm, piece_ref, sems):
    replica = place_ref[1]
    width_rows, unit_rows = w_in_hbm.shape[0] // CHUNKS, w_down_hbm.shape[0] // CHUNKS
    rows = width_rows + unit_rows
    local = w_out_hbm.shape[0]
    at = pl.multiple_of(replica * width_rows, 16)
    down_at = pl.multiple_of(replica * unit_rows, 16)
    copies = start_copies(
        [
            (w_in_hbm.at[pl.ds(at, width_rows), :], piece_ref.at[pl.ds(0, width_rows), :]),
            (w_down_hbm.at[pl.ds(down_at, unit_rows), :], piece_ref.at[pl.ds(width_rows, unit_rows), :]),
        ],
        sems,
    )
    holds = replica * OUT_ROWS < local

    @pl.when(holds)
    def copy_out():
        out_at = pl.multiple_of(replica * OUT_ROWS, 16)
        wait_copies(
            start_copies(
                [(w_out_hbm.at[pl.ds(out_at, OUT_ROWS), :], piece_ref.at[pl.ds(rows, OUT_ROWS), :])],
                sems.at[pl.ds(2, 1)],
            )
        )

    @pl.when(jnp.logical_not(holds))
    def blank():
        piece_ref[rows:, :] = jnp.zeros((OUT_ROWS, piece_ref.shape[1]), BF16)

    wait_copies(copies)


def own_piece(place, w_in, w_down, w_out):
    width = w_down.shape[1]
    rows = w_in.shape[0] // CHUNKS + w_down.shape[0] // CHUNKS + OUT_ROWS
    return kernel_call(
        piece_kernel,
        "own_piece",
        0,
        700_000,
        4,
        in_specs=[SCALARS] + [IN_HBM] * 3,
        out_specs=IN_VMEM,
        out_shape=Shape((rows, width), BF16),
        scratch_shapes=[pltpu.SemaphoreType.DMA((3,))],
    )(place, *in_hbm(w_in, w_down, w_out))


def token_kernel(place_ref, *refs):
    groups = SEQMAX // TILE
    context_refs, refs = refs[:groups], refs[groups:]
    hidden_ref, out_grad_ref, norms_ref, w_in_ref, w_down_ref, w_out_ref = refs[:6]
    piece_refs, refs = refs[6 : 6 + len(GATHERED)], refs[6 + len(GATHERED) :]
    (
        output_ref, resid_ref, first_low_ref, act_out, pre_grad_out, ffn_grad_ref, attn_grad_ref,
        norm_grads_ref, *refs,
    ) = refs
    context_grad_refs, late_refs, refs = refs[:groups], refs[groups : groups + 2], refs[groups + 2 :]
    packed_vmem, out_vmem, slope_ref, sem, act_ref, pre_grad_ref, sems_out, *late_scratch = refs
    sent = []
    width = hidden_ref.shape[1]
    units = act_ref.shape[2]
    local = context_refs[0].shape[1]
    unit_rows, width_rows = units // CHUNKS, width // CHUNKS
    half = groups // 2

    out_copies, copies = gather_copies(piece_refs, packed_vmem, out_vmem, place_ref[1], sem)
    for copy in out_copies + copies:
        copy.start()
    for copy in out_copies:
        copy.wait()

    def packed(shift, first, rows):
        return packed_vmem[shift - 1, :, first : first + rows, :].reshape(CHUNKS * rows, width)

    def w_in(shift):
        return w_in_ref[...] if shift == 0 else packed(shift, 0, width_rows)

    def w_down(shift):
        return w_down_ref[...] if shift == 0 else packed(shift, width_rows, unit_rows)

    def w_out(shift):
        if shift == 0:
            return w_out_ref[...]
        return out_vmem[shift - 1].reshape(CHUNKS * OUT_ROWS, width)[:local]

    gain_one, bias_one = norms_ref[0:1, :], norms_ref[1:2, :]
    gain_two, bias_two = norms_ref[2:3, :], norms_ref[3:4, :]
    resid = hidden_ref[...].astype(F32)
    for g in range(groups):
        resid = resid + mm(context_refs[g][...], w_out(g)).astype(BF16).astype(F32)
    normal_one, scale_one = layer_norm_parts(resid)
    first_norm = normal_one * gain_one + bias_one
    first_low = first_norm.astype(BF16)
    first_low_ref[...] = first_low
    ffn_out = first_norm
    for g in range(groups):
        if g == 1:
            wait_copies(copies)
        pre_act = mm(first_low, w_in(g))
        area = 0.5 * (1.0 + lax.erf(pre_act * math.sqrt(0.5)))
        activated = (pre_act * area).astype(BF16)
        act_ref[g] = activated
        if g < half:
            sent += start_copies([(act_ref.at[g], act_out.at[g])], sems_out.at[pl.ds(g, 1)])
        density = jnp.exp(-0.5 * pre_act * pre_act) * (1.0 / math.sqrt(2.0 * math.pi))
        slope_ref[g] = area + pre_act * density
        ffn_out = ffn_out + mm(activated, w_down(g)).astype(BF16).astype(F32)
    normal_two, scale_two = layer_norm_parts(ffn_out)
    output_ref[...] = (normal_two * gain_two + bias_two).astype(BF16)
    out_grad = out_grad_ref[...].astype(F32)
    norm_grads_ref[...] = jnp.zeros_like(norm_grads_ref)
    norm_grads_ref[2:3, :] = jnp.sum(out_grad * normal_two, axis=0, keepdims=True)
    norm_grads_ref[3:4, :] = jnp.sum(out_grad, axis=0, keepdims=True)
    second_grad = layer_norm_back(normal_two, scale_two, out_grad, gain_two)
    ffn_grad = second_grad.astype(BF16)
    ffn_grad_ref[...] = ffn_grad
    first_grad = second_grad
    for g in range(groups):
        pre_grad = (mm_nt(ffn_grad, w_down(g)) * slope_ref[g]).astype(BF16)
        pre_grad_ref[g] = pre_grad
        if g < half:
            sent += start_copies(
                [(pre_grad_ref.at[g], pre_grad_out.at[g])], sems_out.at[pl.ds(half + g, 1)]
            )
        first_grad = first_grad + mm_nt(pre_grad, w_in(g))
    norm_grads_ref[0:1, :] = jnp.sum(first_grad * normal_one, axis=0, keepdims=True)
    norm_grads_ref[1:2, :] = jnp.sum(first_grad, axis=0, keepdims=True)
    resid_grad = layer_norm_back(normal_one, scale_one, first_grad, gain_one)
    resid_ref[...] = resid_grad
    attn_grad = resid_grad.astype(BF16)
    attn_grad_ref[...] = attn_grad
    for g in range(groups):
        context_grad_refs[g][...] = mm_nt(attn_grad, w_out(g)).astype(BF16)
    sorted_weight_grads(
        place_ref,
        [ref[...] for ref in context_refs[half:]],
        first_low,
        lambda j: act_ref[half + j],
        lambda j: pre_grad_ref[half + j],
        ffn_grad,
        attn_grad,
        late_refs,
        late_scratch,
    )
    wait_copies(sent)


def gather_copies(piece_refs, packed_vmem, out_vmem, replica, sem):
    out_copies, copies = [], []
    kept = packed_vmem.shape[2]
    for (group, relatives, firsts, rows), ref in zip(GATHERED, piece_refs):
        for i, relative in enumerate(relatives):
            chunk = jnp.bitwise_xor(replica, relative)
            first = firsts[i]
            main = min(first + rows, kept) - first
            copies.append(
                pltpu.make_async_copy(
                    ref.at[i, pl.ds(0, main), :],
                    packed_vmem.at[group - 1, chunk, pl.ds(first, main), :],
                    sem.at[len(copies)],
                )
            )
            if main < rows:
                out_copies.append(
                    pltpu.make_async_copy(
                        ref.at[i, pl.ds(main, rows - main), :],
                        out_vmem.at[group - 1, chunk],
                        sem.at[32 + len(out_copies)],
                    )
                )
    return out_copies, copies


def reached(axes):
    order = (0,)
    for bit in axes:
        order = order + tuple(relative + bit for relative in order)
    return order


def gathered_layout():
    layout = []
    for group, axes in ((1, (ACROSS_Y, ACROSS_X)), (2, (ACROSS_X, ACROSS_Y))):
        for core in (0, CORE):
            layout += [(group, (core, core + axes[0]), (0, 0), 2 * HALF_ROWS)]
            layout += [(group, (core + axes[1], core + sum(axes)), (0, 0), 2 * HALF_ROWS)]
    halves = ((0, (ACROSS_Y, ACROSS_X)), (HALF_ROWS, (ACROSS_X, ACROSS_Y)))
    for core in (0, CORE):
        both = tuple((core + r, first) for first, axes in halves for r in reached(axes))
        layout += [(3, tuple(r for r, first in both), tuple(first for r, first in both), HALF_ROWS)]
    return layout


ROW_ORDER = reached((ACROSS_Y, ACROSS_X, CORE))
HALF_ROWS = 112
GATHERED = gathered_layout()


def across(array, bit):
    return lax.ppermute(array, "dp", [(i, i ^ bit) for i in range(CHUNKS)])


def nearby(arrays):
    ways = (ACROSS_Y, ACROSS_X, ACROSS_Y + ACROSS_X)
    return [arrays[0]] + [across(array, way) for array, way in zip(arrays[1:], ways)]


def together(*values):
    return lax.optimization_barrier(values)


def token_layer(place, contexts, hidden, out_grad, norms, w_rows, pieces):
    tokens, width = hidden.shape
    local = contexts[0].shape[1]
    units = w_rows[0].shape[1]
    groups = len(contexts)
    rows = width // CHUNKS + units // CHUNKS + OUT_ROWS
    return kernel_call(
        token_kernel,
        "token_layer",
        15_000_000_000,
        18_000_000,
        40,
        in_specs=[SCALARS]
        + [IN_VMEM] * (groups + 6)
        + [ANYWHERE] * len(pieces),
        out_specs=[IN_VMEM] * 3 + [IN_HBM] * 2 + [IN_VMEM] * (3 + groups) + [IN_HBM] * 2,
        out_shape=[
            Shape((tokens, width), BF16),
            Shape((tokens, width), F32),
            Shape((tokens, width), BF16),
            hbm_shape((groups // 2, tokens, units), BF16),
            hbm_shape((groups // 2, tokens, units), BF16),
            Shape((tokens, width), BF16),
            Shape((tokens, width), BF16),
            Shape((8, width), F32),
        ]
        + [Shape((tokens, local), BF16)] * groups
        + [hbm_shape((2, CHUNKS // 2, rows, width), BF16)] * 2,
        scratch_shapes=[
            pltpu.VMEM((groups - 1, CHUNKS, rows - OUT_ROWS, width), BF16),
            pltpu.VMEM((groups - 1, CHUNKS, OUT_ROWS, width), BF16),
            pltpu.VMEM((groups, tokens, units), F32),
            pltpu.SemaphoreType.DMA((56,)),
            pltpu.VMEM((groups, tokens, units), BF16),
            pltpu.VMEM((groups, tokens, units), BF16),
            pltpu.SemaphoreType.DMA((groups,)),
        ]
        + weight_grad_scratch(width, units, rows),
    )(place, *contexts, hidden, out_grad, norms, *w_rows, *pieces)


def sorted_weight_grads(
    place_ref, contexts, first_low, act_of, pre_grad_of, ffn_grad, attn_grad, out_refs, scratch
):
    in_ref, down_ref, last_ref, sorted_ref, sems = scratch
    local = contexts[0].shape[1]
    width_rows = in_ref.shape[0] // CHUNKS
    unit_rows = down_ref.shape[0] // CHUNKS
    rows = width_rows + unit_rows
    last_ref[local:, :] = jnp.zeros((last_ref.shape[0] - local, last_ref.shape[1]), BF16)
    copies = []
    for j, axes in enumerate(PART_AXES):
        last_ref[:local, :] = mm_tn(contexts[j], attn_grad).astype(BF16)
        in_ref[...] = mm_tn(first_low, pre_grad_of(j)).astype(BF16)
        down_ref[...] = mm_tn(act_of(j), ffn_grad).astype(BF16)
        for side, core in ((1, CORE), (0, 0)):
            for slot, relative in enumerate(reached(axes[::-1])):
                chunk = jnp.bitwise_xor(relative + core, place_ref[1])
                at = pl.multiple_of(chunk * width_rows, 16)
                sorted_ref[side, j, slot, :width_rows] = in_ref[pl.ds(at, width_rows), :]
                at = pl.multiple_of(chunk * unit_rows, 16)
                sorted_ref[side, j, slot, width_rows:rows] = down_ref[pl.ds(at, unit_rows), :]
                at = pl.multiple_of(chunk * OUT_ROWS, 16)
                sorted_ref[side, j, slot, rows:] = last_ref[pl.ds(at, OUT_ROWS), :]
            copies += start_copies(
                [(sorted_ref.at[side, j], out_refs[side].at[j])], sems.at[pl.ds(2 * side + j, 1)]
            )
    wait_copies(copies)


def weight_grad_scratch(width, units, rows):
    return [
        pltpu.VMEM((width, width), BF16),
        pltpu.VMEM((units, width), BF16),
        pltpu.VMEM((CHUNKS * OUT_ROWS, width), BF16),
        pltpu.VMEM((2, 2, CHUNKS // 2, rows, width), BF16),
        pltpu.SemaphoreType.DMA((4,)),
    ]


def weight_grad_kernel(place_ref, *refs):
    context_refs, refs = refs[:2], refs[2:]
    first_low_ref, act_hbm, pre_grad_hbm, ffn_grad_ref, attn_grad_ref, *out_refs = refs[:7]
    scratch, (act_ref, pre_grad_ref, sems_in) = refs[7:12], refs[12:]
    arriving = start_copies(
        [
            (source.at[j], target.at[j])
            for j in range(2)
            for source, target in ((pre_grad_hbm, pre_grad_ref), (act_hbm, act_ref))
        ],
        sems_in,
    )

    def act_of(j):
        arriving[2 * j + 1].wait()
        return act_ref[j]

    def pre_grad_of(j):
        arriving[2 * j].wait()
        return pre_grad_ref[j]

    sorted_weight_grads(
        place_ref,
        [ref[...] for ref in context_refs],
        first_low_ref[...],
        act_of,
        pre_grad_of,
        ffn_grad_ref[...],
        attn_grad_ref[...],
        out_refs,
        scratch,
    )


def weight_grads(place, contexts, first_low, act, pre_grad, ffn_grad, attn_grad):
    tokens, units = act.shape[1:]
    width = first_low.shape[1]
    rows = width // CHUNKS + units // CHUNKS + OUT_ROWS
    return kernel_call(
        weight_grad_kernel,
        "weight_grads",
        4_000_000_000,
        7_000_000,
        15,
        in_specs=[SCALARS] + [IN_VMEM] * 3 + [IN_HBM] * 2 + [IN_VMEM] * 2,
        out_specs=[IN_HBM] * 2,
        out_shape=[hbm_shape((2, CHUNKS // 2, rows, width), BF16)] * 2,
        scratch_shapes=weight_grad_scratch(width, units, rows)
        + [
            pltpu.VMEM((2, tokens, units), BF16),
            pltpu.VMEM((2, tokens, units), BF16),
            pltpu.SemaphoreType.DMA((4,)),
        ],
    )(place, *contexts[:2], first_low, *in_hbm(act, pre_grad), ffn_grad, attn_grad)


def add(left, right):
    return (left.astype(F32) + right.astype(F32)).astype(BF16)


def total_of(arrays):
    return sum(array.astype(F32) for array in arrays).astype(BF16)


def reorder_kernel(place_ref, *refs):
    out_ref = refs[-1]
    groups = out_ref.shape[1]
    blocks = out_ref.shape[0]
    per = len(refs[:-1]) // groups
    for shift in range(groups):
        origin = jnp.bitwise_xor(place_ref[0], shift)
        for b in range(blocks):
            if per == 1:
                out_ref[b, origin] = refs[shift][b * TILE : (b + 1) * TILE, :]
            else:
                out_ref[b, origin] = refs[b * groups + shift][...]


def reorder(place, pieces, blocks):
    width = pieces[0].shape[1]
    groups = SEQMAX // TILE
    out = kernel_call(
        reorder_kernel,
        "reorder",
        0,
        3_000_000,
        8,
        in_specs=[SCALARS] + [IN_VMEM] * len(pieces),
        out_specs=IN_VMEM,
        out_shape=Shape((blocks, groups, TILE, width), BF16),
    )(place, *pieces)
    return out.reshape(blocks * SEQMAX, width)


def unpack_kernel(place_ref, *refs):
    piece_refs, refs = refs[:2], refs[2:]
    grad_in_ref, grad_down_ref, grad_out_ref, q_ref, k_ref, v_ref, all_ref = refs
    local = q_ref.shape[0]
    width_rows = grad_in_ref.shape[0] // CHUNKS
    unit_rows = grad_down_ref.shape[0] // CHUNKS
    row_rows = all_ref.shape[0] // CHUNKS
    out_at = width_rows + unit_rows
    rows_at = out_at + OUT_ROWS
    for slot, relative in enumerate(ROW_ORDER):
        ref = piece_refs[slot // 4].at[slot % 4]
        chunk = jnp.bitwise_xor(place_ref[1], relative)
        at = pl.multiple_of(chunk * width_rows, 8)
        grad_in_ref[pl.ds(at, width_rows), :] = ref[:width_rows, :].astype(F32)
        at = pl.multiple_of(chunk * unit_rows, 8)
        grad_down_ref[pl.ds(at, unit_rows), :] = ref[width_rows:out_at, :].astype(F32)
        at = pl.multiple_of(chunk * row_rows, 8)
        all_ref[pl.ds(at, row_rows), :] = ref[rows_at:, :].astype(F32)

        @pl.when(chunk * OUT_ROWS < grad_out_ref.shape[0])
        def out_rows(chunk=chunk, ref=ref):
            at = pl.multiple_of(chunk * OUT_ROWS, 8)
            grad_out_ref[pl.ds(at, OUT_ROWS), :] = ref[out_at:rows_at, :].astype(F32)

    for i, ref in enumerate((q_ref, k_ref, v_ref)):
        ref[...] = all_ref[i * local : (i + 1) * local, :]


def unpack(place, pieces, width, units, local):
    return kernel_call(
        unpack_kernel,
        "unpack",
        0,
        12_000_000,
        10,
        in_specs=[SCALARS] + [IN_VMEM] * 2,
        out_specs=[IN_VMEM] * 6,
        out_shape=[Shape((width, width), F32), Shape((units, width), F32)]
        + [Shape((local, width), F32)] * 4,
        scratch_shapes=[pltpu.VMEM((3 * local, width), F32)],
    )(place, *pieces)


def small_kernel(place_ref, *refs):
    piece_refs, table_ref, norm_refs, norms_ref = refs[:-6], refs[-6], refs[-5:-1], refs[-1]
    table_rows = table_ref.shape[0] // CHUNKS
    rows = table_rows + SMALL_ROWS
    columns = norms_ref.shape[1]
    per = CHUNKS // len(piece_refs)
    for slot, relative in enumerate(ROW_ORDER):
        ref, first = piece_refs[slot // per], slot % per * rows
        chunk = jnp.bitwise_xor(place_ref[1], relative)
        at = pl.multiple_of(chunk * table_rows, 8)
        table_ref[pl.ds(at, table_rows), :] = ref[first : first + table_rows, :].astype(F32)
        low = ref[first + table_rows : first + rows, :columns].astype(F32)
        norms_ref[pl.ds(chunk, 1), :] = low[:1]
    for i, ref in enumerate(norm_refs):
        ref[:columns] = norms_ref[2 * i, :]
        ref[columns:] = norms_ref[2 * i + 1, :]


def small_unpack(place, small, width, buckets):
    return kernel_call(
        small_kernel,
        "small_unpack",
        0,
        3_000_000,
        8,
        in_specs=[SCALARS] + [IN_VMEM] * len(small),
        out_specs=[IN_VMEM] * 5,
        out_shape=[Shape((buckets, width), F32)] + [Shape((width,), F32)] * 4,
        scratch_shapes=[pltpu.VMEM((CHUNKS, 4 * width // CHUNKS), F32)],
    )(place, *small)


def send(array, bits):
    return lax.ppermute(array, "tensor", [(i, i ^ bits) for i in range(SEQMAX // TILE)])


def exchange(pieces):
    return [pieces[0]] + [send(piece, r) for r, piece in enumerate(pieces) if r > 0]


def second_exchange(context, got):
    near = send(jnp.concatenate([context[1], got[1:]], 0), 1)
    return [context[0][0], near[0], got[0], near[1]]


def spread(array):
    near, far = send(array, 1), send(array, 2)
    return [array, near, far, send(far, 1)]


def shards(
    n_dp,
    n_tensor,
    hidden,
    out_grad,
    w_query,
    w_key,
    w_value,
    w_out,
    w_in,
    w_down,
    bucket_table,
    gain_one,
    bias_one,
    gain_two,
    bias_two,
    rel_buckets,
    group_counts,
    key_mask,
):
    tokens, width = hidden.shape
    local = w_query.shape[1]
    units = w_in.shape[1]
    buckets = bucket_table.shape[0]
    blocks = tokens // SEQMAX
    mine = tokens // n_tensor
    by_axis = n_dp == CHUNKS
    me = lax.axis_index("tensor")
    replica = lax.axis_index("dp") if by_axis else jnp.int32(0)
    place = jnp.stack([me, replica]).astype(jnp.int32)
    rel_rows = offset_rows(rel_buckets)
    width_rows, unit_rows = width // CHUNKS, units // CHUNKS
    padded = jnp.pad(w_out, ((0, CHUNKS * OUT_ROWS - local), (0, 0)))

    w_rows = (w_query.T, w_key.T, w_value.T)

    def my_rows(array):
        array = array.reshape(blocks, n_tensor, TILE, width)
        return lax.dynamic_index_in_dim(array, me, 1, keepdims=False).reshape(mine, width)

    def forward(block, context):
        weights, *context = forward_attention(
            block, place, group_counts, tables, rows, key_mask, context
        )
        return weights, context

    if by_axis:
        piece = own_piece(place, w_in, w_down, w_out)
        near, far = send(piece, 1), send(piece, 2)
        (*tables, q, k, v), saved = prepare(*w_rows, bucket_table, rel_rows, hidden)
        rows = (q, k, v)
        my_hidden, my_out_grad = my_rows(hidden), my_rows(out_grad)
        near, far, tables, rows, saved, my_hidden, my_out_grad = together(
            near, far, tables, rows, saved, my_hidden, my_out_grad
        )
        last = send(far, 1)
        near_y, far_x = across(near[None], ACROSS_Y), across(far[None], ACROSS_X)
        kept_0, context = forward(0, [])
        near, far, near_y, far_x, last, kept_0, context, tables, rows = together(
            near, far, near_y, far_x, last, kept_0, context, tables, rows
        )
        near = jnp.concatenate([near[None], near_y], 0)
        far = jnp.concatenate([far[None], far_x], 0)
        near_x, far_y = across(near, ACROSS_X), across(far, ACROSS_Y)
        top, low = last[None, :HALF_ROWS], last[None, HALF_ROWS:]
        top_y, low_x = across(top, ACROSS_Y), across(low, ACROSS_X)
        kept_1, context = forward(1, context)
        got = send(context[2], 2)
        near, near_x, far, far_y, top, top_y, low, low_x, context, got, kept_0, kept_1 = together(
            near, near_x, far, far_y, top, top_y, low, low_x, context, got, kept_0, kept_1
        )
        contexts = second_exchange(context, got)
        top = jnp.concatenate([top, top_y], 0)
        low = jnp.concatenate([low, low_x], 0)
        top_x, low_y = across(top, ACROSS_X), across(low, ACROSS_Y)
        cores = [across(near, CORE), across(near_x, CORE)]
        near, near_x, cores, far, far_y, top, top_x, low, low_y, contexts, kept_0, kept_1 = (
            together(
                near, near_x, cores, far, far_y, top, top_x, low, low_y, contexts, kept_0, kept_1
            )
        )
        both = jnp.concatenate([top, top_x, low, low_y], 0)
        gathered = [near, near_x, *cores]
        gathered += [far, far_y, across(far, CORE), across(far_y, CORE)]
        gathered += [both, across(both, CORE)]
    else:
        (*tables, q, k, v), saved = prepare(*w_rows, bucket_table, rel_rows, hidden)
        rows = (q, k, v)
        stacked = jnp.concatenate(
            [
                w_in.reshape(CHUNKS, width_rows, width),
                w_down.reshape(CHUNKS, unit_rows, width),
                padded.reshape(CHUNKS, OUT_ROWS, width),
            ],
            1,
        )
        sent = spread(stacked)
        gathered = [
            jnp.stack(
                [
                    sent[group][chunk, at : at + rows]
                    for chunk, at in zip(chunks, first)
                ]
            )
            for group, chunks, first, rows in GATHERED
        ]
        kept_0, context = forward(0, [])
        kept_1, context = forward(1, context)
        contexts = second_exchange(context, send(context[2], 2))
        my_hidden, my_out_grad = my_rows(hidden), my_rows(out_grad)
    *tables, q, k, v = saved
    norms = jnp.stack([gain_one, bias_one, gain_two, bias_two])
    (
        output, resid_grad, first_low, act, pre_grad, ffn_grad, attn_grad, norm_grads, *back,
        late_keep, late_give,
    ) = token_layer(
        place, contexts, my_hidden, my_out_grad, norms, (w_in, w_down, w_out), gathered
    )
    norm_grads = norm_grads[:4].reshape(CHUNKS, 4 * width // CHUNKS)

    def backward(block, kept, before):
        own, near, far, *before = backward_attention(
            block, blocks, place, back, (q, k, v), kept, tables, hidden, w_rows, bucket_table, rel_rows,
            norm_grads, before,
        )
        return [own, near, far], before

    keep_1, give_1 = late_keep, late_give
    back = exchange(back)
    core_1 = across(give_1, CORE) if by_axis else give_1
    keep_0, give_0 = weight_grads(
        place, contexts, first_low, act, pre_grad, ffn_grad, attn_grad
    )

    def first_sums(keep, got):
        return [add(keep[j, 2:], got[j, 2:]) for j in range(2)]

    sums_1 = first_sums(keep_1, core_1) if by_axis else []
    (
        back, core_1, sums_1, keep_0, give_0, keep_1, output, resid_grad, norm_grads, kept_0,
        kept_1, tables, place,
    ) = together(
        back, core_1, sums_1, keep_0, give_0, keep_1, output, resid_grad, norm_grads, kept_0,
        kept_1, tables, place,
    )
    back = [piece.reshape(blocks, TILE, local) for piece in back]

    def first_stage(sums):
        return [across(part, axes[0]) for part, axes in zip(sums, PART_AXES)]

    def second_stage(keep, got, first):
        given = [
            total_of([keep[j, 1:2], got[j, 1:2], first[j][1:2]]) for j in range(2)
        ]
        kept = [[keep[j, 0], got[j, 0], first[j][0]] for j in range(2)]
        return kept, [across(part, axes[1]) for part, axes in zip(given, PART_AXES)]

    def joint(arrays, way):
        rows = [array.shape[0] for array in arrays]
        got = send(jnp.concatenate(arrays, 0), way)
        return [got[sum(rows[:i]) : sum(rows[: i + 1])] for i in range(len(rows))]

    stage_1, core_0 = [], give_0
    if by_axis:
        stage_1 = first_stage(sums_1)
        core_0 = across(give_0, CORE)
    out_near, out_far = send(output, 1), send(output, 2)
    parts, before = backward(0, kept_0, ())
    (
        parts, before, stage_1, core_0, core_1, keep_0, keep_1, out_near, out_far, output,
        resid_grad, norm_grads, kept_1, tables, place, back,
    ) = together(
        parts, before, stage_1, core_0, core_1, keep_0, keep_1, out_near, out_far, output,
        resid_grad, norm_grads, kept_1, tables, place, back,
    )
    stage_0 = first_stage(first_sums(keep_0, core_0)) if by_axis else []
    late = second_stage(keep_1, core_1, stage_1) if by_axis else []
    near, out_last = joint([parts[1], out_far], 1)
    parts = [parts[0], near, parts[2]]
    parts_1, before = backward(1, kept_1, before)
    parts, parts_1, before, stage_0, late, core_0, keep_0, out_last, resid_grad = together(
        parts, parts_1, before, stage_0, late, core_0, keep_0, out_last, resid_grad
    )
    def total(block, pieces):
        wide = resid_grad[block * TILE : (block + 1) * TILE]
        for piece in pieces:
            wide = wide + piece.astype(F32)
        return wide.astype(BF16)

    keep, give = before
    thirds, sums = [], keep
    if not by_axis:
        joined = lax.psum(jnp.concatenate([keep, give], 0).astype(F32), "dp").astype(BF16)
    if by_axis:
        thirds = [second_stage(keep_0, core_0, stage_0), late]
        sums = add(keep, across(give, CORE))
    far_0 = send(add(parts[2], parts[1][TILE:]), 2)
    near_1 = send(parts_1[1], 1)
    grad_0 = total(0, [parts[0], parts[1][:TILE], far_0])
    sum_1 = add(parts_1[2], near_1[TILE:])
    grad_0, sum_1, parts_1, near_1, thirds, sums, resid_grad, out_last = together(
        grad_0, sum_1, parts_1, near_1, thirds, sums, resid_grad, out_last
    )

    output = reorder(place, [output, out_near, out_far, out_last], blocks)
    shard, near_0 = [], [grad_0]
    if by_axis:
        for kept, got in thirds:
            shard += [total_of([*kept[j], got[j][0]]) for j in range(2)]
        near_0 = near_0 + [shard[3]]
        joined = total_of(nearby([sums[i : i + 1] for i in range(CHUNKS // 2)]))
    near_0 = joint(near_0, 1)
    far_0, far_1 = joint([grad_0, sum_1], 2)
    pos_rows = buckets // CHUNKS // 2
    slots = joined.shape[0]
    row_grads = joined[:, pos_rows + SMALL_ROWS :]
    pos = joined[:, :pos_rows]
    pos = jnp.concatenate([pos[:, :, : 2 * local], pos[:, :, 2 * local :]], 1)
    w_table = jnp.concatenate([w_rows[1], w_rows[0]], 0)
    table_part = mm(pos.reshape(slots * 2 * pos_rows, 2 * local), w_table)
    table_part = table_part.astype(BF16).reshape(slots, 2 * pos_rows, width)
    small = jnp.concatenate([table_part, joined[:, pos_rows : pos_rows + SMALL_ROWS]], 1)
    small_rows = small.shape[1]
    small = small.reshape(slots * small_rows, width)
    grad_0, near_0, far_0, far_1, near_1, parts_1, resid_grad, output, shard, small, row_grads = (
        together(
            grad_0, near_0, far_0, far_1, near_1, parts_1, resid_grad, output, shard, small,
            row_grads,
        )
    )
    grad_1 = total(1, [parts_1[0], near_1[:TILE], far_1])
    shard_far = []
    if by_axis:
        shard_1, small_near = joint([shard[1], small], 1)
        shard_far = [shard_1, send(add(shard[2], near_0[1]), 2)]
    else:
        small_near = send(small, 1)
    small = add(small, small_near)
    if by_axis:
        row_grads = nearby([row_grads[0]] * 4)
    grad_0, near_0, far_0, grad_1, row_grads, small, shard, shard_far = together(
        grad_0, near_0, far_0, grad_1, row_grads, small, shard, shard_far
    )
    near_1, last_0 = joint([grad_1, far_0], 1)
    far_1, small_far = joint([grad_1, small], 2)
    small = add(small, small_far)
    if by_axis:
        shard = total_of([shard[0], *shard_far])
        pieces = nearby([shard] * 4)
        grad_0, near_0, far_0, last_0, grad_1, near_1, far_1, small, pieces, row_grads = together(
            grad_0, near_0, far_0, last_0, grad_1, near_1, far_1, small, pieces, row_grads
        )
        pieces = [jnp.concatenate(pair, 0) for pair in zip(pieces, row_grads)]
        pieces = jnp.stack(pieces)
        pieces = [pieces, across(pieces, CORE)]
        small = nearby([small] * 4)
    else:
        natural = []
        for keep, give in ((keep_0, give_0), (keep_1, give_1)):
            for j, axes in enumerate(PART_AXES):
                chunks = reached(axes[::-1] + (CORE,))
                both = jnp.concatenate([keep[j], give[j]], 0)
                natural.append(jnp.stack([both[chunks.index(c)] for c in range(CHUNKS)]))
        shard = jnp.stack(exchange(natural)).astype(F32)
        shard = lax.psum(sum(shard[r] for r in range(n_tensor)), "dp").astype(BF16)
        pieces = jnp.stack(
            [
                jnp.concatenate([shard[chunk], row_grads[slot]], 0)
                for slot, chunk in enumerate(ROW_ORDER)
            ]
        )
        pieces = [pieces[:4], pieces[4:]]
        small = [small]
    last_1 = send(far_1, 1)
    if by_axis:
        grad_0, near_0, far_0, last_0, grad_1, near_1, far_1, last_1, small, pieces = together(
            grad_0, near_0, far_0, last_0, grad_1, near_1, far_1, last_1, small, pieces
        )
        small = jnp.concatenate(small, 0)
        small = [small, across(small, CORE)]
    grad_hidden = reorder(
        place, [grad_0, near_0[0], far_0, last_0, grad_1, near_1, far_1, last_1], blocks
    )
    grad_in, grad_down, grad_out, grad_query, grad_key, grad_value = unpack(
        place, pieces, width, units, local
    )
    if by_axis:
        small, grad_hidden, grad_in, grad_down, grad_out, grad_query, grad_key, grad_value = (
            together(
                small, grad_hidden, grad_in, grad_down, grad_out, grad_query, grad_key, grad_value
            )
        )
    grad_table, *norm_grads = small_unpack(place, small, width, buckets)
    return (
        output,
        grad_hidden,
        grad_query.T,
        grad_key.T,
        grad_value.T,
        grad_out,
        grad_in,
        grad_down,
        grad_table,
        *norm_grads,
    )


def solution(mesh):
    in_specs = (
        P("dp", None),
        P("dp", None),
        P(None, "tensor"),
        P(None, "tensor"),
        P(None, "tensor"),
        P("tensor", None),
        P(None, "tensor"),
        P("tensor", None),
        P(),
        P(),
        P(),
        P(),
        P(),
        P(),
        P("dp", None),
        P("dp"),
    )
    out_specs = (
        P("dp", None),
        P("dp", None),
        P(None, "tensor"),
        P(None, "tensor"),
        P(None, "tensor"),
        P("tensor", None),
        P(None, "tensor"),
        P("tensor", None),
        P(),
        P(),
        P(),
        P(),
        P(),
    )
    body = functools.partial(shards, mesh.shape["dp"], mesh.shape["tensor"])
    return jax.shard_map(body, mesh=mesh, in_specs=in_specs, out_specs=out_specs, check_vma=False)
```

```python
import functools
import math

import jax
import jax.numpy as jnp
from jax import lax
from jax.experimental import pallas as pl
from jax.experimental.pallas import tpu as pltpu
from jax.sharding import PartitionSpec as P

NORM_EPS = 1e-07
HEAD_DIM = 64
SEQMAX = 512
TILE = 128
WINDOW = SEQMAX + TILE
OFFSETS = 2 * SEQMAX
NEGATIVE = -1e30
CHUNKS = 8
CORE, ACROSS_X, ACROSS_Y = 1, 2, 4
OUT_ROWS = 32
SMALL_ROWS = 16
F32 = jnp.float32
BF16 = jnp.bfloat16


def score_factor():
    return 1.0 / math.sqrt(3.0 * HEAD_DIM)


def mm(left, right):
    return jnp.dot(left, right, preferred_element_type=F32)


def mm_nt(left, right):
    return lax.dot_general(left, right, (((1,), (1,)), ((), ())), preferred_element_type=F32)


def mm_tn(left, right):
    return lax.dot_general(left, right, (((0,), (0,)), ((), ())), preferred_element_type=F32)


def starts_of(places, counts_ref):
    long_end = SEQMAX * counts_ref[0, 0]
    mid_end = long_end + SEQMAX // 2 * counts_ref[0, 1]
    in_long = places < long_end
    in_mid = places < mid_end
    anchor = jnp.where(in_long, 0, jnp.where(in_mid, long_end, mid_end))
    shift = jnp.where(in_long, 9, jnp.where(in_mid, 8, 7))
    return anchor + lax.shift_left(lax.shift_right_logical(places - anchor, shift), shift)


def tile_iotas():
    rows = lax.broadcasted_iota(jnp.int32, (TILE, TILE), 0)
    lanes = lax.broadcasted_iota(jnp.int32, (TILE, TILE), 1)
    return rows, lanes


def lane_tiles(wide):
    return [wide[:, c : c + TILE] for c in range(0, wide.shape[1], TILE)]


def skew(wide):
    rows, lanes = tile_iotas()
    keep = lanes <= rows
    turned = [pltpu.roll(part, 1, 1, stride=1, stride_axis=0) for part in lane_tiles(wide)]
    return jnp.concatenate(
        [jnp.where(keep, turned[c], turned[c + 1]) for c in range(len(turned) - 1)], axis=1
    )


def unskew(flipped):
    rows, lanes = tile_iotas()
    late = lanes > rows
    turned = [pltpu.roll(part, 1, 1, stride=1, stride_axis=0) for part in lane_tiles(flipped)]
    zero = jnp.zeros((TILE, TILE), F32)
    turned = [zero] + turned + [zero]
    return jnp.concatenate(
        [jnp.where(late, turned[c], turned[c + 1]) for c in range(len(turned) - 1)], axis=1
    )


def window_of(tile_at):
    low = SEQMAX - TILE - tile_at
    return slice(low, low + WINDOW)


def one_hot_columns(rel_ref, row, buckets):
    ids = lax.broadcasted_iota(jnp.int32, (buckets, OFFSETS), 0)
    return (ids == rel_ref[row : row + 1, :]).astype(BF16)


def split_low(wide):
    high = wide.astype(BF16)
    return high, (wide - high.astype(F32)).astype(BF16)


SCALARS = pl.BlockSpec(memory_space=pltpu.SMEM)
ANYWHERE = pl.BlockSpec(memory_space=pl.ANY)
IN_HBM = pl.BlockSpec(memory_space=pltpu.HBM)
IN_VMEM = pl.BlockSpec(memory_space=pltpu.VMEM)
Shape = jax.ShapeDtypeStruct


def in_hbm(*arrays):
    return [pltpu.with_memory_space_constraint(array, pltpu.HBM) for array in arrays]


def hbm_shape(shape, kind):
    return pltpu.HBM(shape, kind)


def kernel_call(kernel, name, flops, moved, vmem, **rest):
    return pl.pallas_call(
        kernel,
        compiler_params=pltpu.CompilerParams(vmem_limit_bytes=vmem * 2**20),
        cost_estimate=pl.CostEstimate(flops=flops, bytes_accessed=moved, transcendentals=0),
        name=name,
        **rest,
    )


PART_AXES = ((ACROSS_Y, ACROSS_X), (ACROSS_X, ACROSS_Y))


def start_copies(pairs, sems):
    copies = [
        pltpu.make_async_copy(source, target, sems.at[i]) for i, (source, target) in enumerate(pairs)
    ]
    for copy in copies:
        copy.start()
    return copies


def wait_copies(copies):
    for copy in copies:
        copy.wait()


def prepare_kernel(
    wq_ref, wk_ref, wv_ref, table_ref, rel_ref, hidden_ref, pk_ref, pq_ref, q_ref, k_ref, v_ref,
    pk_back_out, pq_back_out, q_out, k_out, v_out, pk_back, pq_back, sems,
):
    table = table_ref[...]
    buckets = table.shape[0]
    pos_key = mm_nt(wk_ref[...], table).astype(BF16)
    pos_query = mm_nt(wq_ref[...], table).astype(BF16)
    plain = one_hot_columns(rel_ref, 0, buckets)
    pk_ref[...] = mm(pos_key, plain).astype(BF16)
    pq_ref[...] = mm(pos_query, plain).astype(BF16)
    back = one_hot_columns(rel_ref, 1, buckets)
    pk_back[...] = mm(pos_key, back).astype(BF16)
    pq_back[...] = mm(pos_query, back).astype(BF16)
    copies = start_copies([(pk_back, pk_back_out), (pq_back, pq_back_out)], sems)
    hidden = hidden_ref[...]
    for i, (ref, w_ref, out) in enumerate(
        ((q_ref, wq_ref, q_out), (k_ref, wk_ref, k_out), (v_ref, wv_ref, v_out))
    ):
        ref[...] = mm_nt(hidden, w_ref[...]).astype(BF16)
        copies += start_copies([(ref, out)], sems.at[pl.ds(2 + i, 1)])
    wait_copies(copies)


def prepare(w_query, w_key, w_value, table, rel_rows, hidden):
    local = w_query.shape[0]
    tokens = hidden.shape[0]
    table_kind = ((local, OFFSETS), BF16)
    row_kind = ((tokens, local), BF16)
    out = kernel_call(
        prepare_kernel,
        "prepare",
        4_000_000_000,
        6_000_000,
        10,
        in_specs=[IN_VMEM] * 6,
        out_specs=[IN_VMEM] * 5 + [IN_HBM] * 5,
        out_shape=[Shape(*table_kind)] * 2
        + [Shape(*row_kind)] * 3
        + [hbm_shape(*table_kind)] * 2
        + [hbm_shape(*row_kind)] * 3,
        scratch_shapes=[pltpu.VMEM(*table_kind)] * 2 + [pltpu.SemaphoreType.DMA((5,))],
    )(w_query, w_key, w_value, table, rel_rows, hidden)
    return out[:5], out[5:]


def forward_kernel(
    block, place_ref, counts_ref, pk_ref, pq_ref, q_ref, k_ref, v_ref, mask_ref, *rest
):
    before, rest = rest[: 3 if block else 0], rest[3 if block else 0 :]
    weights_out, context_refs, rest = rest[0], rest[1:4], rest[4:]
    context_ref, bias_ref, rel_score_ref, weights_ref, sems_out = rest
    heads = q_ref.shape[1] // HEAD_DIM
    first = block * SEQMAX
    here = slice(first, first + SEQMAX)
    column = starts_of(lax.broadcasted_iota(jnp.int32, (SEQMAX, 1), 0) + first, counts_ref)
    row = starts_of(lax.broadcasted_iota(jnp.int32, (1, SEQMAX), 1) + first, counts_ref)
    row = jnp.where(mask_ref[block] == 1, row, -1)
    bias_ref[...] = jnp.where(column == row, 0.0, NEGATIVE)
    copies = []
    for head in range(heads):
        part = slice(head * HEAD_DIM, (head + 1) * HEAD_DIM)
        queries = q_ref[here, part]
        keys = k_ref[here, part]
        values = v_ref[here, part]
        for at in range(0, SEQMAX, TILE):
            rel = mm(keys[at : at + TILE], pq_ref[part, window_of(at)])
            rel_score_ref[at : at + TILE, :] = skew(rel)
        for at in range(0, SEQMAX, TILE):
            rows = slice(at, at + TILE)
            raw = mm_nt(queries[rows], keys)
            raw = raw + skew(mm(queries[rows], pk_ref[part, window_of(at)]))
            raw = raw + rel_score_ref[:, rows].T
            scaled = raw * score_factor() + bias_ref[rows, :]
            top = jnp.max(scaled, axis=-1, keepdims=True)
            exponent = jnp.exp(scaled - top)
            total = jnp.sum(exponent, axis=-1, keepdims=True)
            weights = (exponent * (1.0 / total)).astype(BF16)
            weights_ref[head, rows, :] = weights
            relative = jnp.bitwise_xor(at // TILE, place_ref[0])
            context_ref[relative, :, part] = mm(weights, values).astype(BF16)
        copies += start_copies(
            [(weights_ref.at[head], weights_out.at[head])], sems_out.at[pl.ds(head, 1)]
        )
    at = 0
    for n, ref in enumerate(context_refs):
        for r in range(ref.shape[0]):
            for b in range(block):
                ref[r, b * TILE : (b + 1) * TILE] = before[n][r, b * TILE : (b + 1) * TILE]
            ref[r, block * TILE : (block + 1) * TILE] = context_ref[at]
            at += 1
    wait_copies(copies)


def forward_attention(block, place, counts, tables, rows, key_mask, context):
    tokens, local = rows[0].shape
    heads = local // HEAD_DIM
    blocks = tokens // SEQMAX
    groups = SEQMAX // TILE
    return kernel_call(
        functools.partial(forward_kernel, block),
        f"attention_forward_{block}",
        10_000_000_000,
        5_000_000,
        12,
        in_specs=[SCALARS] * 2 + [IN_VMEM] * (6 + len(context)),
        out_specs=[IN_HBM] + [IN_VMEM] * 3,
        out_shape=[hbm_shape((heads, SEQMAX, SEQMAX), BF16)]
        + [Shape((n, (block + 1) * TILE, local), BF16) for n in (1, 1, 2)],
        scratch_shapes=[pltpu.VMEM((groups, TILE, local), BF16)]
        + [pltpu.VMEM((SEQMAX, SEQMAX), F32)] * 2
        + [pltpu.VMEM((heads, SEQMAX, SEQMAX), BF16), pltpu.SemaphoreType.DMA((heads,))],
    )(place, counts, *tables, *rows, key_mask.reshape(blocks, 1, SEQMAX), *context)


def backward_kernel(block, blocks, place_ref, *refs):
    groups = SEQMAX // TILE
    cg_refs, refs = refs[:groups], refs[groups:]
    q_hbm, k_hbm, v_hbm, weights_hbm, pk_hbm, pq_hbm, hidden_hbm = refs[:7]
    w_hbms, table_hbm, rel_ref, norms_ref = refs[7:10], *refs[10:13]
    refs = refs[13:]
    before, refs = (refs[:3], refs[3:]) if block > 0 else (None, refs)
    q_ref, k_ref, v_ref, weights_ref, pk_back_ref, pq_back_ref, hidden_ref = refs[-12:-5]
    wq_ref, wk_ref, wv_ref, table_ref, sems = refs[-5:]
    refs = refs[:-12]
    local = wq_ref.shape[0]
    heads = local // HEAD_DIM
    buckets = table_ref.shape[0]
    if block < blocks - 1:
        part_refs, refs = refs[:3], refs[3:]
        rg_key_ref, rg_query_ref, sum_ref, cg_ref, ds_ref, rows_ref, part_ref = refs
    else:
        part_refs, joined_refs, refs = refs[:3], refs[3:5], refs[5:]
        cg_ref, ds_ref, rows_ref, part_ref, rg_key_ref, rg_query_ref, sum_ref, joined_ref = refs
    first = block * SEQMAX
    copies = start_copies(
        [
            (q_hbm.at[pl.ds(first, SEQMAX), :], q_ref),
            (k_hbm.at[pl.ds(first, SEQMAX), :], k_ref),
            (v_hbm.at[pl.ds(first, SEQMAX), :], v_ref),
            (weights_hbm, weights_ref),
            (pk_hbm, pk_back_ref),
            (pq_hbm, pq_back_ref),
            (hidden_hbm.at[pl.ds(first, SEQMAX), :], hidden_ref),
            (w_hbms[0], wq_ref),
            (w_hbms[1], wk_ref),
            (w_hbms[2], wv_ref),
        ]
        + ([(table_hbm, table_ref)] if block == blocks - 1 else []),
        sems,
    )
    if before is None:
        rg_key_ref[...] = jnp.zeros_like(rg_key_ref)
        rg_query_ref[...] = jnp.zeros_like(rg_query_ref)
    else:
        rg_key_ref[...] = before[0][...]
        rg_query_ref[...] = before[1][...]
    me = place_ref[0]
    for relative in range(groups):
        cg_ref[jnp.bitwise_xor(me, relative)] = cg_refs[relative][block]
    wait_copies(copies[:6])

    tile_rows, tile_lanes = tile_iotas()
    flip = (tile_rows + tile_lanes == TILE - 1).astype(BF16)

    def flipped(low):
        return jnp.concatenate([mm(part, flip) for part in lane_tiles(low)], axis=1)

    for head in range(heads):
        part = slice(head * HEAD_DIM, (head + 1) * HEAD_DIM)
        at_k = slice(local + head * HEAD_DIM, local + (head + 1) * HEAD_DIM)
        at_v = slice(2 * local + head * HEAD_DIM, 2 * local + (head + 1) * HEAD_DIM)
        queries = q_ref[:, part]
        keys = k_ref[:, part]
        values = v_ref[:, part]
        value_grad = jnp.zeros((SEQMAX, HEAD_DIM), F32)
        for at in range(0, SEQMAX, TILE):
            rows = slice(at, at + TILE)
            cotangent = cg_ref[at // TILE, :, part]
            low_weights = weights_ref[head, rows, :]
            weights = low_weights.astype(F32)
            weight_grad = mm_nt(cotangent, values)
            inner = jnp.sum(weights * weight_grad, axis=-1, keepdims=True)
            score_grad = (weights * (weight_grad - inner) * score_factor()).astype(BF16)
            ds_ref[rows, :] = score_grad
            value_grad = value_grad + mm_tn(low_weights, cotangent)
            by_offset = unskew(flipped(score_grad)).astype(BF16)
            window = window_of(at)
            query_grad = mm(score_grad, keys) + mm_nt(by_offset, pk_back_ref[part, window])
            rows_ref[rows, part] = query_grad.astype(BF16)
            rg_key_ref[part, window] += mm_tn(queries[rows], by_offset)
        rows_ref[:, at_v] = value_grad.astype(BF16)
        for at in range(0, SEQMAX, TILE):
            rows = slice(at, at + TILE)
            turned = ds_ref[:, rows].T
            by_offset = unskew(flipped(turned)).astype(BF16)
            window = window_of(at)
            key_grad = mm(turned, queries) + mm_nt(by_offset, pq_back_ref[part, window])
            rows_ref[rows, at_k] = key_grad.astype(BF16)
            rg_query_ref[part, window] += mm_tn(keys[rows], by_offset)
    wait_copies(copies[6:])
    total = mm(rows_ref[:, :local], wq_ref[...])
    total = total + mm(rows_ref[:, local : 2 * local], wk_ref[...])
    total = total + mm(rows_ref[:, 2 * local :], wv_ref[...])
    for at in range(0, SEQMAX, TILE):
        part_ref[jnp.bitwise_xor(at // TILE, me)] = total[at : at + TILE].astype(BF16)
    part_refs[0][...] = part_ref[0]
    part_refs[1][:TILE, :] = part_ref[1]
    part_refs[1][TILE:, :] = part_ref[3]
    part_refs[2][...] = part_ref[2]
    sums = mm_tn(rows_ref[...], hidden_ref[...])
    sum_ref[...] = sums if before is None else before[2][...] + sums
    if block < blocks - 1:
        return

    back = one_hot_columns(rel_ref, 1, buckets)

    def by_bucket(rg_ref):
        high, low = split_low(rg_ref[...])
        return (mm_nt(high, back) + mm_nt(low, back)).T

    def through_table(grad):
        high, low = split_low(grad)
        return mm_tn(high, table_ref[...]) + mm_tn(low, table_ref[...])

    pos_key = by_bucket(rg_key_ref)
    pos_query = by_bucket(rg_query_ref)
    sum_ref[:local, :] += through_table(pos_query)
    sum_ref[local : 2 * local, :] += through_table(pos_key)
    pos = jnp.concatenate([pos_key, pos_query], axis=1).astype(BF16)
    slots = joined_ref.shape[0]
    row_rows, pos_rows = 3 * local // slots, buckets // slots // 2
    for chunk in range(slots):
        slot = slot_of(jnp.bitwise_xor(chunk, place_ref[1]), (CORE, ACROSS_X, ACROSS_Y))
        at = 2 * chunk * pos_rows
        low = [norms_ref[chunk : chunk + 1, :], jnp.zeros((SMALL_ROWS - 1, 2 * local), F32)]
        low = jnp.concatenate(low, axis=0)
        pieces = [
            jnp.concatenate([pos[at : at + pos_rows], pos[at + pos_rows : at + 2 * pos_rows]], 1),
            jnp.concatenate([low, jnp.zeros_like(low)], axis=1).astype(BF16),
            sum_ref[chunk * row_rows : (chunk + 1) * row_rows, :].astype(BF16),
        ]
        joined_ref[slot] = jnp.concatenate(pieces, axis=0)
    joined_refs[0][...] = joined_ref[: slots // 2]
    joined_refs[1][...] = joined_ref[slots // 2 :]


def slot_of(relative, order):
    slot = 0
    for position, bit in enumerate(order):
        slot = slot + jnp.minimum(jnp.bitwise_and(relative, bit), 1) * (4 >> position)
    return slot


def backward_attention(
    block, blocks, place, context_grads, kept, weights, tables, hidden, w_rows, table, rel_rows,
    norms, before,
):
    width = hidden.shape[1]
    local = w_rows[0].shape[0]
    heads = local // HEAD_DIM
    buckets = table.shape[0]
    groups = SEQMAX // TILE
    last = block == blocks - 1
    parts = [Shape((rows, width), BF16) for rows in (TILE, 2 * TILE, TILE)]
    sums = [(local, OFFSETS), (local, OFFSETS), (3 * local, width)]
    joined_rows = 3 * local // CHUNKS + buckets // CHUNKS // 2 + SMALL_ROWS
    joined = Shape((CHUNKS // 2, joined_rows, width), BF16)
    scratch = [
        pltpu.VMEM((groups, TILE, local), BF16),
        pltpu.VMEM((SEQMAX, SEQMAX), BF16),
        pltpu.VMEM((SEQMAX, 3 * local), BF16),
        pltpu.VMEM((groups, TILE, width), BF16),
    ]
    if last:
        out_shape = parts + [joined] * 2
        scratch = scratch + [pltpu.VMEM(shape, F32) for shape in sums]
        scratch = scratch + [pltpu.VMEM((CHUNKS,) + joined.shape[1:], BF16)]
    else:
        out_shape = parts + [Shape(shape, F32) for shape in sums]
    scratch = scratch + [pltpu.VMEM((SEQMAX, local), BF16)] * 3
    scratch = scratch + [pltpu.VMEM((heads, SEQMAX, SEQMAX), BF16)]
    scratch = scratch + [pltpu.VMEM((local, OFFSETS), BF16)] * 2
    scratch = scratch + [pltpu.VMEM((SEQMAX, width), BF16)]
    scratch = scratch + [pltpu.VMEM((local, width), BF16)] * 3
    scratch = scratch + [pltpu.VMEM((buckets, width), BF16), pltpu.SemaphoreType.DMA((11,))]
    return kernel_call(
        functools.partial(backward_kernel, block, blocks),
        f"attention_backward_{block}",
        20_000_000_000,
        8_000_000,
        24,
        in_specs=[SCALARS]
        + [IN_VMEM] * groups
        + [IN_HBM] * 11
        + [IN_VMEM] * (2 + len(before)),
        out_specs=[IN_VMEM] * len(out_shape),
        out_shape=out_shape,
        scratch_shapes=scratch,
    )(
        place,
        *context_grads,
        *in_hbm(*kept, weights, *tables, hidden, *w_rows, table),
        rel_rows,
        norms,
        *before,
    )


def offset_rows(rel_buckets):
    plain = jnp.concatenate([rel_buckets[::-1], rel_buckets[:1]])
    back = plain.reshape(OFFSETS // TILE, TILE)[:, ::-1].reshape(OFFSETS)
    return jnp.stack([plain, back])


def layer_norm_parts(resid):
    centered = resid - jnp.mean(resid, axis=-1, keepdims=True)
    scale = lax.rsqrt(jnp.mean(centered * centered, axis=-1, keepdims=True) + NORM_EPS)
    return centered * scale, scale


def layer_norm_back(normal, scale, grad, gain):
    inner = grad * gain
    mean = jnp.mean(inner, axis=-1, keepdims=True)
    along = jnp.mean(inner * normal, axis=-1, keepdims=True)
    return scale * (inner - mean - normal * along)


def piece_kernel(place_ref, w_in_hbm, w_down_hbm, w_out_hbm, piece_ref, sems):
    replica = place_ref[1]
    width_rows, unit_rows = w_in_hbm.shape[0] // CHUNKS, w_down_hbm.shape[0] // CHUNKS
    rows = width_rows + unit_rows
    local = w_out_hbm.shape[0]
    at = pl.multiple_of(replica * width_rows, 16)
    down_at = pl.multiple_of(replica * unit_rows, 16)
    copies = start_copies(
        [
            (w_in_hbm.at[pl.ds(at, width_rows), :], piece_ref.at[pl.ds(0, width_rows), :]),
            (w_down_hbm.at[pl.ds(down_at, unit_rows), :], piece_ref.at[pl.ds(width_rows, unit_rows), :]),
        ],
        sems,
    )
    holds = replica * OUT_ROWS < local

    @pl.when(holds)
    def copy_out():
        out_at = pl.multiple_of(replica * OUT_ROWS, 16)
        wait_copies(
            start_copies(
                [(w_out_hbm.at[pl.ds(out_at, OUT_ROWS), :], piece_ref.at[pl.ds(rows, OUT_ROWS), :])],
                sems.at[pl.ds(2, 1)],
            )
        )

    @pl.when(jnp.logical_not(holds))
    def blank():
        piece_ref[rows:, :] = jnp.zeros((OUT_ROWS, piece_ref.shape[1]), BF16)

    wait_copies(copies)


def own_piece(place, w_in, w_down, w_out):
    width = w_down.shape[1]
    rows = w_in.shape[0] // CHUNKS + w_down.shape[0] // CHUNKS + OUT_ROWS
    return kernel_call(
        piece_kernel,
        "own_piece",
        0,
        700_000,
        4,
        in_specs=[SCALARS] + [IN_HBM] * 3,
        out_specs=IN_VMEM,
        out_shape=Shape((rows, width), BF16),
        scratch_shapes=[pltpu.SemaphoreType.DMA((3,))],
    )(place, *in_hbm(w_in, w_down, w_out))


def token_kernel(place_ref, *refs):
    groups = SEQMAX // TILE
    context_refs, refs = refs[:groups], refs[groups:]
    hidden_ref, out_grad_ref, norms_ref, w_in_ref, w_down_ref, w_out_ref = refs[:6]
    piece_refs, refs = refs[6 : 6 + len(GATHERED)], refs[6 + len(GATHERED) :]
    (
        output_ref, resid_ref, first_low_ref, act_out, pre_grad_out, ffn_grad_ref, attn_grad_ref,
        norm_grads_ref, *refs,
    ) = refs
    context_grad_refs, late_refs, refs = refs[:groups], refs[groups : groups + 2], refs[groups + 2 :]
    packed_vmem, out_vmem, slope_ref, sem, act_ref, pre_grad_ref, sems_out, *late_scratch = refs
    sent = []
    width = hidden_ref.shape[1]
    units = act_ref.shape[2]
    local = context_refs[0].shape[1]
    unit_rows, width_rows = units // CHUNKS, width // CHUNKS
    half = groups // 2

    out_copies, copies = gather_copies(piece_refs, packed_vmem, out_vmem, place_ref[1], sem)
    for copy in out_copies + copies:
        copy.start()
    for copy in out_copies:
        copy.wait()

    def packed(shift, first, rows):
        return packed_vmem[shift - 1, :, first : first + rows, :].reshape(CHUNKS * rows, width)

    def w_in(shift):
        return w_in_ref[...] if shift == 0 else packed(shift, 0, width_rows)

    def w_down(shift):
        return w_down_ref[...] if shift == 0 else packed(shift, width_rows, unit_rows)

    def w_out(shift):
        if shift == 0:
            return w_out_ref[...]
        return out_vmem[shift - 1].reshape(CHUNKS * OUT_ROWS, width)[:local]

    gain_one, bias_one = norms_ref[0:1, :], norms_ref[1:2, :]
    gain_two, bias_two = norms_ref[2:3, :], norms_ref[3:4, :]
    resid = hidden_ref[...].astype(F32)
    for g in range(groups):
        resid = resid + mm(context_refs[g][...], w_out(g)).astype(BF16).astype(F32)
    normal_one, scale_one = layer_norm_parts(resid)
    first_norm = normal_one * gain_one + bias_one
    first_low = first_norm.astype(BF16)
    first_low_ref[...] = first_low
    ffn_out = first_norm
    for g in range(groups):
        if g == 1:
            wait_copies(copies)
        pre_act = mm(first_low, w_in(g))
        area = 0.5 * (1.0 + lax.erf(pre_act * math.sqrt(0.5)))
        activated = (pre_act * area).astype(BF16)
        act_ref[g] = activated
        if g < half:
            sent += start_copies([(act_ref.at[g], act_out.at[g])], sems_out.at[pl.ds(g, 1)])
        density = jnp.exp(-0.5 * pre_act * pre_act) * (1.0 / math.sqrt(2.0 * math.pi))
        slope_ref[g] = area + pre_act * density
        ffn_out = ffn_out + mm(activated, w_down(g)).astype(BF16).astype(F32)
    normal_two, scale_two = layer_norm_parts(ffn_out)
    output_ref[...] = (normal_two * gain_two + bias_two).astype(BF16)
    out_grad = out_grad_ref[...].astype(F32)
    norm_grads_ref[...] = jnp.zeros_like(norm_grads_ref)
    norm_grads_ref[2:3, :] = jnp.sum(out_grad * normal_two, axis=0, keepdims=True)
    norm_grads_ref[3:4, :] = jnp.sum(out_grad, axis=0, keepdims=True)
    second_grad = layer_norm_back(normal_two, scale_two, out_grad, gain_two)
    ffn_grad = second_grad.astype(BF16)
    ffn_grad_ref[...] = ffn_grad
    first_grad = second_grad
    for g in range(groups):
        pre_grad = (mm_nt(ffn_grad, w_down(g)) * slope_ref[g]).astype(BF16)
        pre_grad_ref[g] = pre_grad
        if g < half:
            sent += start_copies(
                [(pre_grad_ref.at[g], pre_grad_out.at[g])], sems_out.at[pl.ds(half + g, 1)]
            )
        first_grad = first_grad + mm_nt(pre_grad, w_in(g))
    norm_grads_ref[0:1, :] = jnp.sum(first_grad * normal_one, axis=0, keepdims=True)
    norm_grads_ref[1:2, :] = jnp.sum(first_grad, axis=0, keepdims=True)
    resid_grad = layer_norm_back(normal_one, scale_one, first_grad, gain_one)
    resid_ref[...] = resid_grad
    attn_grad = resid_grad.astype(BF16)
    attn_grad_ref[...] = attn_grad
    for g in range(groups):
        context_grad_refs[g][...] = mm_nt(attn_grad, w_out(g)).astype(BF16)
    sorted_weight_grads(
        place_ref,
        [ref[...] for ref in context_refs[half:]],
        first_low,
        lambda j: act_ref[half + j],
        lambda j: pre_grad_ref[half + j],
        ffn_grad,
        attn_grad,
        late_refs,
        late_scratch,
    )
    wait_copies(sent)


def gather_copies(piece_refs, packed_vmem, out_vmem, replica, sem):
    out_copies, copies = [], []
    kept = packed_vmem.shape[2]
    for (group, relatives, firsts, rows), ref in zip(GATHERED, piece_refs):
        for i, relative in enumerate(relatives):
            chunk = jnp.bitwise_xor(replica, relative)
            first = firsts[i]
            main = min(first + rows, kept) - first
            copies.append(
                pltpu.make_async_copy(
                    ref.at[i, pl.ds(0, main), :],
                    packed_vmem.at[group - 1, chunk, pl.ds(first, main), :],
                    sem.at[len(copies)],
                )
            )
            if main < rows:
                out_copies.append(
                    pltpu.make_async_copy(
                        ref.at[i, pl.ds(main, rows - main), :],
                        out_vmem.at[group - 1, chunk],
                        sem.at[32 + len(out_copies)],
                    )
                )
    return out_copies, copies


def reached(axes):
    order = (0,)
    for bit in axes:
        order = order + tuple(relative + bit for relative in order)
    return order


def gathered_layout():
    layout = []
    for group, axes in ((1, (ACROSS_Y, ACROSS_X)), (2, (ACROSS_X, ACROSS_Y))):
        for core in (0, CORE):
            layout += [(group, (core, core + axes[0]), (0, 0), 2 * HALF_ROWS)]
            layout += [(group, (core + axes[1], core + sum(axes)), (0, 0), 2 * HALF_ROWS)]
    halves = ((0, (ACROSS_Y, ACROSS_X)), (HALF_ROWS, (ACROSS_X, ACROSS_Y)))
    for core in (0, CORE):
        both = tuple((core + r, first) for first, axes in halves for r in reached(axes))
        layout += [(3, tuple(r for r, first in both), tuple(first for r, first in both), HALF_ROWS)]
    return layout


ROW_ORDER = reached((ACROSS_Y, ACROSS_X, CORE))
HALF_ROWS = 112
GATHERED = gathered_layout()


def across(array, bit):
    return lax.ppermute(array, "dp", [(i, i ^ bit) for i in range(CHUNKS)])


def nearby(arrays):
    ways = (ACROSS_Y, ACROSS_X, ACROSS_Y + ACROSS_X)
    return [arrays[0]] + [across(array, way) for array, way in zip(arrays[1:], ways)]


def together(*values):
    return lax.optimization_barrier(values)


def token_layer(place, contexts, hidden, out_grad, norms, w_rows, pieces):
    tokens, width = hidden.shape
    local = contexts[0].shape[1]
    units = w_rows[0].shape[1]
    groups = len(contexts)
    rows = width // CHUNKS + units // CHUNKS + OUT_ROWS
    return kernel_call(
        token_kernel,
        "token_layer",
        15_000_000_000,
        18_000_000,
        40,
        in_specs=[SCALARS]
        + [IN_VMEM] * (groups + 6)
        + [ANYWHERE] * len(pieces),
        out_specs=[IN_VMEM] * 3 + [IN_HBM] * 2 + [IN_VMEM] * (3 + groups) + [IN_HBM] * 2,
        out_shape=[
            Shape((tokens, width), BF16),
            Shape((tokens, width), F32),
            Shape((tokens, width), BF16),
            hbm_shape((groups // 2, tokens, units), BF16),
            hbm_shape((groups // 2, tokens, units), BF16),
            Shape((tokens, width), BF16),
            Shape((tokens, width), BF16),
            Shape((8, width), F32),
        ]
        + [Shape((tokens, local), BF16)] * groups
        + [hbm_shape((2, CHUNKS // 2, rows, width), BF16)] * 2,
        scratch_shapes=[
            pltpu.VMEM((groups - 1, CHUNKS, rows - OUT_ROWS, width), BF16),
            pltpu.VMEM((groups - 1, CHUNKS, OUT_ROWS, width), BF16),
            pltpu.VMEM((groups, tokens, units), F32),
            pltpu.SemaphoreType.DMA((56,)),
            pltpu.VMEM((groups, tokens, units), BF16),
            pltpu.VMEM((groups, tokens, units), BF16),
            pltpu.SemaphoreType.DMA((groups,)),
        ]
        + weight_grad_scratch(width, units, rows),
    )(place, *contexts, hidden, out_grad, norms, *w_rows, *pieces)


def sorted_weight_grads(
    place_ref, contexts, first_low, act_of, pre_grad_of, ffn_grad, attn_grad, out_refs, scratch
):
    in_ref, down_ref, last_ref, sorted_ref, sems = scratch
    local = contexts[0].shape[1]
    width_rows = in_ref.shape[0] // CHUNKS
    unit_rows = down_ref.shape[0] // CHUNKS
    rows = width_rows + unit_rows
    last_ref[local:, :] = jnp.zeros((last_ref.shape[0] - local, last_ref.shape[1]), BF16)
    copies = []
    for j, axes in enumerate(PART_AXES):
        last_ref[:local, :] = mm_tn(contexts[j], attn_grad).astype(BF16)
        in_ref[...] = mm_tn(first_low, pre_grad_of(j)).astype(BF16)
        down_ref[...] = mm_tn(act_of(j), ffn_grad).astype(BF16)
        for side, core in ((1, CORE), (0, 0)):
            for slot, relative in enumerate(reached(axes[::-1])):
                chunk = jnp.bitwise_xor(relative + core, place_ref[1])
                at = pl.multiple_of(chunk * width_rows, 16)
                sorted_ref[side, j, slot, :width_rows] = in_ref[pl.ds(at, width_rows), :]
                at = pl.multiple_of(chunk * unit_rows, 16)
                sorted_ref[side, j, slot, width_rows:rows] = down_ref[pl.ds(at, unit_rows), :]
                at = pl.multiple_of(chunk * OUT_ROWS, 16)
                sorted_ref[side, j, slot, rows:] = last_ref[pl.ds(at, OUT_ROWS), :]
            copies += start_copies(
                [(sorted_ref.at[side, j], out_refs[side].at[j])], sems.at[pl.ds(2 * side + j, 1)]
            )
    wait_copies(copies)


def weight_grad_scratch(width, units, rows):
    return [
        pltpu.VMEM((width, width), BF16),
        pltpu.VMEM((units, width), BF16),
        pltpu.VMEM((CHUNKS * OUT_ROWS, width), BF16),
        pltpu.VMEM((2, 2, CHUNKS // 2, rows, width), BF16),
        pltpu.SemaphoreType.DMA((4,)),
    ]


def weight_grad_kernel(place_ref, *refs):
    context_refs, refs = refs[:2], refs[2:]
    first_low_ref, act_hbm, pre_grad_hbm, ffn_grad_ref, attn_grad_ref, *out_refs = refs[:7]
    scratch, (act_ref, pre_grad_ref, sems_in) = refs[7:12], refs[12:]
    arriving = start_copies(
        [
            (source.at[j], target.at[j])
            for j in range(2)
            for source, target in ((pre_grad_hbm, pre_grad_ref), (act_hbm, act_ref))
        ],
        sems_in,
    )

    def act_of(j):
        arriving[2 * j + 1].wait()
        return act_ref[j]

    def pre_grad_of(j):
        arriving[2 * j].wait()
        return pre_grad_ref[j]

    sorted_weight_grads(
        place_ref,
        [ref[...] for ref in context_refs],
        first_low_ref[...],
        act_of,
        pre_grad_of,
        ffn_grad_ref[...],
        attn_grad_ref[...],
        out_refs,
        scratch,
    )


def weight_grads(place, contexts, first_low, act, pre_grad, ffn_grad, attn_grad):
    tokens, units = act.shape[1:]
    width = first_low.shape[1]
    rows = width // CHUNKS + units // CHUNKS + OUT_ROWS
    return kernel_call(
        weight_grad_kernel,
        "weight_grads",
        4_000_000_000,
        7_000_000,
        15,
        in_specs=[SCALARS] + [IN_VMEM] * 3 + [IN_HBM] * 2 + [IN_VMEM] * 2,
        out_specs=[IN_HBM] * 2,
        out_shape=[hbm_shape((2, CHUNKS // 2, rows, width), BF16)] * 2,
        scratch_shapes=weight_grad_scratch(width, units, rows)
        + [
            pltpu.VMEM((2, tokens, units), BF16),
            pltpu.VMEM((2, tokens, units), BF16),
            pltpu.SemaphoreType.DMA((4,)),
        ],
    )(place, *contexts[:2], first_low, *in_hbm(act, pre_grad), ffn_grad, attn_grad)


def add(left, right):
    return (left.astype(F32) + right.astype(F32)).astype(BF16)


def total_of(arrays):
    return sum(array.astype(F32) for array in arrays).astype(BF16)


def reorder_kernel(place_ref, *refs):
    out_ref = refs[-1]
    groups = out_ref.shape[1]
    blocks = out_ref.shape[0]
    per = len(refs[:-1]) // groups
    for shift in range(groups):
        origin = jnp.bitwise_xor(place_ref[0], shift)
        for b in range(blocks):
            if per == 1:
                out_ref[b, origin] = refs[shift][b * TILE : (b + 1) * TILE, :]
            else:
                out_ref[b, origin] = refs[b * groups + shift][...]


def reorder(place, pieces, blocks):
    width = pieces[0].shape[1]
    groups = SEQMAX // TILE
    out = kernel_call(
        reorder_kernel,
        "reorder",
        0,
        3_000_000,
        8,
        in_specs=[SCALARS] + [IN_VMEM] * len(pieces),
        out_specs=IN_VMEM,
        out_shape=Shape((blocks, groups, TILE, width), BF16),
    )(place, *pieces)
    return out.reshape(blocks * SEQMAX, width)


def unpack_kernel(place_ref, *refs):
    piece_refs, refs = refs[:2], refs[2:]
    grad_in_ref, grad_down_ref, grad_out_ref, q_ref, k_ref, v_ref, all_ref = refs
    local = q_ref.shape[0]
    width_rows = grad_in_ref.shape[0] // CHUNKS
    unit_rows = grad_down_ref.shape[0] // CHUNKS
    row_rows = all_ref.shape[0] // CHUNKS
    out_at = width_rows + unit_rows
    rows_at = out_at + OUT_ROWS
    for slot, relative in enumerate(ROW_ORDER):
        ref = piece_refs[slot // 4].at[slot % 4]
        chunk = jnp.bitwise_xor(place_ref[1], relative)
        at = pl.multiple_of(chunk * width_rows, 8)
        grad_in_ref[pl.ds(at, width_rows), :] = ref[:width_rows, :].astype(F32)
        at = pl.multiple_of(chunk * unit_rows, 8)
        grad_down_ref[pl.ds(at, unit_rows), :] = ref[width_rows:out_at, :].astype(F32)
        at = pl.multiple_of(chunk * row_rows, 8)
        all_ref[pl.ds(at, row_rows), :] = ref[rows_at:, :].astype(F32)

        @pl.when(chunk * OUT_ROWS < grad_out_ref.shape[0])
        def out_rows(chunk=chunk, ref=ref):
            at = pl.multiple_of(chunk * OUT_ROWS, 8)
            grad_out_ref[pl.ds(at, OUT_ROWS), :] = ref[out_at:rows_at, :].astype(F32)

    for i, ref in enumerate((q_ref, k_ref, v_ref)):
        ref[...] = all_ref[i * local : (i + 1) * local, :]


def unpack(place, pieces, width, units, local):
    return kernel_call(
        unpack_kernel,
        "unpack",
        0,
        12_000_000,
        10,
        in_specs=[SCALARS] + [IN_VMEM] * 2,
        out_specs=[IN_VMEM] * 6,
        out_shape=[Shape((width, width), F32), Shape((units, width), F32)]
        + [Shape((local, width), F32)] * 4,
        scratch_shapes=[pltpu.VMEM((3 * local, width), F32)],
    )(place, *pieces)


def small_kernel(place_ref, *refs):
    piece_refs, table_ref, norm_refs, norms_ref = refs[:-6], refs[-6], refs[-5:-1], refs[-1]
    table_rows = table_ref.shape[0] // CHUNKS
    rows = table_rows + SMALL_ROWS
    columns = norms_ref.shape[1]
    per = CHUNKS // len(piece_refs)
    for slot, relative in enumerate(ROW_ORDER):
        ref, first = piece_refs[slot // per], slot % per * rows
        chunk = jnp.bitwise_xor(place_ref[1], relative)
        at = pl.multiple_of(chunk * table_rows, 8)
        table_ref[pl.ds(at, table_rows), :] = ref[first : first + table_rows, :].astype(F32)
        low = ref[first + table_rows : first + rows, :columns].astype(F32)
        norms_ref[pl.ds(chunk, 1), :] = low[:1]
    for i, ref in enumerate(norm_refs):
        ref[:columns] = norms_ref[2 * i, :]
        ref[columns:] = norms_ref[2 * i + 1, :]


def small_unpack(place, small, width, buckets):
    return kernel_call(
        small_kernel,
        "small_unpack",
        0,
        3_000_000,
        8,
        in_specs=[SCALARS] + [IN_VMEM] * len(small),
        out_specs=[IN_VMEM] * 5,
        out_shape=[Shape((buckets, width), F32)] + [Shape((width,), F32)] * 4,
        scratch_shapes=[pltpu.VMEM((CHUNKS, 4 * width // CHUNKS), F32)],
    )(place, *small)


def send(array, bits):
    return lax.ppermute(array, "tensor", [(i, i ^ bits) for i in range(SEQMAX // TILE)])


def exchange(pieces):
    return [pieces[0]] + [send(piece, r) for r, piece in enumerate(pieces) if r > 0]


def second_exchange(context, got):
    near = send(jnp.concatenate([context[1], got[1:]], 0), 1)
    return [context[0][0], near[0], got[0], near[1]]


def spread(array):
    near, far = send(array, 1), send(array, 2)
    return [array, near, far, send(far, 1)]


def shards(
    n_dp,
    n_tensor,
    hidden,
    out_grad,
    w_query,
    w_key,
    w_value,
    w_out,
    w_in,
    w_down,
    bucket_table,
    gain_one,
    bias_one,
    gain_two,
    bias_two,
    rel_buckets,
    group_counts,
    key_mask,
):
    tokens, width = hidden.shape
    local = w_query.shape[1]
    units = w_in.shape[1]
    buckets = bucket_table.shape[0]
    blocks = tokens // SEQMAX
    mine = tokens // n_tensor
    by_axis = n_dp == CHUNKS
    me = lax.axis_index("tensor")
    replica = lax.axis_index("dp") if by_axis else jnp.int32(0)
    place = jnp.stack([me, replica]).astype(jnp.int32)
    rel_rows = offset_rows(rel_buckets)
    width_rows, unit_rows = width // CHUNKS, units // CHUNKS
    padded = jnp.pad(w_out, ((0, CHUNKS * OUT_ROWS - local), (0, 0)))

    w_rows = (w_query.T, w_key.T, w_value.T)

    def my_rows(array):
        array = array.reshape(blocks, n_tensor, TILE, width)
        return lax.dynamic_index_in_dim(array, me, 1, keepdims=False).reshape(mine, width)

    def forward(block, context):
        weights, *context = forward_attention(
            block, place, group_counts, tables, rows, key_mask, context
        )
        return weights, context

    if by_axis:
        piece = own_piece(place, w_in, w_down, w_out)
        near, far = send(piece, 1), send(piece, 2)
        (*tables, q, k, v), saved = prepare(*w_rows, bucket_table, rel_rows, hidden)
        rows = (q, k, v)
        my_hidden, my_out_grad = my_rows(hidden), my_rows(out_grad)
        near, far, tables, rows, saved, my_hidden, my_out_grad = together(
            near, far, tables, rows, saved, my_hidden, my_out_grad
        )
        last = send(far, 1)
        near_y, far_x = across(near[None], ACROSS_Y), across(far[None], ACROSS_X)
        kept_0, context = forward(0, [])
        near, far, near_y, far_x, last, kept_0, context, tables, rows = together(
            near, far, near_y, far_x, last, kept_0, context, tables, rows
        )
        near = jnp.concatenate([near[None], near_y], 0)
        far = jnp.concatenate([far[None], far_x], 0)
        near_x, far_y = across(near, ACROSS_X), across(far, ACROSS_Y)
        top, low = last[None, :HALF_ROWS], last[None, HALF_ROWS:]
        top_y, low_x = across(top, ACROSS_Y), across(low, ACROSS_X)
        kept_1, context = forward(1, context)
        got = send(context[2], 2)
        near, near_x, far, far_y, top, top_y, low, low_x, context, got, kept_0, kept_1 = together(
            near, near_x, far, far_y, top, top_y, low, low_x, context, got, kept_0, kept_1
        )
        contexts = second_exchange(context, got)
        top = jnp.concatenate([top, top_y], 0)
        low = jnp.concatenate([low, low_x], 0)
        top_x, low_y = across(top, ACROSS_X), across(low, ACROSS_Y)
        cores = [across(near, CORE), across(near_x, CORE)]
        near, near_x, cores, far, far_y, top, top_x, low, low_y, contexts, kept_0, kept_1 = (
            together(
                near, near_x, cores, far, far_y, top, top_x, low, low_y, contexts, kept_0, kept_1
            )
        )
        both = jnp.concatenate([top, top_x, low, low_y], 0)
        gathered = [near, near_x, *cores]
        gathered += [far, far_y, across(far, CORE), across(far_y, CORE)]
        gathered += [both, across(both, CORE)]
    else:
        (*tables, q, k, v), saved = prepare(*w_rows, bucket_table, rel_rows, hidden)
        rows = (q, k, v)
        stacked = jnp.concatenate(
            [
                w_in.reshape(CHUNKS, width_rows, width),
                w_down.reshape(CHUNKS, unit_rows, width),
                padded.reshape(CHUNKS, OUT_ROWS, width),
            ],
            1,
        )
        sent = spread(stacked)
        gathered = [
            jnp.stack(
                [
                    sent[group][chunk, at : at + rows]
                    for chunk, at in zip(chunks, first)
                ]
            )
            for group, chunks, first, rows in GATHERED
        ]
        kept_0, context = forward(0, [])
        kept_1, context = forward(1, context)
        contexts = second_exchange(context, send(context[2], 2))
        my_hidden, my_out_grad = my_rows(hidden), my_rows(out_grad)
    *tables, q, k, v = saved
    norms = jnp.stack([gain_one, bias_one, gain_two, bias_two])
    (
        output, resid_grad, first_low, act, pre_grad, ffn_grad, attn_grad, norm_grads, *back,
        late_keep, late_give,
    ) = token_layer(
        place, contexts, my_hidden, my_out_grad, norms, (w_in, w_down, w_out), gathered
    )
    norm_grads = norm_grads[:4].reshape(CHUNKS, 4 * width // CHUNKS)

    def backward(block, kept, before):
        own, near, far, *before = backward_attention(
            block, blocks, place, back, (q, k, v), kept, tables, hidden, w_rows, bucket_table, rel_rows,
            norm_grads, before,
        )
        return [own, near, far], before

    keep_1, give_1 = late_keep, late_give
    back = exchange(back)
    core_1 = across(give_1, CORE) if by_axis else give_1
    keep_0, give_0 = weight_grads(
        place, contexts, first_low, act, pre_grad, ffn_grad, attn_grad
    )

    def first_sums(keep, got):
        return [add(keep[j, 2:], got[j, 2:]) for j in range(2)]

    sums_1 = first_sums(keep_1, core_1) if by_axis else []
    (
        back, core_1, sums_1, keep_0, give_0, keep_1, output, resid_grad, norm_grads, kept_0,
        kept_1, tables, place,
    ) = together(
        back, core_1, sums_1, keep_0, give_0, keep_1, output, resid_grad, norm_grads, kept_0,
        kept_1, tables, place,
    )
    back = [piece.reshape(blocks, TILE, local) for piece in back]

    def first_stage(sums):
        return [across(part, axes[0]) for part, axes in zip(sums, PART_AXES)]

    def second_stage(keep, got, first):
        given = [
            total_of([keep[j, 1:2], got[j, 1:2], first[j][1:2]]) for j in range(2)
        ]
        kept = [[keep[j, 0], got[j, 0], first[j][0]] for j in range(2)]
        return kept, [across(part, axes[1]) for part, axes in zip(given, PART_AXES)]

    def joint(arrays, way):
        rows = [array.shape[0] for array in arrays]
        got = send(jnp.concatenate(arrays, 0), way)
        return [got[sum(rows[:i]) : sum(rows[: i + 1])] for i in range(len(rows))]

    stage_1, core_0 = [], give_0
    if by_axis:
        stage_1 = first_stage(sums_1)
        core_0 = across(give_0, CORE)
    out_near, out_far = send(output, 1), send(output, 2)
    parts, before = backward(0, kept_0, ())
    (
        parts, before, stage_1, core_0, core_1, keep_0, keep_1, out_near, out_far, output,
        resid_grad, norm_grads, kept_1, tables, place, back,
    ) = together(
        parts, before, stage_1, core_0, core_1, keep_0, keep_1, out_near, out_far, output,
        resid_grad, norm_grads, kept_1, tables, place, back,
    )
    stage_0 = first_stage(first_sums(keep_0, core_0)) if by_axis else []
    late = second_stage(keep_1, core_1, stage_1) if by_axis else []
    near, out_last = joint([parts[1], out_far], 1)
    parts = [parts[0], near, parts[2]]
    parts_1, before = backward(1, kept_1, before)
    parts, parts_1, before, stage_0, late, core_0, keep_0, out_last, resid_grad = together(
        parts, parts_1, before, stage_0, late, core_0, keep_0, out_last, resid_grad
    )
    def total(block, pieces):
        wide = resid_grad[block * TILE : (block + 1) * TILE]
        for piece in pieces:
            wide = wide + piece.astype(F32)
        return wide.astype(BF16)

    keep, give = before
    thirds, sums = [], keep
    if not by_axis:
        joined = lax.psum(jnp.concatenate([keep, give], 0).astype(F32), "dp").astype(BF16)
    if by_axis:
        thirds = [second_stage(keep_0, core_0, stage_0), late]
        sums = add(keep, across(give, CORE))
    far_0 = send(add(parts[2], parts[1][TILE:]), 2)
    near_1 = send(parts_1[1], 1)
    grad_0 = total(0, [parts[0], parts[1][:TILE], far_0])
    sum_1 = add(parts_1[2], near_1[TILE:])
    grad_0, sum_1, parts_1, near_1, thirds, sums, resid_grad, out_last = together(
        grad_0, sum_1, parts_1, near_1, thirds, sums, resid_grad, out_last
    )

    output = reorder(place, [output, out_near, out_far, out_last], blocks)
    shard, near_0 = [], [grad_0]
    if by_axis:
        for kept, got in thirds:
            shard += [total_of([*kept[j], got[j][0]]) for j in range(2)]
        near_0 = near_0 + [shard[3]]
        joined = total_of(nearby([sums[i : i + 1] for i in range(CHUNKS // 2)]))
    near_0 = joint(near_0, 1)
    far_0, far_1 = joint([grad_0, sum_1], 2)
    pos_rows = buckets // CHUNKS // 2
    slots = joined.shape[0]
    row_grads = joined[:, pos_rows + SMALL_ROWS :]
    pos = joined[:, :pos_rows]
    pos = jnp.concatenate([pos[:, :, : 2 * local], pos[:, :, 2 * local :]], 1)
    w_table = jnp.concatenate([w_rows[1], w_rows[0]], 0)
    table_part = mm(pos.reshape(slots * 2 * pos_rows, 2 * local), w_table)
    table_part = table_part.astype(BF16).reshape(slots, 2 * pos_rows, width)
    small = jnp.concatenate([table_part, joined[:, pos_rows : pos_rows + SMALL_ROWS]], 1)
    small_rows = small.shape[1]
    small = small.reshape(slots * small_rows, width)
    grad_0, near_0, far_0, far_1, near_1, parts_1, resid_grad, output, shard, small, row_grads = (
        together(
            grad_0, near_0, far_0, far_1, near_1, parts_1, resid_grad, output, shard, small,
            row_grads,
        )
    )
    grad_1 = total(1, [parts_1[0], near_1[:TILE], far_1])
    shard_far = []
    if by_axis:
        shard_1, small_near = joint([shard[1], small], 1)
        shard_far = [shard_1, send(add(shard[2], near_0[1]), 2)]
    else:
        small_near = send(small, 1)
    small = add(small, small_near)
    if by_axis:
        row_grads = nearby([row_grads[0]] * 4)
    grad_0, near_0, far_0, grad_1, row_grads, small, shard, shard_far = together(
        grad_0, near_0, far_0, grad_1, row_grads, small, shard, shard_far
    )
    near_1, last_0 = joint([grad_1, far_0], 1)
    far_1, small_far = joint([grad_1, small], 2)
    small = add(small, small_far)
    if by_axis:
        shard = total_of([shard[0], *shard_far])
        pieces = nearby([shard] * 4)
        grad_0, near_0, far_0, last_0, grad_1, near_1, far_1, small, pieces, row_grads = together(
            grad_0, near_0, far_0, last_0, grad_1, near_1, far_1, small, pieces, row_grads
        )
        pieces = [jnp.concatenate(pair, 0) for pair in zip(pieces, row_grads)]
        pieces = jnp.stack(pieces)
        pieces = [pieces, across(pieces, CORE)]
        small = nearby([small] * 4)
    else:
        natural = []
        for keep, give in ((keep_0, give_0), (keep_1, give_1)):
            for j, axes in enumerate(PART_AXES):
                chunks = reached(axes[::-1] + (CORE,))
                both = jnp.concatenate([keep[j], give[j]], 0)
                natural.append(jnp.stack([both[chunks.index(c)] for c in range(CHUNKS)]))
        shard = jnp.stack(exchange(natural)).astype(F32)
        shard = lax.psum(sum(shard[r] for r in range(n_tensor)), "dp").astype(BF16)
        pieces = jnp.stack(
            [
                jnp.concatenate([shard[chunk], row_grads[slot]], 0)
                for slot, chunk in enumerate(ROW_ORDER)
            ]
        )
        pieces = [pieces[:4], pieces[4:]]
        small = [small]
    last_1 = send(far_1, 1)
    grad_hidden = reorder(
        place, [grad_0, near_0[0], far_0, last_0, grad_1, near_1, far_1, last_1], blocks
    )
    if by_axis:
        grad_hidden, small, pieces = together(grad_hidden, small, pieces)
        small = jnp.concatenate(small, 0)
        small = [small, across(small, CORE)]
    grad_in, grad_down, grad_out, grad_query, grad_key, grad_value = unpack(
        place, pieces, width, units, local
    )
    if by_axis:
        small, grad_hidden, grad_in, grad_down, grad_out, grad_query, grad_key, grad_value = (
            together(
                small, grad_hidden, grad_in, grad_down, grad_out, grad_query, grad_key, grad_value
            )
        )
    grad_table, *norm_grads = small_unpack(place, small, width, buckets)
    return (
        output,
        grad_hidden,
        grad_query.T,
        grad_key.T,
        grad_value.T,
        grad_out,
        grad_in,
        grad_down,
        grad_table,
        *norm_grads,
    )


def solution(mesh):
    in_specs = (
        P("dp", None),
        P("dp", None),
        P(None, "tensor"),
        P(None, "tensor"),
        P(None, "tensor"),
        P("tensor", None),
        P(None, "tensor"),
        P("tensor", None),
        P(),
        P(),
        P(),
        P(),
        P(),
        P(),
        P("dp", None),
        P("dp"),
    )
    out_specs = (
        P("dp", None),
        P("dp", None),
        P(None, "tensor"),
        P(None, "tensor"),
        P(None, "tensor"),
        P("tensor", None),
        P(None, "tensor"),
        P("tensor", None),
        P(),
        P(),
        P(),
        P(),
        P(),
    )
    body = functools.partial(shards, mesh.shape["dp"], mesh.shape["tensor"])
    return jax.shard_map(body, mesh=mesh, in_specs=in_specs, out_specs=out_specs, check_vma=False)
```

```python
import functools
import math

import jax
import jax.numpy as jnp
from jax import lax
from jax.experimental import pallas as pl
from jax.experimental.pallas import tpu as pltpu
from jax.sharding import PartitionSpec as P

NORM_EPS = 1e-07
HEAD_DIM = 64
SEQMAX = 512
TILE = 128
WINDOW = SEQMAX + TILE
OFFSETS = 2 * SEQMAX
NEGATIVE = -1e30
CHUNKS = 8
CORE, ACROSS_X, ACROSS_Y = 1, 2, 4
OUT_ROWS = 32
SMALL_ROWS = 16
F32 = jnp.float32
BF16 = jnp.bfloat16


def score_factor():
    return 1.0 / math.sqrt(3.0 * HEAD_DIM)


def mm(left, right):
    return jnp.dot(left, right, preferred_element_type=F32)


def mm_nt(left, right):
    return lax.dot_general(left, right, (((1,), (1,)), ((), ())), preferred_element_type=F32)


def mm_tn(left, right):
    return lax.dot_general(left, right, (((0,), (0,)), ((), ())), preferred_element_type=F32)


def starts_of(places, counts_ref):
    long_end = SEQMAX * counts_ref[0, 0]
    mid_end = long_end + SEQMAX // 2 * counts_ref[0, 1]
    in_long = places < long_end
    in_mid = places < mid_end
    anchor = jnp.where(in_long, 0, jnp.where(in_mid, long_end, mid_end))
    shift = jnp.where(in_long, 9, jnp.where(in_mid, 8, 7))
    return anchor + lax.shift_left(lax.shift_right_logical(places - anchor, shift), shift)


def tile_iotas():
    rows = lax.broadcasted_iota(jnp.int32, (TILE, TILE), 0)
    lanes = lax.broadcasted_iota(jnp.int32, (TILE, TILE), 1)
    return rows, lanes


def lane_tiles(wide):
    return [wide[:, c : c + TILE] for c in range(0, wide.shape[1], TILE)]


def skew(wide):
    rows, lanes = tile_iotas()
    keep = lanes <= rows
    turned = [pltpu.roll(part, 1, 1, stride=1, stride_axis=0) for part in lane_tiles(wide)]
    return jnp.concatenate(
        [jnp.where(keep, turned[c], turned[c + 1]) for c in range(len(turned) - 1)], axis=1
    )


def unskew(flipped):
    rows, lanes = tile_iotas()
    late = lanes > rows
    turned = [pltpu.roll(part, 1, 1, stride=1, stride_axis=0) for part in lane_tiles(flipped)]
    zero = jnp.zeros((TILE, TILE), F32)
    turned = [zero] + turned + [zero]
    return jnp.concatenate(
        [jnp.where(late, turned[c], turned[c + 1]) for c in range(len(turned) - 1)], axis=1
    )


def window_of(tile_at):
    low = SEQMAX - TILE - tile_at
    return slice(low, low + WINDOW)


def one_hot_columns(rel_ref, row, buckets):
    ids = lax.broadcasted_iota(jnp.int32, (buckets, OFFSETS), 0)
    return (ids == rel_ref[row : row + 1, :]).astype(BF16)


def split_low(wide):
    high = wide.astype(BF16)
    return high, (wide - high.astype(F32)).astype(BF16)


SCALARS = pl.BlockSpec(memory_space=pltpu.SMEM)
ANYWHERE = pl.BlockSpec(memory_space=pl.ANY)
IN_HBM = pl.BlockSpec(memory_space=pltpu.HBM)
IN_VMEM = pl.BlockSpec(memory_space=pltpu.VMEM)
Shape = jax.ShapeDtypeStruct


def in_hbm(*arrays):
    return [pltpu.with_memory_space_constraint(array, pltpu.HBM) for array in arrays]


def hbm_shape(shape, kind):
    return pltpu.HBM(shape, kind)


def kernel_call(kernel, name, flops, moved, vmem, **rest):
    return pl.pallas_call(
        kernel,
        compiler_params=pltpu.CompilerParams(vmem_limit_bytes=vmem * 2**20),
        cost_estimate=pl.CostEstimate(flops=flops, bytes_accessed=moved, transcendentals=0),
        name=name,
        **rest,
    )


PART_AXES = ((ACROSS_Y, ACROSS_X), (ACROSS_X, ACROSS_Y))


def start_copies(pairs, sems):
    copies = [
        pltpu.make_async_copy(source, target, sems.at[i]) for i, (source, target) in enumerate(pairs)
    ]
    for copy in copies:
        copy.start()
    return copies


def wait_copies(copies):
    for copy in copies:
        copy.wait()


def prepare_kernel(
    wq_ref, wk_ref, wv_ref, table_ref, rel_ref, hidden_ref, pk_ref, pq_ref, q_ref, k_ref, v_ref,
    pk_back_out, pq_back_out, q_out, k_out, v_out, pk_back, pq_back, sems,
):
    table = table_ref[...]
    buckets = table.shape[0]
    pos_key = mm_nt(wk_ref[...], table).astype(BF16)
    pos_query = mm_nt(wq_ref[...], table).astype(BF16)
    plain = one_hot_columns(rel_ref, 0, buckets)
    pk_ref[...] = mm(pos_key, plain).astype(BF16)
    pq_ref[...] = mm(pos_query, plain).astype(BF16)
    back = one_hot_columns(rel_ref, 1, buckets)
    pk_back[...] = mm(pos_key, back).astype(BF16)
    pq_back[...] = mm(pos_query, back).astype(BF16)
    copies = start_copies([(pk_back, pk_back_out), (pq_back, pq_back_out)], sems)
    hidden = hidden_ref[...]
    for i, (ref, w_ref, out) in enumerate(
        ((q_ref, wq_ref, q_out), (k_ref, wk_ref, k_out), (v_ref, wv_ref, v_out))
    ):
        ref[...] = mm_nt(hidden, w_ref[...]).astype(BF16)
        copies += start_copies([(ref, out)], sems.at[pl.ds(2 + i, 1)])
    wait_copies(copies)


def prepare(w_query, w_key, w_value, table, rel_rows, hidden):
    local = w_query.shape[0]
    tokens = hidden.shape[0]
    table_kind = ((local, OFFSETS), BF16)
    row_kind = ((tokens, local), BF16)
    out = kernel_call(
        prepare_kernel,
        "prepare",
        4_000_000_000,
        6_000_000,
        10,
        in_specs=[IN_VMEM] * 6,
        out_specs=[IN_VMEM] * 5 + [IN_HBM] * 5,
        out_shape=[Shape(*table_kind)] * 2
        + [Shape(*row_kind)] * 3
        + [hbm_shape(*table_kind)] * 2
        + [hbm_shape(*row_kind)] * 3,
        scratch_shapes=[pltpu.VMEM(*table_kind)] * 2 + [pltpu.SemaphoreType.DMA((5,))],
    )(w_query, w_key, w_value, table, rel_rows, hidden)
    return out[:5], out[5:]


def forward_kernel(
    block, place_ref, counts_ref, pk_ref, pq_ref, q_ref, k_ref, v_ref, mask_ref, *rest
):
    before, rest = rest[: 3 if block else 0], rest[3 if block else 0 :]
    weights_out, context_refs, rest = rest[0], rest[1:4], rest[4:]
    context_ref, bias_ref, rel_score_ref, weights_ref, sems_out = rest
    heads = q_ref.shape[1] // HEAD_DIM
    first = block * SEQMAX
    here = slice(first, first + SEQMAX)
    column = starts_of(lax.broadcasted_iota(jnp.int32, (SEQMAX, 1), 0) + first, counts_ref)
    row = starts_of(lax.broadcasted_iota(jnp.int32, (1, SEQMAX), 1) + first, counts_ref)
    row = jnp.where(mask_ref[block] == 1, row, -1)
    bias_ref[...] = jnp.where(column == row, 0.0, NEGATIVE)
    copies = []
    for head in range(heads):
        part = slice(head * HEAD_DIM, (head + 1) * HEAD_DIM)
        queries = q_ref[here, part]
        keys = k_ref[here, part]
        values = v_ref[here, part]
        for at in range(0, SEQMAX, TILE):
            rel = mm(keys[at : at + TILE], pq_ref[part, window_of(at)])
            rel_score_ref[at : at + TILE, :] = skew(rel)
        for at in range(0, SEQMAX, TILE):
            rows = slice(at, at + TILE)
            raw = mm_nt(queries[rows], keys)
            raw = raw + skew(mm(queries[rows], pk_ref[part, window_of(at)]))
            raw = raw + rel_score_ref[:, rows].T
            scaled = raw * score_factor() + bias_ref[rows, :]
            top = jnp.max(scaled, axis=-1, keepdims=True)
            exponent = jnp.exp(scaled - top)
            total = jnp.sum(exponent, axis=-1, keepdims=True)
            weights = (exponent * (1.0 / total)).astype(BF16)
            weights_ref[head, rows, :] = weights
            relative = jnp.bitwise_xor(at // TILE, place_ref[0])
            context_ref[relative, :, part] = mm(weights, values).astype(BF16)
        copies += start_copies(
            [(weights_ref.at[head], weights_out.at[head])], sems_out.at[pl.ds(head, 1)]
        )
    at = 0
    for n, ref in enumerate(context_refs):
        for r in range(ref.shape[0]):
            for b in range(block):
                ref[r, b * TILE : (b + 1) * TILE] = before[n][r, b * TILE : (b + 1) * TILE]
            ref[r, block * TILE : (block + 1) * TILE] = context_ref[at]
            at += 1
    wait_copies(copies)


def forward_attention(block, place, counts, tables, rows, key_mask, context):
    tokens, local = rows[0].shape
    heads = local // HEAD_DIM
    blocks = tokens // SEQMAX
    groups = SEQMAX // TILE
    return kernel_call(
        functools.partial(forward_kernel, block),
        f"attention_forward_{block}",
        10_000_000_000,
        5_000_000,
        12,
        in_specs=[SCALARS] * 2 + [IN_VMEM] * (6 + len(context)),
        out_specs=[IN_HBM] + [IN_VMEM] * 3,
        out_shape=[hbm_shape((heads, SEQMAX, SEQMAX), BF16)]
        + [Shape((n, (block + 1) * TILE, local), BF16) for n in (1, 1, 2)],
        scratch_shapes=[pltpu.VMEM((groups, TILE, local), BF16)]
        + [pltpu.VMEM((SEQMAX, SEQMAX), F32)] * 2
        + [pltpu.VMEM((heads, SEQMAX, SEQMAX), BF16), pltpu.SemaphoreType.DMA((heads,))],
    )(place, counts, *tables, *rows, key_mask.reshape(blocks, 1, SEQMAX), *context)


def backward_kernel(block, blocks, place_ref, *refs):
    groups = SEQMAX // TILE
    cg_refs, refs = refs[:groups], refs[groups:]
    q_hbm, k_hbm, v_hbm, weights_hbm, pk_hbm, pq_hbm, hidden_hbm = refs[:7]
    w_hbms, table_hbm, rel_ref, norms_ref = refs[7:10], *refs[10:13]
    refs = refs[13:]
    before, refs = (refs[:3], refs[3:]) if block > 0 else (None, refs)
    q_ref, k_ref, v_ref, weights_ref, pk_back_ref, pq_back_ref, hidden_ref = refs[-12:-5]
    wq_ref, wk_ref, wv_ref, table_ref, sems = refs[-5:]
    refs = refs[:-12]
    local = wq_ref.shape[0]
    heads = local // HEAD_DIM
    buckets = table_ref.shape[0]
    if block < blocks - 1:
        part_refs, refs = refs[:3], refs[3:]
        rg_key_ref, rg_query_ref, sum_ref, cg_ref, ds_ref, rows_ref, part_ref = refs
    else:
        part_refs, joined_refs, refs = refs[:3], refs[3:5], refs[5:]
        cg_ref, ds_ref, rows_ref, part_ref, rg_key_ref, rg_query_ref, sum_ref, joined_ref = refs
    first = block * SEQMAX
    copies = start_copies(
        [
            (q_hbm.at[pl.ds(first, SEQMAX), :], q_ref),
            (k_hbm.at[pl.ds(first, SEQMAX), :], k_ref),
            (v_hbm.at[pl.ds(first, SEQMAX), :], v_ref),
            (weights_hbm, weights_ref),
            (pk_hbm, pk_back_ref),
            (pq_hbm, pq_back_ref),
            (hidden_hbm.at[pl.ds(first, SEQMAX), :], hidden_ref),
            (w_hbms[0], wq_ref),
            (w_hbms[1], wk_ref),
            (w_hbms[2], wv_ref),
        ]
        + ([(table_hbm, table_ref)] if block == blocks - 1 else []),
        sems,
    )
    if before is None:
        rg_key_ref[...] = jnp.zeros_like(rg_key_ref)
        rg_query_ref[...] = jnp.zeros_like(rg_query_ref)
    else:
        rg_key_ref[...] = before[0][...]
        rg_query_ref[...] = before[1][...]
    me = place_ref[0]
    for relative in range(groups):
        cg_ref[jnp.bitwise_xor(me, relative)] = cg_refs[relative][block]
    wait_copies(copies[:6])

    tile_rows, tile_lanes = tile_iotas()
    flip = (tile_rows + tile_lanes == TILE - 1).astype(BF16)

    def flipped(low):
        return jnp.concatenate([mm(part, flip) for part in lane_tiles(low)], axis=1)

    for head in range(heads):
        part = slice(head * HEAD_DIM, (head + 1) * HEAD_DIM)
        at_k = slice(local + head * HEAD_DIM, local + (head + 1) * HEAD_DIM)
        at_v = slice(2 * local + head * HEAD_DIM, 2 * local + (head + 1) * HEAD_DIM)
        queries = q_ref[:, part]
        keys = k_ref[:, part]
        values = v_ref[:, part]
        value_grad = jnp.zeros((SEQMAX, HEAD_DIM), F32)
        for at in range(0, SEQMAX, TILE):
            rows = slice(at, at + TILE)
            cotangent = cg_ref[at // TILE, :, part]
            low_weights = weights_ref[head, rows, :]
            weights = low_weights.astype(F32)
            weight_grad = mm_nt(cotangent, values)
            inner = jnp.sum(weights * weight_grad, axis=-1, keepdims=True)
            score_grad = (weights * (weight_grad - inner) * score_factor()).astype(BF16)
            ds_ref[rows, :] = score_grad
            value_grad = value_grad + mm_tn(low_weights, cotangent)
            by_offset = unskew(flipped(score_grad)).astype(BF16)
            window = window_of(at)
            query_grad = mm(score_grad, keys) + mm_nt(by_offset, pk_back_ref[part, window])
            rows_ref[rows, part] = query_grad.astype(BF16)
            rg_key_ref[part, window] += mm_tn(queries[rows], by_offset)
        rows_ref[:, at_v] = value_grad.astype(BF16)
        for at in range(0, SEQMAX, TILE):
            rows = slice(at, at + TILE)
            turned = ds_ref[:, rows].T
            by_offset = unskew(flipped(turned)).astype(BF16)
            window = window_of(at)
            key_grad = mm(turned, queries) + mm_nt(by_offset, pq_back_ref[part, window])
            rows_ref[rows, at_k] = key_grad.astype(BF16)
            rg_query_ref[part, window] += mm_tn(keys[rows], by_offset)
    wait_copies(copies[6:])
    total = mm(rows_ref[:, :local], wq_ref[...])
    total = total + mm(rows_ref[:, local : 2 * local], wk_ref[...])
    total = total + mm(rows_ref[:, 2 * local :], wv_ref[...])
    for at in range(0, SEQMAX, TILE):
        part_ref[jnp.bitwise_xor(at // TILE, me)] = total[at : at + TILE].astype(BF16)
    part_refs[0][...] = part_ref[0]
    part_refs[1][:TILE, :] = part_ref[1]
    part_refs[1][TILE:, :] = part_ref[3]
    part_refs[2][...] = part_ref[2]
    sums = mm_tn(rows_ref[...], hidden_ref[...])
    sum_ref[...] = sums if before is None else before[2][...] + sums
    if block < blocks - 1:
        return

    back = one_hot_columns(rel_ref, 1, buckets)

    def by_bucket(rg_ref):
        high, low = split_low(rg_ref[...])
        return (mm_nt(high, back) + mm_nt(low, back)).T

    def through_table(grad):
        high, low = split_low(grad)
        return mm_tn(high, table_ref[...]) + mm_tn(low, table_ref[...])

    pos_key = by_bucket(rg_key_ref)
    pos_query = by_bucket(rg_query_ref)
    sum_ref[:local, :] += through_table(pos_query)
    sum_ref[local : 2 * local, :] += through_table(pos_key)
    pos = jnp.concatenate([pos_key, pos_query], axis=1).astype(BF16)
    slots = joined_ref.shape[0]
    row_rows, pos_rows = 3 * local // slots, buckets // slots // 2
    for chunk in range(slots):
        slot = slot_of(jnp.bitwise_xor(chunk, place_ref[1]), (CORE, ACROSS_X, ACROSS_Y))
        at = 2 * chunk * pos_rows
        low = [norms_ref[chunk : chunk + 1, :], jnp.zeros((SMALL_ROWS - 1, 2 * local), F32)]
        low = jnp.concatenate(low, axis=0)
        pieces = [
            jnp.concatenate([pos[at : at + pos_rows], pos[at + pos_rows : at + 2 * pos_rows]], 1),
            jnp.concatenate([low, jnp.zeros_like(low)], axis=1).astype(BF16),
            sum_ref[chunk * row_rows : (chunk + 1) * row_rows, :].astype(BF16),
        ]
        joined_ref[slot] = jnp.concatenate(pieces, axis=0)
    joined_refs[0][...] = joined_ref[: slots // 2]
    joined_refs[1][...] = joined_ref[slots // 2 :]


def slot_of(relative, order):
    slot = 0
    for position, bit in enumerate(order):
        slot = slot + jnp.minimum(jnp.bitwise_and(relative, bit), 1) * (4 >> position)
    return slot


def backward_attention(
    block, blocks, place, context_grads, kept, weights, tables, hidden, w_rows, table, rel_rows,
    norms, before,
):
    width = hidden.shape[1]
    local = w_rows[0].shape[0]
    heads = local // HEAD_DIM
    buckets = table.shape[0]
    groups = SEQMAX // TILE
    last = block == blocks - 1
    parts = [Shape((rows, width), BF16) for rows in (TILE, 2 * TILE, TILE)]
    sums = [(local, OFFSETS), (local, OFFSETS), (3 * local, width)]
    joined_rows = 3 * local // CHUNKS + buckets // CHUNKS // 2 + SMALL_ROWS
    joined = Shape((CHUNKS // 2, joined_rows, width), BF16)
    scratch = [
        pltpu.VMEM((groups, TILE, local), BF16),
        pltpu.VMEM((SEQMAX, SEQMAX), BF16),
        pltpu.VMEM((SEQMAX, 3 * local), BF16),
        pltpu.VMEM((groups, TILE, width), BF16),
    ]
    if last:
        out_shape = parts + [joined] * 2
        scratch = scratch + [pltpu.VMEM(shape, F32) for shape in sums]
        scratch = scratch + [pltpu.VMEM((CHUNKS,) + joined.shape[1:], BF16)]
    else:
        out_shape = parts + [Shape(shape, F32) for shape in sums]
    scratch = scratch + [pltpu.VMEM((SEQMAX, local), BF16)] * 3
    scratch = scratch + [pltpu.VMEM((heads, SEQMAX, SEQMAX), BF16)]
    scratch = scratch + [pltpu.VMEM((local, OFFSETS), BF16)] * 2
    scratch = scratch + [pltpu.VMEM((SEQMAX, width), BF16)]
    scratch = scratch + [pltpu.VMEM((local, width), BF16)] * 3
    scratch = scratch + [pltpu.VMEM((buckets, width), BF16), pltpu.SemaphoreType.DMA((11,))]
    return kernel_call(
        functools.partial(backward_kernel, block, blocks),
        f"attention_backward_{block}",
        20_000_000_000,
        8_000_000,
        24,
        in_specs=[SCALARS]
        + [IN_VMEM] * groups
        + [IN_HBM] * 11
        + [IN_VMEM] * (2 + len(before)),
        out_specs=[IN_VMEM] * len(out_shape),
        out_shape=out_shape,
        scratch_shapes=scratch,
    )(
        place,
        *context_grads,
        *in_hbm(*kept, weights, *tables, hidden, *w_rows, table),
        rel_rows,
        norms,
        *before,
    )


def offset_rows(rel_buckets):
    plain = jnp.concatenate([rel_buckets[::-1], rel_buckets[:1]])
    back = plain.reshape(OFFSETS // TILE, TILE)[:, ::-1].reshape(OFFSETS)
    return jnp.stack([plain, back])


def layer_norm_parts(resid):
    centered = resid - jnp.mean(resid, axis=-1, keepdims=True)
    scale = lax.rsqrt(jnp.mean(centered * centered, axis=-1, keepdims=True) + NORM_EPS)
    return centered * scale, scale


def layer_norm_back(normal, scale, grad, gain):
    inner = grad * gain
    mean = jnp.mean(inner, axis=-1, keepdims=True)
    along = jnp.mean(inner * normal, axis=-1, keepdims=True)
    return scale * (inner - mean - normal * along)


def piece_kernel(place_ref, w_in_hbm, w_down_hbm, w_out_hbm, piece_ref, sems):
    replica = place_ref[1]
    width_rows, unit_rows = w_in_hbm.shape[0] // CHUNKS, w_down_hbm.shape[0] // CHUNKS
    rows = width_rows + unit_rows
    local = w_out_hbm.shape[0]
    at = pl.multiple_of(replica * width_rows, 16)
    down_at = pl.multiple_of(replica * unit_rows, 16)
    copies = start_copies(
        [
            (w_in_hbm.at[pl.ds(at, width_rows), :], piece_ref.at[pl.ds(0, width_rows), :]),
            (w_down_hbm.at[pl.ds(down_at, unit_rows), :], piece_ref.at[pl.ds(width_rows, unit_rows), :]),
        ],
        sems,
    )
    holds = replica * OUT_ROWS < local

    @pl.when(holds)
    def copy_out():
        out_at = pl.multiple_of(replica * OUT_ROWS, 16)
        wait_copies(
            start_copies(
                [(w_out_hbm.at[pl.ds(out_at, OUT_ROWS), :], piece_ref.at[pl.ds(rows, OUT_ROWS), :])],
                sems.at[pl.ds(2, 1)],
            )
        )

    @pl.when(jnp.logical_not(holds))
    def blank():
        piece_ref[rows:, :] = jnp.zeros((OUT_ROWS, piece_ref.shape[1]), BF16)

    wait_copies(copies)


def own_piece(place, w_in, w_down, w_out):
    width = w_down.shape[1]
    rows = w_in.shape[0] // CHUNKS + w_down.shape[0] // CHUNKS + OUT_ROWS
    return kernel_call(
        piece_kernel,
        "own_piece",
        0,
        700_000,
        4,
        in_specs=[SCALARS] + [IN_HBM] * 3,
        out_specs=IN_VMEM,
        out_shape=Shape((rows, width), BF16),
        scratch_shapes=[pltpu.SemaphoreType.DMA((3,))],
    )(place, *in_hbm(w_in, w_down, w_out))


def token_kernel(place_ref, *refs):
    groups = SEQMAX // TILE
    context_refs, refs = refs[:groups], refs[groups:]
    hidden_ref, out_grad_ref, norms_ref, w_in_ref, w_down_ref, w_out_ref = refs[:6]
    piece_refs, refs = refs[6 : 6 + len(GATHERED)], refs[6 + len(GATHERED) :]
    (
        output_ref, resid_ref, first_low_ref, act_out, pre_grad_out, ffn_grad_ref, attn_grad_ref,
        norm_grads_ref, *refs,
    ) = refs
    context_grad_refs, late_refs, refs = refs[:groups], refs[groups : groups + 2], refs[groups + 2 :]
    packed_vmem, out_vmem, slope_ref, sem, act_ref, pre_grad_ref, sems_out, *late_scratch = refs
    sent = []
    width = hidden_ref.shape[1]
    units = act_ref.shape[2]
    local = context_refs[0].shape[1]
    unit_rows, width_rows = units // CHUNKS, width // CHUNKS
    half = groups // 2

    out_copies, copies = gather_copies(piece_refs, packed_vmem, out_vmem, place_ref[1], sem)
    for copy in out_copies + copies:
        copy.start()
    for copy in out_copies:
        copy.wait()

    def packed(shift, first, rows):
        return packed_vmem[shift - 1, :, first : first + rows, :].reshape(CHUNKS * rows, width)

    def w_in(shift):
        return w_in_ref[...] if shift == 0 else packed(shift, 0, width_rows)

    def w_down(shift):
        return w_down_ref[...] if shift == 0 else packed(shift, width_rows, unit_rows)

    def w_out(shift):
        if shift == 0:
            return w_out_ref[...]
        return out_vmem[shift - 1].reshape(CHUNKS * OUT_ROWS, width)[:local]

    gain_one, bias_one = norms_ref[0:1, :], norms_ref[1:2, :]
    gain_two, bias_two = norms_ref[2:3, :], norms_ref[3:4, :]
    resid = hidden_ref[...].astype(F32)
    for g in range(groups):
        resid = resid + mm(context_refs[g][...], w_out(g)).astype(BF16).astype(F32)
    normal_one, scale_one = layer_norm_parts(resid)
    first_norm = normal_one * gain_one + bias_one
    first_low = first_norm.astype(BF16)
    first_low_ref[...] = first_low
    ffn_out = first_norm
    for g in range(groups):
        if g == 1:
            wait_copies(copies)
        pre_act = mm(first_low, w_in(g))
        area = 0.5 * (1.0 + lax.erf(pre_act * math.sqrt(0.5)))
        activated = (pre_act * area).astype(BF16)
        act_ref[g] = activated
        if g < half:
            sent += start_copies([(act_ref.at[g], act_out.at[g])], sems_out.at[pl.ds(g, 1)])
        density = jnp.exp(-0.5 * pre_act * pre_act) * (1.0 / math.sqrt(2.0 * math.pi))
        slope_ref[g] = area + pre_act * density
        ffn_out = ffn_out + mm(activated, w_down(g)).astype(BF16).astype(F32)
    normal_two, scale_two = layer_norm_parts(ffn_out)
    output_ref[...] = (normal_two * gain_two + bias_two).astype(BF16)
    out_grad = out_grad_ref[...].astype(F32)
    norm_grads_ref[...] = jnp.zeros_like(norm_grads_ref)
    norm_grads_ref[2:3, :] = jnp.sum(out_grad * normal_two, axis=0, keepdims=True)
    norm_grads_ref[3:4, :] = jnp.sum(out_grad, axis=0, keepdims=True)
    second_grad = layer_norm_back(normal_two, scale_two, out_grad, gain_two)
    ffn_grad = second_grad.astype(BF16)
    ffn_grad_ref[...] = ffn_grad
    first_grad = second_grad
    for g in range(groups):
        pre_grad = (mm_nt(ffn_grad, w_down(g)) * slope_ref[g]).astype(BF16)
        pre_grad_ref[g] = pre_grad
        if g < half:
            sent += start_copies(
                [(pre_grad_ref.at[g], pre_grad_out.at[g])], sems_out.at[pl.ds(half + g, 1)]
            )
        first_grad = first_grad + mm_nt(pre_grad, w_in(g))
    norm_grads_ref[0:1, :] = jnp.sum(first_grad * normal_one, axis=0, keepdims=True)
    norm_grads_ref[1:2, :] = jnp.sum(first_grad, axis=0, keepdims=True)
    resid_grad = layer_norm_back(normal_one, scale_one, first_grad, gain_one)
    resid_ref[...] = resid_grad
    attn_grad = resid_grad.astype(BF16)
    attn_grad_ref[...] = attn_grad
    for g in range(groups):
        context_grad_refs[g][...] = mm_nt(attn_grad, w_out(g)).astype(BF16)
    sorted_weight_grads(
        place_ref,
        [ref[...] for ref in context_refs[half:]],
        first_low,
        lambda j: act_ref[half + j],
        lambda j: pre_grad_ref[half + j],
        ffn_grad,
        attn_grad,
        late_refs,
        late_scratch,
    )
    wait_copies(sent)


def gather_copies(piece_refs, packed_vmem, out_vmem, replica, sem):
    out_copies, copies = [], []
    kept = packed_vmem.shape[2]
    for (group, relatives, firsts, rows), ref in zip(GATHERED, piece_refs):
        for i, relative in enumerate(relatives):
            chunk = jnp.bitwise_xor(replica, relative)
            first = firsts[i]
            main = min(first + rows, kept) - first
            copies.append(
                pltpu.make_async_copy(
                    ref.at[i, pl.ds(0, main), :],
                    packed_vmem.at[group - 1, chunk, pl.ds(first, main), :],
                    sem.at[len(copies)],
                )
            )
            if main < rows:
                out_copies.append(
                    pltpu.make_async_copy(
                        ref.at[i, pl.ds(main, rows - main), :],
                        out_vmem.at[group - 1, chunk],
                        sem.at[32 + len(out_copies)],
                    )
                )
    return out_copies, copies


def reached(axes):
    order = (0,)
    for bit in axes:
        order = order + tuple(relative + bit for relative in order)
    return order


def gathered_layout():
    layout = []
    for group, axes in ((1, (ACROSS_Y, ACROSS_X)), (2, (ACROSS_X, ACROSS_Y))):
        for core in (0, CORE):
            layout += [(group, (core, core + axes[0]), (0, 0), 2 * HALF_ROWS)]
            layout += [(group, (core + axes[1], core + sum(axes)), (0, 0), 2 * HALF_ROWS)]
    halves = ((0, (ACROSS_Y, ACROSS_X)), (HALF_ROWS, (ACROSS_X, ACROSS_Y)))
    for core in (0, CORE):
        both = tuple((core + r, first) for first, axes in halves for r in reached(axes))
        layout += [(3, tuple(r for r, first in both), tuple(first for r, first in both), HALF_ROWS)]
    return layout


ROW_ORDER = reached((ACROSS_Y, ACROSS_X, CORE))
HALF_ROWS = 112
GATHERED = gathered_layout()


def across(array, bit):
    return lax.ppermute(array, "dp", [(i, i ^ bit) for i in range(CHUNKS)])


def nearby(arrays):
    ways = (ACROSS_Y, ACROSS_X, ACROSS_Y + ACROSS_X)
    return [arrays[0]] + [across(array, way) for array, way in zip(arrays[1:], ways)]


def together(*values):
    return lax.optimization_barrier(values)


def token_layer(place, contexts, hidden, out_grad, norms, w_rows, pieces):
    tokens, width = hidden.shape
    local = contexts[0].shape[1]
    units = w_rows[0].shape[1]
    groups = len(contexts)
    rows = width // CHUNKS + units // CHUNKS + OUT_ROWS
    return kernel_call(
        token_kernel,
        "token_layer",
        15_000_000_000,
        18_000_000,
        40,
        in_specs=[SCALARS]
        + [IN_VMEM] * (groups + 6)
        + [ANYWHERE] * len(pieces),
        out_specs=[IN_VMEM] * 3 + [IN_HBM] * 2 + [IN_VMEM] * (3 + groups) + [IN_HBM] * 2,
        out_shape=[
            Shape((tokens, width), BF16),
            Shape((tokens, width), F32),
            Shape((tokens, width), BF16),
            hbm_shape((groups // 2, tokens, units), BF16),
            hbm_shape((groups // 2, tokens, units), BF16),
            Shape((tokens, width), BF16),
            Shape((tokens, width), BF16),
            Shape((8, width), F32),
        ]
        + [Shape((tokens, local), BF16)] * groups
        + [hbm_shape((2, CHUNKS // 2, rows, width), BF16)] * 2,
        scratch_shapes=[
            pltpu.VMEM((groups - 1, CHUNKS, rows - OUT_ROWS, width), BF16),
            pltpu.VMEM((groups - 1, CHUNKS, OUT_ROWS, width), BF16),
            pltpu.VMEM((groups, tokens, units), F32),
            pltpu.SemaphoreType.DMA((56,)),
            pltpu.VMEM((groups, tokens, units), BF16),
            pltpu.VMEM((groups, tokens, units), BF16),
            pltpu.SemaphoreType.DMA((groups,)),
        ]
        + weight_grad_scratch(width, units, rows),
    )(place, *contexts, hidden, out_grad, norms, *w_rows, *pieces)


def sorted_weight_grads(
    place_ref, contexts, first_low, act_of, pre_grad_of, ffn_grad, attn_grad, out_refs, scratch
):
    in_ref, down_ref, last_ref, sorted_ref, sems = scratch
    local = contexts[0].shape[1]
    width_rows = in_ref.shape[0] // CHUNKS
    unit_rows = down_ref.shape[0] // CHUNKS
    rows = width_rows + unit_rows
    last_ref[local:, :] = jnp.zeros((last_ref.shape[0] - local, last_ref.shape[1]), BF16)
    copies = []
    for j, axes in enumerate(PART_AXES):
        last_ref[:local, :] = mm_tn(contexts[j], attn_grad).astype(BF16)
        in_ref[...] = mm_tn(first_low, pre_grad_of(j)).astype(BF16)
        down_ref[...] = mm_tn(act_of(j), ffn_grad).astype(BF16)
        for side, core in ((1, CORE), (0, 0)):
            for slot, relative in enumerate(reached(axes[::-1])):
                chunk = jnp.bitwise_xor(relative + core, place_ref[1])
                at = pl.multiple_of(chunk * width_rows, 16)
                sorted_ref[side, j, slot, :width_rows] = in_ref[pl.ds(at, width_rows), :]
                at = pl.multiple_of(chunk * unit_rows, 16)
                sorted_ref[side, j, slot, width_rows:rows] = down_ref[pl.ds(at, unit_rows), :]
                at = pl.multiple_of(chunk * OUT_ROWS, 16)
                sorted_ref[side, j, slot, rows:] = last_ref[pl.ds(at, OUT_ROWS), :]
            copies += start_copies(
                [(sorted_ref.at[side, j], out_refs[side].at[j])], sems.at[pl.ds(2 * side + j, 1)]
            )
    wait_copies(copies)


def weight_grad_scratch(width, units, rows):
    return [
        pltpu.VMEM((width, width), BF16),
        pltpu.VMEM((units, width), BF16),
        pltpu.VMEM((CHUNKS * OUT_ROWS, width), BF16),
        pltpu.VMEM((2, 2, CHUNKS // 2, rows, width), BF16),
        pltpu.SemaphoreType.DMA((4,)),
    ]


def weight_grad_kernel(place_ref, *refs):
    context_refs, refs = refs[:2], refs[2:]
    first_low_ref, act_hbm, pre_grad_hbm, ffn_grad_ref, attn_grad_ref, *out_refs = refs[:7]
    scratch, (act_ref, pre_grad_ref, sems_in) = refs[7:12], refs[12:]
    arriving = start_copies(
        [
            (source.at[j], target.at[j])
            for j in range(2)
            for source, target in ((pre_grad_hbm, pre_grad_ref), (act_hbm, act_ref))
        ],
        sems_in,
    )

    def act_of(j):
        arriving[2 * j + 1].wait()
        return act_ref[j]

    def pre_grad_of(j):
        arriving[2 * j].wait()
        return pre_grad_ref[j]

    sorted_weight_grads(
        place_ref,
        [ref[...] for ref in context_refs],
        first_low_ref[...],
        act_of,
        pre_grad_of,
        ffn_grad_ref[...],
        attn_grad_ref[...],
        out_refs,
        scratch,
    )


def weight_grads(place, contexts, first_low, act, pre_grad, ffn_grad, attn_grad):
    tokens, units = act.shape[1:]
    width = first_low.shape[1]
    rows = width // CHUNKS + units // CHUNKS + OUT_ROWS
    return kernel_call(
        weight_grad_kernel,
        "weight_grads",
        4_000_000_000,
        7_000_000,
        15,
        in_specs=[SCALARS] + [IN_VMEM] * 3 + [IN_HBM] * 2 + [IN_VMEM] * 2,
        out_specs=[IN_HBM] * 2,
        out_shape=[hbm_shape((2, CHUNKS // 2, rows, width), BF16)] * 2,
        scratch_shapes=weight_grad_scratch(width, units, rows)
        + [
            pltpu.VMEM((2, tokens, units), BF16),
            pltpu.VMEM((2, tokens, units), BF16),
            pltpu.SemaphoreType.DMA((4,)),
        ],
    )(place, *contexts[:2], first_low, *in_hbm(act, pre_grad), ffn_grad, attn_grad)


def add(left, right):
    return (left.astype(F32) + right.astype(F32)).astype(BF16)


def total_of(arrays):
    return sum(array.astype(F32) for array in arrays).astype(BF16)


def reorder_kernel(place_ref, *refs):
    out_ref = refs[-1]
    groups = out_ref.shape[1]
    blocks = out_ref.shape[0]
    per = len(refs[:-1]) // groups
    for shift in range(groups):
        origin = jnp.bitwise_xor(place_ref[0], shift)
        for b in range(blocks):
            if per == 1:
                out_ref[b, origin] = refs[shift][b * TILE : (b + 1) * TILE, :]
            else:
                out_ref[b, origin] = refs[b * groups + shift][...]


def reorder(place, pieces, blocks):
    width = pieces[0].shape[1]
    groups = SEQMAX // TILE
    out = kernel_call(
        reorder_kernel,
        "reorder",
        0,
        3_000_000,
        8,
        in_specs=[SCALARS] + [IN_VMEM] * len(pieces),
        out_specs=IN_VMEM,
        out_shape=Shape((blocks, groups, TILE, width), BF16),
    )(place, *pieces)
    return out.reshape(blocks * SEQMAX, width)


def unpack_kernel(place_ref, *refs):
    piece_refs, refs = refs[:2], refs[2:]
    grad_in_ref, grad_down_ref, grad_out_ref, q_ref, k_ref, v_ref, all_ref = refs
    local = q_ref.shape[0]
    width_rows = grad_in_ref.shape[0] // CHUNKS
    unit_rows = grad_down_ref.shape[0] // CHUNKS
    row_rows = all_ref.shape[0] // CHUNKS
    out_at = width_rows + unit_rows
    rows_at = out_at + OUT_ROWS
    for slot, relative in enumerate(ROW_ORDER):
        ref = piece_refs[slot // 4].at[slot % 4]
        chunk = jnp.bitwise_xor(place_ref[1], relative)
        at = pl.multiple_of(chunk * width_rows, 8)
        grad_in_ref[pl.ds(at, width_rows), :] = ref[:width_rows, :].astype(F32)
        at = pl.multiple_of(chunk * unit_rows, 8)
        grad_down_ref[pl.ds(at, unit_rows), :] = ref[width_rows:out_at, :].astype(F32)
        at = pl.multiple_of(chunk * row_rows, 8)
        all_ref[pl.ds(at, row_rows), :] = ref[rows_at:, :].astype(F32)

        @pl.when(chunk * OUT_ROWS < grad_out_ref.shape[0])
        def out_rows(chunk=chunk, ref=ref):
            at = pl.multiple_of(chunk * OUT_ROWS, 8)
            grad_out_ref[pl.ds(at, OUT_ROWS), :] = ref[out_at:rows_at, :].astype(F32)

    for i, ref in enumerate((q_ref, k_ref, v_ref)):
        ref[...] = all_ref[i * local : (i + 1) * local, :]


def unpack(place, pieces, width, units, local):
    return kernel_call(
        unpack_kernel,
        "unpack",
        0,
        12_000_000,
        10,
        in_specs=[SCALARS] + [IN_VMEM] * 2,
        out_specs=[IN_VMEM] * 6,
        out_shape=[Shape((width, width), F32), Shape((units, width), F32)]
        + [Shape((local, width), F32)] * 4,
        scratch_shapes=[pltpu.VMEM((3 * local, width), F32)],
    )(place, *pieces)


def small_kernel(place_ref, *refs):
    piece_refs, table_ref, norm_refs, norms_ref = refs[:-6], refs[-6], refs[-5:-1], refs[-1]
    table_rows = table_ref.shape[0] // CHUNKS
    rows = table_rows + SMALL_ROWS
    columns = norms_ref.shape[1]
    per = CHUNKS // len(piece_refs)
    for slot, relative in enumerate(ROW_ORDER):
        ref, first = piece_refs[slot // per], slot % per * rows
        chunk = jnp.bitwise_xor(place_ref[1], relative)
        at = pl.multiple_of(chunk * table_rows, 8)
        table_ref[pl.ds(at, table_rows), :] = ref[first : first + table_rows, :].astype(F32)
        low = ref[first + table_rows : first + rows, :columns].astype(F32)
        norms_ref[pl.ds(chunk, 1), :] = low[:1]
    for i, ref in enumerate(norm_refs):
        ref[:columns] = norms_ref[2 * i, :]
        ref[columns:] = norms_ref[2 * i + 1, :]


def small_unpack(place, small, width, buckets):
    return kernel_call(
        small_kernel,
        "small_unpack",
        0,
        3_000_000,
        8,
        in_specs=[SCALARS] + [IN_VMEM] * len(small),
        out_specs=[IN_VMEM] * 5,
        out_shape=[Shape((buckets, width), F32)] + [Shape((width,), F32)] * 4,
        scratch_shapes=[pltpu.VMEM((CHUNKS, 4 * width // CHUNKS), F32)],
    )(place, *small)


def send(array, bits):
    return lax.ppermute(array, "tensor", [(i, i ^ bits) for i in range(SEQMAX // TILE)])


def exchange(pieces):
    return [pieces[0]] + [send(piece, r) for r, piece in enumerate(pieces) if r > 0]


def second_exchange(context, got):
    near = send(jnp.concatenate([context[1], got[1:]], 0), 1)
    return [context[0][0], near[0], got[0], near[1]]


def spread(array):
    near, far = send(array, 1), send(array, 2)
    return [array, near, far, send(far, 1)]


def shards(
    n_dp,
    n_tensor,
    hidden,
    out_grad,
    w_query,
    w_key,
    w_value,
    w_out,
    w_in,
    w_down,
    bucket_table,
    gain_one,
    bias_one,
    gain_two,
    bias_two,
    rel_buckets,
    group_counts,
    key_mask,
):
    tokens, width = hidden.shape
    local = w_query.shape[1]
    units = w_in.shape[1]
    buckets = bucket_table.shape[0]
    blocks = tokens // SEQMAX
    mine = tokens // n_tensor
    by_axis = n_dp == CHUNKS
    me = lax.axis_index("tensor")
    replica = lax.axis_index("dp") if by_axis else jnp.int32(0)
    place = jnp.stack([me, replica]).astype(jnp.int32)
    rel_rows = offset_rows(rel_buckets)
    width_rows, unit_rows = width // CHUNKS, units // CHUNKS
    padded = jnp.pad(w_out, ((0, CHUNKS * OUT_ROWS - local), (0, 0)))

    w_rows = (w_query.T, w_key.T, w_value.T)

    def my_rows(array):
        array = array.reshape(blocks, n_tensor, TILE, width)
        return lax.dynamic_index_in_dim(array, me, 1, keepdims=False).reshape(mine, width)

    def forward(block, context):
        weights, *context = forward_attention(
            block, place, group_counts, tables, rows, key_mask, context
        )
        return weights, context

    if by_axis:
        piece = own_piece(place, w_in, w_down, w_out)
        near, far = send(piece, 1), send(piece, 2)
        (*tables, q, k, v), saved = prepare(*w_rows, bucket_table, rel_rows, hidden)
        rows = (q, k, v)
        my_hidden, my_out_grad = my_rows(hidden), my_rows(out_grad)
        near, far, tables, rows, saved, my_hidden, my_out_grad = together(
            near, far, tables, rows, saved, my_hidden, my_out_grad
        )
        last = send(far, 1)
        near_y, far_x = across(near[None], ACROSS_Y), across(far[None], ACROSS_X)
        kept_0, context = forward(0, [])
        near, far, near_y, far_x, last, kept_0, context, tables, rows = together(
            near, far, near_y, far_x, last, kept_0, context, tables, rows
        )
        near = jnp.concatenate([near[None], near_y], 0)
        far = jnp.concatenate([far[None], far_x], 0)
        near_x, far_y = across(near, ACROSS_X), across(far, ACROSS_Y)
        top, low = last[None, :HALF_ROWS], last[None, HALF_ROWS:]
        top_y, low_x = across(top, ACROSS_Y), across(low, ACROSS_X)
        kept_1, context = forward(1, context)
        got = send(context[2], 2)
        near, near_x, far, far_y, top, top_y, low, low_x, context, got, kept_0, kept_1 = together(
            near, near_x, far, far_y, top, top_y, low, low_x, context, got, kept_0, kept_1
        )
        contexts = second_exchange(context, got)
        top = jnp.concatenate([top, top_y], 0)
        low = jnp.concatenate([low, low_x], 0)
        top_x, low_y = across(top, ACROSS_X), across(low, ACROSS_Y)
        cores = [across(near, CORE), across(near_x, CORE)]
        near, near_x, cores, far, far_y, top, top_x, low, low_y, contexts, kept_0, kept_1 = (
            together(
                near, near_x, cores, far, far_y, top, top_x, low, low_y, contexts, kept_0, kept_1
            )
        )
        both = jnp.concatenate([top, top_x, low, low_y], 0)
        gathered = [near, near_x, *cores]
        gathered += [far, far_y, across(far, CORE), across(far_y, CORE)]
        gathered += [both, across(both, CORE)]
    else:
        (*tables, q, k, v), saved = prepare(*w_rows, bucket_table, rel_rows, hidden)
        rows = (q, k, v)
        stacked = jnp.concatenate(
            [
                w_in.reshape(CHUNKS, width_rows, width),
                w_down.reshape(CHUNKS, unit_rows, width),
                padded.reshape(CHUNKS, OUT_ROWS, width),
            ],
            1,
        )
        sent = spread(stacked)
        gathered = [
            jnp.stack(
                [
                    sent[group][chunk, at : at + rows]
                    for chunk, at in zip(chunks, first)
                ]
            )
            for group, chunks, first, rows in GATHERED
        ]
        kept_0, context = forward(0, [])
        kept_1, context = forward(1, context)
        contexts = second_exchange(context, send(context[2], 2))
        my_hidden, my_out_grad = my_rows(hidden), my_rows(out_grad)
    *tables, q, k, v = saved
    norms = jnp.stack([gain_one, bias_one, gain_two, bias_two])
    (
        output, resid_grad, first_low, act, pre_grad, ffn_grad, attn_grad, norm_grads, *back,
        late_keep, late_give,
    ) = token_layer(
        place, contexts, my_hidden, my_out_grad, norms, (w_in, w_down, w_out), gathered
    )
    norm_grads = norm_grads[:4].reshape(CHUNKS, 4 * width // CHUNKS)

    def backward(block, kept, before):
        own, near, far, *before = backward_attention(
            block, blocks, place, back, (q, k, v), kept, tables, hidden, w_rows, bucket_table, rel_rows,
            norm_grads, before,
        )
        return [own, near, far], before

    keep_1, give_1 = late_keep, late_give
    back = exchange(back)
    core_1 = across(give_1, CORE) if by_axis else give_1
    keep_0, give_0 = weight_grads(
        place, contexts, first_low, act, pre_grad, ffn_grad, attn_grad
    )

    def first_sums(keep, got):
        return [add(keep[j, 2:], got[j, 2:]) for j in range(2)]

    sums_1 = first_sums(keep_1, core_1) if by_axis else []
    (
        back, core_1, sums_1, keep_0, give_0, keep_1, output, resid_grad, norm_grads, kept_0,
        kept_1, tables, place,
    ) = together(
        back, core_1, sums_1, keep_0, give_0, keep_1, output, resid_grad, norm_grads, kept_0,
        kept_1, tables, place,
    )
    back = [piece.reshape(blocks, TILE, local) for piece in back]

    def first_stage(sums):
        return [across(part, axes[0]) for part, axes in zip(sums, PART_AXES)]

    def second_sums(keep, got, first):
        return [total_of([keep[j, 1:2], got[j, 1:2], first[j][1:2]]) for j in range(2)]

    def second_stage(keep, got, first, given):
        kept = [[keep[j, 0], got[j, 0], first[j][0]] for j in range(2)]
        return kept, [across(part, axes[1]) for part, axes in zip(given, PART_AXES)]

    def joint(arrays, way):
        rows = [array.shape[0] for array in arrays]
        got = send(jnp.concatenate(arrays, 0), way)
        return [got[sum(rows[:i]) : sum(rows[: i + 1])] for i in range(len(rows))]

    stage_1, core_0 = [], give_0
    if by_axis:
        stage_1 = first_stage(sums_1)
        core_0 = across(give_0, CORE)
    out_near, out_far = send(output, 1), send(output, 2)
    parts, before = backward(0, kept_0, ())
    sums_0, given_1 = [], []
    if by_axis:
        sums_0, given_1 = first_sums(keep_0, core_0), second_sums(keep_1, core_1, stage_1)
    (
        parts, before, stage_1, core_0, core_1, keep_0, keep_1, out_near, out_far, output,
        resid_grad, norm_grads, kept_1, tables, place, back, sums_0, given_1,
    ) = together(
        parts, before, stage_1, core_0, core_1, keep_0, keep_1, out_near, out_far, output,
        resid_grad, norm_grads, kept_1, tables, place, back, sums_0, given_1,
    )
    stage_0 = first_stage(sums_0) if by_axis else []
    late = second_stage(keep_1, core_1, stage_1, given_1) if by_axis else []
    near, out_last = joint([parts[1], out_far], 1)
    parts = [parts[0], near, parts[2]]
    parts_1, before = backward(1, kept_1, before)
    parts, parts_1, before, stage_0, late, core_0, keep_0, out_last, resid_grad = together(
        parts, parts_1, before, stage_0, late, core_0, keep_0, out_last, resid_grad
    )
    def total(block, pieces):
        wide = resid_grad[block * TILE : (block + 1) * TILE]
        for piece in pieces:
            wide = wide + piece.astype(F32)
        return wide.astype(BF16)

    keep, give = before
    thirds, sums = [], keep
    if not by_axis:
        joined = lax.psum(jnp.concatenate([keep, give], 0).astype(F32), "dp").astype(BF16)
    if by_axis:
        given_0 = second_sums(keep_0, core_0, stage_0)
        thirds = [second_stage(keep_0, core_0, stage_0, given_0), late]
        sums = add(keep, across(give, CORE))
    far_0 = send(add(parts[2], parts[1][TILE:]), 2)
    near_1 = send(parts_1[1], 1)
    grad_0 = total(0, [parts[0], parts[1][:TILE], far_0])
    sum_1 = add(parts_1[2], near_1[TILE:])
    grad_0, sum_1, parts_1, near_1, thirds, sums, resid_grad, out_last = together(
        grad_0, sum_1, parts_1, near_1, thirds, sums, resid_grad, out_last
    )

    output = reorder(place, [output, out_near, out_far, out_last], blocks)
    shard, near_0 = [], [grad_0]
    if by_axis:
        for kept, got in thirds:
            shard += [total_of([*kept[j], got[j][0]]) for j in range(2)]
        near_0 = near_0 + [shard[3]]
        joined = total_of(nearby([sums[i : i + 1] for i in range(CHUNKS // 2)]))
    near_0 = joint(near_0, 1)
    far_0, far_1 = joint([grad_0, sum_1], 2)
    pos_rows = buckets // CHUNKS // 2
    slots = joined.shape[0]
    row_grads = joined[:, pos_rows + SMALL_ROWS :]
    pos = joined[:, :pos_rows]
    pos = jnp.concatenate([pos[:, :, : 2 * local], pos[:, :, 2 * local :]], 1)
    w_table = jnp.concatenate([w_rows[1], w_rows[0]], 0)
    table_part = mm(pos.reshape(slots * 2 * pos_rows, 2 * local), w_table)
    table_part = table_part.astype(BF16).reshape(slots, 2 * pos_rows, width)
    small = jnp.concatenate([table_part, joined[:, pos_rows : pos_rows + SMALL_ROWS]], 1)
    small_rows = small.shape[1]
    small = small.reshape(slots * small_rows, width)
    grad_0, near_0, far_0, far_1, near_1, parts_1, resid_grad, output, shard, small, row_grads = (
        together(
            grad_0, near_0, far_0, far_1, near_1, parts_1, resid_grad, output, shard, small,
            row_grads,
        )
    )
    grad_1 = total(1, [parts_1[0], near_1[:TILE], far_1])
    shard_far = []
    if by_axis:
        shard_1, small_near = joint([shard[1], small], 1)
        shard_far = [shard_1, send(add(shard[2], near_0[1]), 2)]
    else:
        small_near = send(small, 1)
    small = add(small, small_near)
    if by_axis:
        row_grads = nearby([row_grads[0]] * 4)
    grad_0, near_0, far_0, grad_1, row_grads, small, shard, shard_far = together(
        grad_0, near_0, far_0, grad_1, row_grads, small, shard, shard_far
    )
    near_1, last_0 = joint([grad_1, far_0], 1)
    far_1, small_far = joint([grad_1, small], 2)
    small = add(small, small_far)
    if by_axis:
        shard = total_of([shard[0], *shard_far])
        pieces = nearby([shard] * 4)
        grad_0, near_0, far_0, last_0, grad_1, near_1, far_1, small, pieces, row_grads = together(
            grad_0, near_0, far_0, last_0, grad_1, near_1, far_1, small, pieces, row_grads
        )
        pieces = [jnp.concatenate(pair, 0) for pair in zip(pieces, row_grads)]
        pieces = jnp.stack(pieces)
        pieces = [pieces, across(pieces, CORE)]
        small = nearby([small] * 4)
    else:
        natural = []
        for keep, give in ((keep_0, give_0), (keep_1, give_1)):
            for j, axes in enumerate(PART_AXES):
                chunks = reached(axes[::-1] + (CORE,))
                both = jnp.concatenate([keep[j], give[j]], 0)
                natural.append(jnp.stack([both[chunks.index(c)] for c in range(CHUNKS)]))
        shard = jnp.stack(exchange(natural)).astype(F32)
        shard = lax.psum(sum(shard[r] for r in range(n_tensor)), "dp").astype(BF16)
        pieces = jnp.stack(
            [
                jnp.concatenate([shard[chunk], row_grads[slot]], 0)
                for slot, chunk in enumerate(ROW_ORDER)
            ]
        )
        pieces = [pieces[:4], pieces[4:]]
        small = [small]
    last_1 = send(far_1, 1)
    grad_hidden = reorder(
        place, [grad_0, near_0[0], far_0, last_0, grad_1, near_1, far_1, last_1], blocks
    )
    if by_axis:
        grad_hidden, small, pieces = together(grad_hidden, small, pieces)
        small = jnp.concatenate(small, 0)
        small = [small, across(small, CORE)]
    grad_in, grad_down, grad_out, grad_query, grad_key, grad_value = unpack(
        place, pieces, width, units, local
    )
    if by_axis:
        small, grad_hidden, grad_in, grad_down, grad_out, grad_query, grad_key, grad_value = (
            together(
                small, grad_hidden, grad_in, grad_down, grad_out, grad_query, grad_key, grad_value
            )
        )
    grad_table, *norm_grads = small_unpack(place, small, width, buckets)
    return (
        output,
        grad_hidden,
        grad_query.T,
        grad_key.T,
        grad_value.T,
        grad_out,
        grad_in,
        grad_down,
        grad_table,
        *norm_grads,
    )


def solution(mesh):
    in_specs = (
        P("dp", None),
        P("dp", None),
        P(None, "tensor"),
        P(None, "tensor"),
        P(None, "tensor"),
        P("tensor", None),
        P(None, "tensor"),
        P("tensor", None),
        P(),
        P(),
        P(),
        P(),
        P(),
        P(),
        P("dp", None),
        P("dp"),
    )
    out_specs = (
        P("dp", None),
        P("dp", None),
        P(None, "tensor"),
        P(None, "tensor"),
        P(None, "tensor"),
        P("tensor", None),
        P(None, "tensor"),
        P("tensor", None),
        P(),
        P(),
        P(),
        P(),
        P(),
    )
    body = functools.partial(shards, mesh.shape["dp"], mesh.shape["tensor"])
    return jax.shard_map(body, mesh=mesh, in_specs=in_specs, out_specs=out_specs, check_vma=False)
```
